512 devices in a mesh: lon: 64 (over z, y_lo, core), lat: 8 (over x, y_hi).
Axes of the slice: x: 4, y: 8 (y_hi: 2, y_lo: 4; y = y_hi * 4 + y_lo), z: 8, core: 2. Of those that a mesh axis runs over, the one named last changes fastest.
Arguments:
- potential_warmth: float32 [16, 128, 8192], P(None, 'lat', 'lon'), may hold values from -6 to 6
- saltiness_anomaly: float32 [16, 128, 8192], P(None, 'lat', 'lon'), may hold values from -6 to 6
- zonal_face_fraction: float32 [16, 128, 8192], P(None, 'lat', 'lon'), may hold values from -0.45 to 0.45
- poleward_face_fraction: float32 [16, 128, 8192], P(None, 'lat', 'lon'), may hold values from -0.45 to 0.45
- water_indicator: int32 [128, 8192], P('lat', 'lon'), may hold values 0 or 1
- water_depth_layers: int32 [128, 8192], P('lat', 'lon'), may hold values from 0 to 16
- hyperdiffusion_factor: float32 [16], replicated, may hold values from 0.005 to 0.03
Outputs:
- transported_warmth: float32 [16, 128, 8192], P(None, 'lat', 'lon')
- transported_saltiness: float32 [16, 128, 8192], P(None, 'lat', 'lon')
- zonal_flow_damped: float32 [16, 128, 8192], P(None, 'lat', 'lon')
- poleward_flow_damped: float32 [16, 128, 8192], P(None, 'lat', 'lon')
The draws below stay inside these ranges and needn't reach their ends.
All inputs are finite; a program needn't handle non-finite values. No bound on the sum of `water_indicator` on one device may be relied on, other than what follows from the above.
Results may differ from the reference program's by a relative error of at most 0.0003.
Values sent between devices are 32-bit elements; how exact they have to be, the bound alone decides.
No kernel may reach another device: no remote copies, remote signals or barrier semaphores. Data moves between devices by JAX's collectives and lax.ppermute only.
A program may use at most 64 MiB of HBM per device.

```python
import math
import jax
import jax.numpy as jnp
from jax import lax

DEPTH_LAYERS = 16
PARALLEL_TOTAL = 128
MERIDIAN_TOTAL = 8192


def touch_ends(values, key, least, top_value):
    dims = values.shape
    spot = [jax.random.randint(jax.random.fold_in(key, axis), (), 0, dims[axis]) for axis in range(len(dims))]
    values = values.at[tuple(spot)].set(least)
    longest = dims.index(max(dims))
    spot[longest] = (spot[longest] + 1) % dims[longest]
    return values.at[tuple(spot)].set(top_value)


def shard_levels(rng, shape, split, low, high):
    level, own = 1.0, jax.random.fold_in(rng, 6)
    for axis_at, shards_of in split:
        draws = jnp.exp(jax.random.uniform(jax.random.fold_in(own, axis_at), (shards_of,), jnp.float32, low / len(split), high / len(split)))
        level = level * jnp.repeat(draws, shape[axis_at] // shards_of).reshape([-1 if axis == axis_at else 1 for axis in range(len(shape))])
    return level


def normal_values(stream_key, extent, scale, most, cuts=(), kind=jnp.bfloat16):
    drawn = scale * jax.random.normal(stream_key, extent, jnp.float32)
    if cuts:
        drawn = drawn * shard_levels(stream_key, extent, cuts, -0.22, 0.18)
    return jnp.clip(drawn, -most, most).astype(kind)


def setup_inputs(seed: int = 0) -> dict:
    keys = jax.random.split(jax.random.key(seed), 8)
    potential_warmth = normal_values(keys[0], (DEPTH_LAYERS, PARALLEL_TOTAL, MERIDIAN_TOTAL), 1.0, 6.0, ((1, 8), (2, 64)), jnp.float32)
    saltiness_anomaly = normal_values(keys[1], (DEPTH_LAYERS, PARALLEL_TOTAL, MERIDIAN_TOTAL), 1.0, 6.0, ((1, 8), (2, 64)), jnp.float32)
    zonal_face_fraction = jnp.clip(jax.random.uniform(keys[2], (DEPTH_LAYERS, PARALLEL_TOTAL, MERIDIAN_TOTAL), jnp.float32, -0.45, 0.45) * shard_levels(keys[2], (DEPTH_LAYERS, PARALLEL_TOTAL, MERIDIAN_TOTAL), ((1, 8), (2, 64)), -0.4, 0.0), -0.45, 0.45)
    poleward_face_fraction = jnp.clip(jax.random.uniform(keys[3], (DEPTH_LAYERS, PARALLEL_TOTAL, MERIDIAN_TOTAL), jnp.float32, -0.45, 0.45) * shard_levels(keys[3], (DEPTH_LAYERS, PARALLEL_TOTAL, MERIDIAN_TOTAL), ((1, 8), (2, 64)), -0.4, 0.0), -0.45, 0.45)
    water_indicator = touch_ends((jax.random.randint(keys[4], (PARALLEL_TOTAL, MERIDIAN_TOTAL), 0, 5) < 4).astype(jnp.int32), jax.random.fold_in(keys[4], 1), 0, 1)
    water_depth_layers = touch_ends(jax.random.randint(keys[5], (PARALLEL_TOTAL, MERIDIAN_TOTAL), 0, DEPTH_LAYERS + 1), jax.random.fold_in(keys[5], 1), 0, DEPTH_LAYERS).astype(jnp.int32)
    hyperdiffusion_factor = jnp.clip(jnp.exp(jax.random.uniform(keys[6], (DEPTH_LAYERS,), jnp.float32, math.log(0.005), math.log(0.03))), 0.005, 0.03)
    return {"potential_warmth": potential_warmth, "saltiness_anomaly": saltiness_anomaly, "zonal_face_fraction": zonal_face_fraction, "poleward_face_fraction": poleward_face_fraction, "water_indicator": water_indicator, "water_depth_layers": water_depth_layers, "hyperdiffusion_factor": hyperdiffusion_factor}


def cut_along(source, start_at, count_of, along):
    return lax.slice_in_dim(source, start_at, start_at + count_of, axis=source.ndim + along)


def parabolic_update(tracer, courant, wet_cells, length, along):
    far_left = cut_along(tracer, 0, length + 3, along)
    near_left = cut_along(tracer, 1, length + 3, along)
    near_right = cut_along(tracer, 2, length + 3, along)
    far_right = cut_along(tracer, 3, length + 3, along)
    edges = (7.0 / 12.0) * (near_left + near_right) - (1.0 / 12.0) * (far_left + far_right)
    edges = jnp.clip(edges, jnp.minimum(near_left, near_right), jnp.maximum(near_left, near_right))
    left_edge = cut_along(edges, 0, length + 2, along)
    right_edge = cut_along(edges, 1, length + 2, along)
    middle = cut_along(tracer, 2, length + 2, along)
    flatten = (right_edge - middle) * (middle - left_edge) <= 0.0
    left_edge = jnp.where(flatten, middle, left_edge)
    right_edge = jnp.where(flatten, middle, right_edge)
    steepness = right_edge - left_edge
    bending = steepness * (middle - 0.5 * (left_edge + right_edge))
    bound_cap = steepness * steepness / 6.0
    left_final = jnp.where(bending > bound_cap, 3.0 * middle - 2.0 * right_edge, left_edge)
    right_final = jnp.where(bending < -bound_cap, 3.0 * middle - 2.0 * left_edge, right_edge)
    steepness = right_final - left_final
    curvature = 6.0 * middle - 3.0 * (left_final + right_final)
    from_left = cut_along(right_final, 0, length + 1, along) - 0.5 * courant * (
        cut_along(steepness, 0, length + 1, along) - (1.0 - (2.0 / 3.0) * courant) * cut_along(curvature, 0, length + 1, along))
    reverse = -courant
    from_right = cut_along(left_final, 1, length + 1, along) + 0.5 * reverse * (
        cut_along(steepness, 1, length + 1, along) + (1.0 - (2.0 / 3.0) * reverse) * cut_along(curvature, 1, length + 1, along))
    face_flux = courant * jnp.where(courant > 0.0, from_left, from_right)
    face_flux = face_flux * cut_along(wet_cells, 0, length + 1, along) * cut_along(wet_cells, 1, length + 1, along)
    return cut_along(tracer, 3, length, along) - (cut_along(face_flux, 1, length, along) - cut_along(face_flux, 0, length, along))


def laplace(source, wet_cells):
    centre = source[..., 1:-1, 1:-1]
    wet_centre = wet_cells[..., 1:-1, 1:-1]
    total = wet_centre * wet_cells[..., 2:, 1:-1] * (source[..., 2:, 1:-1] - centre)
    total = total + wet_centre * wet_cells[..., :-2, 1:-1] * (source[..., :-2, 1:-1] - centre)
    total = total + wet_centre * wet_cells[..., 1:-1, 2:] * (source[..., 1:-1, 2:] - centre)
    total = total + wet_centre * wet_cells[..., 1:-1, :-2] * (source[..., 1:-1, :-2] - centre)
    return total


def wrap_lon(source, width):
    return jnp.concatenate([source[..., -width:], source, source[..., :width]], axis=-1)


def close_lat(source, width, sign_value):
    row_count = source.shape[-2]
    south_rows = jnp.zeros_like(source[..., :width, :])
    north_rows = sign_value * source[..., row_count - width:, :][..., ::-1, :][..., ::-1]
    return jnp.concatenate([south_rows, source, north_rows], axis=-2)


def reference(potential_warmth, saltiness_anomaly, zonal_face_fraction, poleward_face_fraction, water_indicator, water_depth_layers, hyperdiffusion_factor):
    depth_stack = (water_indicator * water_depth_layers).astype(jnp.float32)
    layerwise_entries = jnp.arange(DEPTH_LAYERS, dtype=jnp.float32)

    def one_layer(packed):
        heat, salt_level, zonal, meridional, friction_coef, level_value = packed
        wet_cells = (level_value < depth_stack).astype(jnp.float32)
        tracers = jnp.stack([heat, salt_level])
        tracer_ext = wrap_lon(tracers, 3)
        courant_x = wrap_lon(zonal, 1)[:, :MERIDIAN_TOTAL + 1]
        wet_x = wrap_lon(wet_cells, 1)
        swept_x = parabolic_update(tracer_ext, courant_x, wet_x, MERIDIAN_TOTAL, -1)
        swept_ext = close_lat(swept_x, 3, 1.0)
        courant_y = close_lat(meridional, 1, -1.0)[:PARALLEL_TOTAL + 1, :]
        wet_y = close_lat(wet_cells, 1, 1.0)
        swept_y = parabolic_update(swept_ext, courant_y, wet_y, PARALLEL_TOTAL, -2)
        velocity = jnp.stack([zonal, meridional])
        wet_one = close_lat(wrap_lon(wet_cells, 1), 1, 1.0)
        inner = laplace(close_lat(wrap_lon(velocity, 1), 1, -1.0), wet_one)
        fourth = laplace(close_lat(wrap_lon(inner, 1), 1, -1.0), wet_one)
        velocity_next = velocity - friction_coef * fourth
        return swept_y[0], swept_y[1], velocity_next[0], velocity_next[1]

    transported_warmth, transported_saltiness, zonal_flow_damped, poleward_flow_damped = lax.map(
        one_layer, (potential_warmth, saltiness_anomaly, zonal_face_fraction, poleward_face_fraction, hyperdiffusion_factor, layerwise_entries))
    return transported_warmth, transported_saltiness, zonal_flow_damped, poleward_flow_damped
```

```python
import functools

import jax
import jax.numpy as jnp
from jax import lax
from jax.experimental import pallas as pl
from jax.experimental.pallas import tpu as pltpu
from jax.sharding import PartitionSpec as P

K, J, W = 16, 16, 128
WIN = 6
SEND_ROWS = 23
F32 = jnp.float32


def lanes():
    return lax.broadcasted_iota(jnp.int32, (K, W), 1)


def levels():
    return lax.broadcasted_iota(jnp.int32, (K, W), 0).astype(F32)


def low_half(lane):
    return lane - WIN * ((lane * 43) >> 8) < WIN // 2


def roll(x, shift):
    shift %= W
    return x if shift == 0 else pltpu.roll(x, shift, 1)


def load_row(ref, j):
    return ref[pl.ds(j, K, stride=J), :]


def store_row(ref, j, value):
    ref[pl.ds(j, K, stride=J), :] = value


def depth_row(indicator, layers, j):
    row = (indicator[j : j + 1, :] * layers[j : j + 1, :]).astype(F32)
    return jnp.broadcast_to(row, (K, W))


def wet_of(depth):
    return jnp.where(levels() < depth, 1.0, 0.0).astype(F32)


def unpack(packed, j):
    return roll(packed, -(WIN * j + 3))


def east(x, halo, lane):
    return roll(jnp.where(lane < 1, halo, x), -1)


def west(x, halo, lane):
    return roll(jnp.where(lane == W - 1, halo, x), 1)


def edge_between(far_left, near_left, near_right, far_right):
    edge = (7.0 / 12.0) * (near_left + near_right) - (1.0 / 12.0) * (far_left + far_right)
    return jnp.clip(edge, jnp.minimum(near_left, near_right), jnp.maximum(near_left, near_right))


def limited(q, left, right):
    flat = (right - q) * (q - left) <= 0.0
    left = jnp.where(flat, q, left)
    right = jnp.where(flat, q, right)
    steep = right - left
    bend = steep * (q - 0.5 * (left + right))
    cap = steep * steep * (1.0 / 6.0)
    q3 = 3.0 * q
    left_out = jnp.where(bend > cap, q3 - 2.0 * right, left)
    right_out = jnp.where(bend < -cap, q3 - 2.0 * left, right)
    return left_out, right_out, right_out - left_out, 6.0 * q - 3.0 * (left_out + right_out)


def out_right(cell, c):
    _, right, steep, curve = cell
    return right - 0.5 * c * (steep - (1.0 - (2.0 / 3.0) * c) * curve)


def out_left(cell, c):
    left, _, steep, curve = cell
    return left - 0.5 * c * (steep + (1.0 + (2.0 / 3.0) * c) * curve)


def pack_columns(rows):
    lane = lanes()
    packed = jnp.zeros((K, W), F32)
    for j, row in enumerate(rows):
        mine = (lane >= WIN * j) & (lane < WIN * j + WIN)
        packed = jnp.where(mine, roll(row, WIN * j + 3), packed)
    return packed


def pack_kernel(t_ref, s_ref, u_ref, v_ref, ind_ref, lay_ref, own_ref, ev_ref, od_ref):
    fields = [pack_columns([load_row(r, j) for j in range(J)]) for r in (t_ref, s_ref, u_ref)]
    fields.append(pack_columns([depth_row(ind_ref, lay_ref, j) for j in range(J)]))
    fields.append(pack_columns([load_row(v_ref, j) for j in range(J)]))
    for n, x in enumerate(fields):
        own_ref[:, n * W : (n + 1) * W] = x
    t, s, u, d, v = fields
    low = low_half(lanes())
    even = (lax.axis_index("lon") & 1) == 0
    for n, (a, b) in enumerate(((t, s), (u, d), (v, v))):
        to_east = jnp.where(low, a, roll(b, 3))
        to_west = jnp.where(low, roll(b, -3), a)
        at = slice(n * W, (n + 1) * W)
        ev_ref[:, at] = jnp.where(even, to_east, to_west)
        od_ref[:, at] = jnp.where(even, to_west, to_east)


def seams(own_ref, ev_ref, od_ref):
    low = low_half(lanes())
    even = (lax.axis_index("lon") & 1) == 0
    mate = pl.multiple_of(jnp.where(even, K, 0), K)
    out = []
    for n in range(5):
        at = slice((n // 2) * W, (n // 2 + 1) * W)
        ev = ev_ref[pl.ds(mate, K), at]
        od = od_ref[:, at]
        from_west = jnp.where(even, od, ev)
        from_east = jnp.where(even, ev, od)
        if n in (1, 3):
            from_west, from_east = roll(from_west, -3), roll(from_east, 3)
        own = own_ref[:, n * W : (n + 1) * W]
        out.append(
            (
                jnp.where(low, from_west, from_east),
                jnp.where(low, from_west, own),
                jnp.where(low, own, from_east),
            )
        )
    return out


def seam_flux(q, c, wet):
    edge = edge_between(roll(q, 1), q, roll(q, -1), roll(q, -2))
    cell = limited(q, roll(edge, 1), edge)
    flux = jnp.where(c > 0.0, out_right(cell, c), roll(out_left(cell, roll(c, 1)), -1))
    return edge, c * wet * roll(wet, -1) * flux


class Zonal:
    def __init__(self, packs, u_ref, ind_ref, lay_ref):
        self.packs, self.u_ref, self.ind, self.lay = packs, u_ref, ind_ref, lay_ref
        lane = lanes()
        third = lane - WIN * ((lane * 43) >> 8) == 2
        _, uw, ue = packs[2]
        _, dw, de = packs[3]
        ww, we = wet_of(dw), wet_of(de)
        self.fix = []
        for n in range(2):
            edge_w, flux_w = seam_flux(packs[n][1], uw, ww)
            _, flux_e = seam_flux(packs[n][2], ue, we)
            self.fix.append((jnp.where(third, flux_e, roll(edge_w, 1)), flux_w))

    def row(self, refs, j):
        lane = lanes()
        u = load_row(self.u_ref, j)
        wet = wet_of(depth_row(self.ind, self.lay, j))
        halo_wet = wet_of(unpack(self.packs[3][0], j))
        c_west = west(u, unpack(self.packs[2][0], j), lane)
        face = u * wet * east(wet, halo_wet, lane)
        forward = u > 0.0
        out = []
        for n, ref in enumerate(refs):
            q = load_row(ref, j)
            halo = unpack(self.packs[n][0], j)
            fix, flux_in = (unpack(x, j) for x in self.fix[n])
            edge = edge_between(
                west(q, halo, lane),
                q,
                east(q, halo, lane),
                roll(jnp.where(lane < 2, halo, q), -2),
            )
            cell = limited(q, jnp.where(lane == 0, fix, roll(edge, 1)), edge)
            flux = face * jnp.where(
                forward, out_right(cell, u), roll(out_left(cell, c_west), -1)
            )
            last = lane == W - 1
            flux_west = roll(jnp.where(last, flux_in, flux), 1)
            out.append(q - (jnp.where(last, fix, flux) - flux_west))
        return out


def zonal_lap(f, halo, wet, halo_wet, lane):
    grad = wet * east(wet, halo_wet, lane) * (east(f, halo, lane) - f)
    grad_w = wet * west(wet, halo_wet, lane) * (f - west(f, halo, lane))
    return grad - grad_w


def seam_lap(f, wet):
    total = None
    for shift in (1, -1, WIN, -WIN):
        term = wet * roll(wet, shift) * (roll(f, shift) - f)
        total = term if total is None else total + term
    return total


def edge_kernel(
    t_ref, s_ref, u_ref, v_ref, ind_ref, lay_ref, own_ref, ev_ref, od_ref, swept_ref, e_ref, o_ref
):
    lane = lanes()
    packs = seams(own_ref, ev_ref, od_ref)
    zonal = Zonal(packs, u_ref, ind_ref, lay_ref)
    halves = []
    for rows in ((J - 1, J - 2, J - 3), (0, 1, 2)):
        planes = [zonal.row((t_ref, s_ref), j) for j in rows]
        for j, (t, s) in zip(rows, planes):
            swept_ref[j if j < 3 else j - 10] = t
            swept_ref[6 + (j if j < 3 else j - 10)] = s
        half = [p[0] for p in planes] + [p[1] for p in planes]
        j, inward = rows[0], rows[1]
        depth = depth_row(ind_ref, lay_ref, j)
        halo_depth = unpack(packs[3][0], j)
        wet, halo_wet = wet_of(depth), wet_of(halo_depth)
        to_inner = wet * wet_of(depth_row(ind_ref, lay_ref, inward))
        corner = roll(halo_depth, 2)
        corner = jnp.where(lane < W // 2, corner, roll(halo_depth, -2))
        for ref, pack, reach in ((v_ref, packs[4], 1), (u_ref, packs[2], 0)):
            halo = unpack(pack[0], j)
            f = load_row(ref, j)
            partial = zonal_lap(f, halo, wet, halo_wet, lane) + to_inner * (load_row(ref, inward) - f)
            half[6:6] = [f, partial]
            take = jnp.where(lane < W // 2, roll(halo, reach), roll(halo, -reach))
            corner = jnp.where((lane == reach) | (lane == W - 1 - reach), take, corner)
        halves.append((half + [corner], depth[:8]))
    lat = lax.axis_index("lat")
    even = (lat & 1) == 0
    top = lat == lax.axis_size("lat") - 1
    (north, north_d), (south, south_d) = halves
    for n, (a, b) in enumerate(zip(north, south)):
        e_ref[2 * n : 2 * n + 2] = jnp.where(even, a, b).reshape(2, 8, W)
        o_ref[2 * n : 2 * n + 2] = jnp.where(even, b, a).reshape(2, 8, W)
    e_ref[SEND_ROWS - 1] = jnp.where(even, north_d, south_d)
    o_ref[SEND_ROWS - 1] = jnp.where(even, south_d, north_d)

    @pl.when(top)
    def _():
        mirror = W - 1 - lax.broadcasted_iota(jnp.int32, (8, W), 1)
        lane8 = lax.broadcasted_iota(jnp.int32, (8, W), 1)
        for n in range(SEND_ROWS):
            x = jnp.take_along_axis(o_ref[n], mirror, axis=1)
            if 12 <= n < 20:
                x = -x
            elif 20 <= n < 22:
                x = jnp.where((lane8 < 2) | (lane8 > W - 3), -x, x)
            o_ref[n] = x


def merid_cell(q, j):
    return limited(
        q[j],
        edge_between(q[j - 2], q[j - 1], q[j], q[j + 1]),
        edge_between(q[j - 1], q[j], q[j + 1], q[j + 2]),
    )


AUX_TRACER, AUX_FLOW = 12, 10


def inner_kernel(
    t_ref,
    s_ref,
    u_ref,
    v_ref,
    ind_ref,
    lay_ref,
    visc_ref,
    own_ref,
    ev_ref,
    od_ref,
    swept_ref,
    t_out,
    s_out,
    u_out,
    v_out,
    aux_ref,
):
    lane = lanes()
    packs = seams(own_ref, ev_ref, od_ref)
    zonal = Zonal(packs, u_ref, ind_ref, lay_ref)
    rows = [{}, {}]
    for j in (0, 1, 2, 13, 14, 15):
        for n in range(2):
            rows[n][j] = swept_ref[6 * n + (j if j < 3 else j - 10)]
    for j in range(3, 13):
        rows[0][j], rows[1][j] = zonal.row((t_ref, s_ref), j)
    wet = [wet_of(depth_row(ind_ref, lay_ref, j)) for j in range(J)]
    for n, out in enumerate((t_out, s_out)):
        q = rows[n]
        for at, j in enumerate((0, 1, 2, 3, 4, 11, 12, 13, 14, 15)):
            aux_ref[AUX_TRACER * n + at] = q[j]
        cell = merid_cell(q, 2)
        before = None
        for j in range(2, 13):
            after = merid_cell(q, j + 1)
            c = load_row(v_ref, j)
            flux = c * wet[j] * wet[j + 1] * jnp.where(c > 0.0, out_right(cell, c), out_left(after, c))
            if j == 2:
                aux_ref[AUX_TRACER * n + 10] = flux
            else:
                store_row(out, j, q[j] - (flux - before))
            if j == 12:
                aux_ref[AUX_TRACER * n + 11] = flux
            cell, before = after, flux
    wet_w, wet_e = wet_of(packs[3][1]), wet_of(packs[3][2])
    low = low_half(lane)
    visc = viscosity(visc_ref)
    halo_wet = [wet_of(unpack(packs[3][0], j)) for j in range(J)]
    for n, (ref, pack, out) in enumerate(((u_ref, packs[2], u_out), (v_ref, packs[4], v_out))):
        base = 2 * AUX_TRACER + AUX_FLOW * n
        halo_lap = jnp.where(low, seam_lap(pack[1], wet_w), seam_lap(pack[2], wet_e))
        f = [load_row(ref, j) for j in range(J)]
        lap = []
        step = None
        for j in range(J):
            total = zonal_lap(f[j], unpack(pack[0], j), wet[j], halo_wet[j], lane)
            if step is not None:
                total = total - step
            if j < J - 1:
                step = wet[j] * wet[j + 1] * (f[j + 1] - f[j])
                total = total + step
            lap.append(total)
        step = None
        for j in range(1, J - 1):
            total = zonal_lap(lap[j], unpack(halo_lap, j), wet[j], halo_wet[j], lane)
            if step is not None:
                total = total - step
            if j < J - 2:
                step = wet[j] * wet[j + 1] * (lap[j + 1] - lap[j])
                total = total + step
            if j == 1:
                aux_ref[base + 2] = total
            elif j == J - 2:
                aux_ref[base + 5] = total
            else:
                store_row(out, j, f[j] - visc * total)
        aux_ref[base + 0] = lap[0]
        aux_ref[base + 1] = lap[1]
        aux_ref[base + 3] = lap[J - 1]
        aux_ref[base + 4] = lap[J - 2]
        aux_ref[base + 6] = unpack(halo_lap, 0)
        aux_ref[base + 7] = unpack(halo_lap, J - 1)
        aux_ref[base + 8] = unpack(pack[0], 0)
        aux_ref[base + 9] = unpack(pack[0], J - 1)
    aux_ref[2 * AUX_TRACER + 2 * AUX_FLOW] = halo_wet[0]
    aux_ref[2 * AUX_TRACER + 2 * AUX_FLOW + 1] = halo_wet[J - 1]


def viscosity(visc_ref):
    level = lax.broadcasted_iota(jnp.int32, (K, W), 0)
    visc = jnp.zeros((K, W), F32)
    for k in range(K):
        visc = jnp.where(level == k, visc_ref[k], visc)
    return visc


def finish_kernel(
    u_ref,
    v_ref,
    ind_ref,
    lay_ref,
    visc_ref,
    t_in,
    s_in,
    u_in,
    v_in,
    aux_ref,
    e_ref,
    o_ref,
    t_out,
    s_out,
    u_out,
    v_out,
):
    lane = lanes()
    for src, dst, lo in ((t_in, t_out, 3), (s_in, s_out, 3), (u_in, u_out, 2), (v_in, v_out, 2)):
        for j in range(lo, J - lo):
            store_row(dst, j, load_row(src, j))
    even = (lax.axis_index("lat") & 1) == 0
    visc = viscosity(visc_ref)
    halo_at = 2 * AUX_TRACER + 2 * AUX_FLOW

    def recv(side, n):
        e, o = e_ref[2 * n : 2 * n + 2].reshape(K, W), o_ref[2 * n : 2 * n + 2].reshape(K, W)
        return jnp.where(even, e, o) if side == 0 else jnp.where(even, o, e)

    def recv_depth(side):
        e, o = e_ref[SEND_ROWS - 1], o_ref[SEND_ROWS - 1]
        x = jnp.where(even, e, o) if side == 0 else jnp.where(even, o, e)
        return jnp.concatenate([x, x], axis=0)

    for side in (0, 1):
        edge, inward = (J - 1, J - 2) if side == 0 else (0, 1)
        wet = {j: wet_of(depth_row(ind_ref, lay_ref, j)) for j in ((12, 13, 14, 15) if side == 0 else (0, 1, 2, 3))}
        out_depth = recv_depth(side)
        wet_out = wet_of(out_depth)
        v_beyond = recv(side, 8)
        corner = recv(side, 10)
        for n, out in enumerate((t_out, s_out)):
            aux = AUX_TRACER * n
            if side == 0:
                q = {11: aux_ref[aux + 5], 12: aux_ref[aux + 6], 13: aux_ref[aux + 7], 14: aux_ref[aux + 8], 15: aux_ref[aux + 9]}
                q.update({16 + m: recv(side, 3 * n + m) for m in range(3)})
                wet[16] = wet_out
                before, faces = aux_ref[aux + 11], (13, 14, 15)
            else:
                q = {j: aux_ref[aux + j] for j in range(5)}
                q.update({-1 - m: recv(side, 3 * n + m) for m in range(3)})
                wet[-1] = wet_out
                before, faces = None, (-1, 0, 1)
            cell = merid_cell(q, faces[0])
            for j in faces:
                after = merid_cell(q, j + 1)
                c = v_beyond if j < 0 else load_row(v_ref, j)
                flux = c * wet[j] * wet[j + 1] * jnp.where(c > 0.0, out_right(cell, c), out_left(after, c))
                if before is not None:
                    store_row(out, j, q[j] - (flux - before))
                cell, before = after, flux
            if side == 1:
                store_row(out, 2, q[2] - (aux_ref[aux + 10] - before))
        halo_wet = aux_ref[halo_at + (1 if side == 0 else 0)]
        corner_depth = jnp.where(lane < W // 2, roll(corner, -2), roll(corner, 2))
        corner_wet = halo_wet * wet_of(corner_depth)
        for n, (ref, out) in enumerate(((u_ref, u_out), (v_ref, v_out))):
            base = 2 * AUX_TRACER + AUX_FLOW * n
            at = (3, 4, 5, 7, 9) if side == 0 else (0, 1, 2, 6, 8)
            lap_edge, lap_in, partial, halo_lap, halo_f = (aux_ref[base + a] for a in at)
            f, f_in = load_row(ref, edge), load_row(ref, inward)
            f_out, lap_out = recv(side, 6 + 2 * n), recv(side, 7 + 2 * n)
            step = wet[edge] * wet_out * (f_out - f)
            lap_edge = lap_edge + step
            lap_out = lap_out - step
            if n == 0:
                corner_f = corner
            else:
                corner_f = jnp.where(lane < W // 2, roll(corner, -1), roll(corner, 1))
            halo_lap = halo_lap + corner_wet * (corner_f - halo_f)
            inner_step = wet[edge] * wet[inward] * (lap_in - lap_edge)
            total = (
                zonal_lap(lap_edge, halo_lap, wet[edge], halo_wet, lane)
                + inner_step
                + wet[edge] * wet_out * (lap_out - lap_edge)
            )
            store_row(out, edge, f - visc * total)
            store_row(out, inward, f_in - visc * (partial - inner_step))


VMEM = pl.BlockSpec(memory_space=pltpu.VMEM)
SMEM = pl.BlockSpec(memory_space=pltpu.SMEM)


def call(kernel, in_specs, out_shapes, flops, *args):
    return pl.pallas_call(
        kernel,
        out_shape=[jax.ShapeDtypeStruct(s, F32) for s in out_shapes],
        in_specs=in_specs,
        out_specs=[VMEM] * len(out_shapes),
        cost_estimate=pl.CostEstimate(flops=flops, bytes_accessed=1 << 20, transcendentals=0),
        compiler_params=pltpu.CompilerParams(vmem_limit_bytes=32 << 20),
    )(*args)


def body(t, s, u, v, ind, lay, visc):
    flat = (K * J, W)
    t, s, u, v = (x.reshape(flat) for x in (t, s, u, v))
    n_lon, n_lat = lax.axis_size("lon"), lax.axis_size("lat")
    own, ev, od = call(
        pack_kernel, [VMEM] * 6, [(K, 5 * W), (K, 3 * W), (K, 3 * W)], 1 << 20, t, s, u, v, ind, lay
    )
    od = lax.ppermute(od, "lon", [(i, (((i + 1) ^ 1) - 1) % n_lon) for i in range(n_lon)])
    ev = lax.all_gather(
        ev, "lon", axis_index_groups=[[i, i + 1] for i in range(0, n_lon, 2)], tiled=True
    )
    swept, edge_e, edge_o = call(
        edge_kernel,
        [VMEM] * 9,
        [(12, K, W), (SEND_ROWS, 8, W), (SEND_ROWS, 8, W)],
        1 << 20,
        *(t, s, u, v, ind, lay, own, ev, od),
    )
    pairs_e, pairs_o = [], []
    for p in range(n_lon):
        for l in range(n_lat):
            pairs_e.append((p * n_lat + l, p * n_lat + (l ^ 1)))
            if 0 < l < n_lat - 1:
                pairs_o.append((p * n_lat + l, p * n_lat + ((l + 1) ^ 1) - 1))
        top = n_lat - 1
        pairs_o.append((p * n_lat + top, (n_lon - 1 - p) * n_lat + top))
    got_o = lax.ppermute(edge_o, ("lon", "lat"), pairs_o)
    got_e = lax.ppermute(edge_e, ("lon", "lat"), pairs_e)
    *parts, aux = call(
        inner_kernel,
        [VMEM] * 6 + [SMEM] + [VMEM] * 4,
        [flat] * 4 + [(2 * AUX_TRACER + 2 * AUX_FLOW + 2, K, W)],
        1 << 24,
        *(t, s, u, v, ind, lay, visc, own, ev, od, swept),
    )
    outs = call(
        finish_kernel,
        [VMEM] * 4 + [SMEM] + [VMEM] * 7,
        [flat] * 4,
        1 << 22,
        *(u, v, ind, lay, visc, *parts, aux, got_e, got_o),
    )
    return tuple(x.reshape(K, J, W) for x in outs)


def solution(mesh):
    field, flat = P(None, "lat", "lon"), P("lat", "lon")
    return jax.shard_map(
        body,
        mesh=mesh,
        in_specs=(field, field, field, field, flat, flat, P()),
        out_specs=(field,) * 4,
        check_vma=False,
    )
```

```python
import jax
import jax.numpy as jnp
from jax import lax
from jax.experimental import pallas as pl
from jax.experimental.pallas import tpu as pltpu
from jax.sharding import PartitionSpec as P

K, J, W = 16, 16, 128
WIN = 6
SEND_ROWS = 23
F32 = jnp.float32


def lanes():
    return lax.broadcasted_iota(jnp.int32, (K, W), 1)


def levels():
    return lax.broadcasted_iota(jnp.int32, (K, W), 0).astype(F32)


def low_half(lane):
    return lane - WIN * ((lane * 43) >> 8) < WIN // 2


def roll(x, shift):
    shift %= W
    return x if shift == 0 else pltpu.roll(x, shift, 1)


def load_row(ref, j):
    return ref[pl.ds(j, K, stride=J), :]


def store_row(ref, j, value):
    ref[pl.ds(j, K, stride=J), :] = value


def depth_row(depth_ref, j):
    return jnp.broadcast_to(depth_ref[pl.ds(j, 1), :], (K, W))


def wet_of(depth):
    return jnp.where(levels() < depth, 1.0, 0.0).astype(F32)


def unpack(packed, j):
    return roll(packed, -(WIN * j + 3))


def east(x, halo, lane):
    return roll(jnp.where(lane < 1, halo, x), -1)


def west(x, halo, lane):
    return roll(jnp.where(lane == W - 1, halo, x), 1)


def minmod(a, b):
    return jnp.maximum(jnp.minimum(a, jnp.maximum(b, 0.0)), jnp.minimum(b, 0.0))


def rise_fall(before, here, after):
    rise = minmod(0.5 * here + (1.0 / 12.0) * (before - after), here)
    return rise, here - rise


def limited(fall, rise):
    return minmod(fall, rise + rise), minmod(rise, fall + fall)


def weights(c):
    size = jnp.abs(c)
    rest = 1.0 - size
    return size * rest, rest * rest


def pack_columns(rows):
    lane = lanes()
    packed = jnp.zeros((K, W), F32)
    for j, row in enumerate(rows):
        mine = (lane >= WIN * j) & (lane < WIN * j + WIN)
        packed = jnp.where(mine, roll(row, WIN * j + 3), packed)
    return packed


def pack_kernel(*refs):
    sources, (t_ref, s_ref, u_ref, v_ref, d_ref, own_ref, ev_ref, od_ref) = refs[:6], refs[6:14]
    ind_ref, lay_ref, sems = refs[14:]
    copies = [
        pltpu.make_async_copy(src, dst, sems.at[n])
        for n, (src, dst) in enumerate(zip(sources, (t_ref, s_ref, u_ref, v_ref, ind_ref, lay_ref)))
    ]
    for n in (4, 5, 0, 1, 2, 3):
        copies[n].start()
    copies[4].wait()
    copies[5].wait()
    d_ref[...] = (ind_ref[...] * lay_ref[...]).astype(F32)
    d = pack_columns([depth_row(d_ref, j) for j in range(J)])
    fields = []
    for n, ref in enumerate((t_ref, s_ref, u_ref, v_ref)):
        copies[n].wait()
        fields.append(pack_columns([load_row(ref, j) for j in range(J)]))
    fields.insert(3, d)
    for n, x in enumerate(fields):
        own_ref[:, n * W : (n + 1) * W] = x
    t, s, u, d, v = fields
    low = low_half(lanes())
    even = (lax.axis_index("lon") & 1) == 0
    for n, (a, b) in enumerate(((t, s), (u, d), (v, v))):
        to_east = jnp.where(low, a, roll(b, 3))
        to_west = jnp.where(low, roll(b, -3), a)
        at = slice(n * W, (n + 1) * W)
        ev_ref[:, at] = jnp.where(even, to_east, to_west)
        od_ref[:, at] = jnp.where(even, to_west, to_east)


def seams(own_ref, ev_ref, od_ref):
    low = low_half(lanes())
    even = (lax.axis_index("lon") & 1) == 0
    mate = pl.multiple_of(jnp.where(even, K, 0), K)
    out = []
    for n in range(5):
        at = slice((n // 2) * W, (n // 2 + 1) * W)
        ev = ev_ref[pl.ds(mate, K), at]
        od = od_ref[:, at]
        from_west = jnp.where(even, od, ev)
        from_east = jnp.where(even, ev, od)
        if n in (1, 3):
            from_west, from_east = roll(from_west, -3), roll(from_east, 3)
        own = own_ref[:, n * W : (n + 1) * W]
        out.append(
            (
                jnp.where(low, from_west, from_east),
                jnp.where(low, from_west, own),
                jnp.where(low, own, from_east),
            )
        )
    return out


def seam_flux(q, c, wet):
    step = roll(q, -1) - q
    rise, fall = rise_fall(roll(step, 1), step, roll(step, -1))
    down, up = limited(roll(fall, 1), rise)
    near, far = weights(c)
    out_right = q + (near * down + far * up)
    near, far = weights(roll(c, 1))
    out_left = q - (near * up + far * down)
    return fall, c * wet * roll(wet, -1) * jnp.where(c > 0.0, out_right, roll(out_left, -1))


class Zonal:
    def __init__(self, packs, u_ref, d_ref):
        self.packs, self.u_ref, self.d_ref = packs, u_ref, d_ref
        lane = lanes()
        third = lane - WIN * ((lane * 43) >> 8) == 2
        _, uw, ue = packs[2]
        _, dw, de = packs[3]
        ww, we = wet_of(dw), wet_of(de)
        self.fix = []
        for n in range(2):
            fall_w, flux_w = seam_flux(packs[n][1], uw, ww)
            _, flux_e = seam_flux(packs[n][2], ue, we)
            self.fix.append((jnp.where(third, flux_e, roll(fall_w, 1)), flux_w))

    def row(self, refs, j):
        lane = lanes()
        last = lane == W - 1
        u = load_row(self.u_ref, j)
        wet = wet_of(depth_row(self.d_ref, j))
        halo_wet = wet_of(unpack(self.packs[3][0], j))
        near, far = weights(u)
        near_w, far_w = weights(west(u, unpack(self.packs[2][0], j), lane))
        face = u * wet * east(wet, halo_wet, lane)
        forward = u > 0.0
        out = []
        for n, ref in enumerate(refs):
            q = load_row(ref, j)
            halo = unpack(self.packs[n][0], j)
            fix, flux_in = (unpack(x, j) for x in self.fix[n])
            right = east(q, halo, lane)
            rise, fall = rise_fall(
                q - west(q, halo, lane),
                right - q,
                roll(jnp.where(lane < 2, halo, q), -2) - right,
            )
            down, up = limited(jnp.where(lane == 0, fix, roll(fall, 1)), rise)
            flux = face * jnp.where(
                forward, q + (near * down + far * up), roll(q - (near_w * up + far_w * down), -1)
            )
            flux_west = roll(jnp.where(last, flux_in, flux), 1)
            out.append(q - (jnp.where(last, fix, flux) - flux_west))
        return out


def zonal_masks(wet, halo_wet, lane):
    return wet * east(wet, halo_wet, lane), wet * west(wet, halo_wet, lane)


def zonal_lap(f, halo, masks, lane):
    return masks[0] * (east(f, halo, lane) - f) - masks[1] * (f - west(f, halo, lane))


def seam_lap(f, wet):
    total = None
    for shift in (1, -1, WIN, -WIN):
        term = wet * roll(wet, shift) * (roll(f, shift) - f)
        total = term if total is None else total + term
    return total


def edge_kernel(
    t_ref, s_ref, u_ref, v_ref, d_ref, own_ref, ev_ref, od_ref, swept_ref, e_ref, o_ref
):
    lane = lanes()
    packs = seams(own_ref, ev_ref, od_ref)
    zonal = Zonal(packs, u_ref, d_ref)
    halves = []
    for rows in ((J - 1, J - 2, J - 3), (0, 1, 2)):
        planes = [zonal.row((t_ref, s_ref), j) for j in rows]
        for j, (t, s) in zip(rows, planes):
            swept_ref[j if j < 3 else j - 10] = t
            swept_ref[6 + (j if j < 3 else j - 10)] = s
        half = [p[0] for p in planes] + [p[1] for p in planes]
        j, inward = rows[0], rows[1]
        depth = depth_row(d_ref, j)
        halo_depth = unpack(packs[3][0], j)
        wet, halo_wet = wet_of(depth), wet_of(halo_depth)
        masks = zonal_masks(wet, halo_wet, lane)
        to_inner = wet * wet_of(depth_row(d_ref, inward))
        corner = roll(halo_depth, 2)
        corner = jnp.where(lane < W // 2, corner, roll(halo_depth, -2))
        for ref, pack, reach in ((v_ref, packs[4], 1), (u_ref, packs[2], 0)):
            halo = unpack(pack[0], j)
            f = load_row(ref, j)
            partial = zonal_lap(f, halo, masks, lane) + to_inner * (load_row(ref, inward) - f)
            half[6:6] = [f, partial]
            take = jnp.where(lane < W // 2, roll(halo, reach), roll(halo, -reach))
            corner = jnp.where((lane == reach) | (lane == W - 1 - reach), take, corner)
        halves.append((half + [corner], depth[:8]))
    lat = lax.axis_index("lat")
    even = (lat & 1) == 0
    top = lat == lax.axis_size("lat") - 1
    (north, north_d), (south, south_d) = halves
    for n, (a, b) in enumerate(zip(north, south)):
        e_ref[2 * n : 2 * n + 2] = jnp.where(even, a, b).reshape(2, 8, W)
        o_ref[2 * n : 2 * n + 2] = jnp.where(even, b, a).reshape(2, 8, W)
    e_ref[SEND_ROWS - 1] = jnp.where(even, north_d, south_d)
    o_ref[SEND_ROWS - 1] = jnp.where(even, south_d, north_d)

    @pl.when(top)
    def _():
        mirror = W - 1 - lax.broadcasted_iota(jnp.int32, (8, W), 1)
        lane8 = lax.broadcasted_iota(jnp.int32, (8, W), 1)
        for n in range(SEND_ROWS):
            x = jnp.take_along_axis(o_ref[n], mirror, axis=1)
            if 12 <= n < 20:
                x = -x
            elif 20 <= n < 22:
                x = jnp.where((lane8 < 2) | (lane8 > W - 3), -x, x)
            o_ref[n] = x


def merid_cell(step, fall_before, j):
    rise, fall = rise_fall(step[j - 1], step[j], step[j + 1])
    down, up = limited(fall_before, rise)
    return down, up, fall


def merid_flux(c, wet_pair, q, q_next, cell, cell_next):
    forward = c > 0.0
    rest = 1.0 - jnp.abs(c)
    square = rest * rest
    near = jnp.where(forward, cell[0], cell_next[1])
    far = jnp.where(forward, cell[1], cell_next[0])
    return c * wet_pair * (
        jnp.where(forward, q, q_next) + (c * rest * near + jnp.where(forward, square, -square) * far)
    )


AUX_TRACER, AUX_FLOW = 12, 10


def inner_kernel(
    t_ref,
    s_ref,
    u_ref,
    v_ref,
    d_ref,
    visc_hbm,
    own_ref,
    ev_ref,
    od_ref,
    swept_ref,
    t_out,
    s_out,
    u_out,
    v_out,
    aux_ref,
    visc_ref,
    sem,
):
    copy = pltpu.make_async_copy(visc_hbm, visc_ref, sem)
    copy.start()
    lane = lanes()
    packs = seams(own_ref, ev_ref, od_ref)
    zonal = Zonal(packs, u_ref, d_ref)
    rows = [{}, {}]
    for j in (0, 1, 2, 13, 14, 15):
        for n in range(2):
            rows[n][j] = swept_ref[6 * n + (j if j < 3 else j - 10)]
    for j in range(3, 13):
        rows[0][j], rows[1][j] = zonal.row((t_ref, s_ref), j)
    wet = [wet_of(depth_row(d_ref, j)) for j in range(J)]
    for n, out in enumerate((t_out, s_out)):
        q = rows[n]
        for at, j in enumerate((0, 1, 2, 3, 4, 11, 12, 13, 14, 15)):
            aux_ref[AUX_TRACER * n + at] = q[j]
        step = [q[j + 1] - q[j] for j in range(J - 1)]
        cell = merid_cell(step, rise_fall(step[0], step[1], step[2])[1], 2)
        before = None
        for j in range(2, 13):
            after = merid_cell(step, cell[2], j + 1)
            flux = merid_flux(load_row(v_ref, j), wet[j] * wet[j + 1], q[j], q[j + 1], cell, after)
            if j == 2:
                aux_ref[AUX_TRACER * n + 10] = flux
            else:
                store_row(out, j, q[j] - (flux - before))
            if j == 12:
                aux_ref[AUX_TRACER * n + 11] = flux
            cell, before = after, flux
    wet_w, wet_e = wet_of(packs[3][1]), wet_of(packs[3][2])
    low = low_half(lane)
    copy.wait()
    visc = viscosity(visc_ref)
    halo_wet = [wet_of(unpack(packs[3][0], j)) for j in range(J)]
    masks = [zonal_masks(wet[j], halo_wet[j], lane) for j in range(J)]
    pair = [wet[j] * wet[j + 1] for j in range(J - 1)]
    for n, (ref, pack, out) in enumerate(((u_ref, packs[2], u_out), (v_ref, packs[4], v_out))):
        base = 2 * AUX_TRACER + AUX_FLOW * n
        halo_lap = jnp.where(low, seam_lap(pack[1], wet_w), seam_lap(pack[2], wet_e))
        f = [load_row(ref, j) for j in range(J)]
        lap = []
        step = None
        for j in range(J):
            total = zonal_lap(f[j], unpack(pack[0], j), masks[j], lane)
            if step is not None:
                total = total - step
            if j < J - 1:
                step = pair[j] * (f[j + 1] - f[j])
                total = total + step
            lap.append(total)
        step = None
        for j in range(1, J - 1):
            total = zonal_lap(lap[j], unpack(halo_lap, j), masks[j], lane)
            if step is not None:
                total = total - step
            if j < J - 2:
                step = pair[j] * (lap[j + 1] - lap[j])
                total = total + step
            if j == 1:
                aux_ref[base + 2] = total
            elif j == J - 2:
                aux_ref[base + 5] = total
            else:
                store_row(out, j, f[j] - visc * total)
        aux_ref[base + 0] = lap[0]
        aux_ref[base + 1] = lap[1]
        aux_ref[base + 3] = lap[J - 1]
        aux_ref[base + 4] = lap[J - 2]
        aux_ref[base + 6] = unpack(halo_lap, 0)
        aux_ref[base + 7] = unpack(halo_lap, J - 1)
        aux_ref[base + 8] = unpack(pack[0], 0)
        aux_ref[base + 9] = unpack(pack[0], J - 1)
    aux_ref[2 * AUX_TRACER + 2 * AUX_FLOW] = halo_wet[0]
    aux_ref[2 * AUX_TRACER + 2 * AUX_FLOW + 1] = halo_wet[J - 1]
    aux_ref[2 * AUX_TRACER + 2 * AUX_FLOW + 2] = visc


def viscosity(visc_ref):
    level = lax.broadcasted_iota(jnp.int32, (K, W), 0)
    visc = jnp.zeros((K, W), F32)
    for k in range(K):
        visc = jnp.where(level == k, visc_ref[k], visc)
    return visc


def finish_kernel(
    u_ref, v_ref, d_ref, t_in, s_in, u_in, v_in, aux_ref, e_ref, o_ref, *outs
):
    finals, (t_out, s_out, u_out, v_out), sems = outs[:4], outs[4:8], outs[8]
    lane = lanes()
    copies = [
        pltpu.make_async_copy(src, dst, sems.at[n])
        for n, (src, dst) in enumerate(zip((t_out, s_out, u_out, v_out), finals))
    ]
    even = (lax.axis_index("lat") & 1) == 0
    halo_at = 2 * AUX_TRACER + 2 * AUX_FLOW
    visc = aux_ref[halo_at + 2]

    def recv(side, n):
        e, o = e_ref[2 * n : 2 * n + 2].reshape(K, W), o_ref[2 * n : 2 * n + 2].reshape(K, W)
        return jnp.where(even, e, o) if side == 0 else jnp.where(even, o, e)

    def recv_depth(side):
        e, o = e_ref[SEND_ROWS - 1], o_ref[SEND_ROWS - 1]
        x = jnp.where(even, e, o) if side == 0 else jnp.where(even, o, e)
        return jnp.concatenate([x, x], axis=0)

    wet = {j: wet_of(depth_row(d_ref, j)) for j in (0, 1, 2, 13, 14, 15)}
    wet[16], wet[-1] = wet_of(recv_depth(0)), wet_of(recv_depth(1))
    courant = {j: load_row(v_ref, j) for j in (0, 1, 13, 14, 15)}
    courant[-1] = recv(1, 8)
    for n, (src, out) in enumerate(((t_in, t_out), (s_in, s_out))):
        aux = AUX_TRACER * n
        for j in range(3, 13):
            store_row(out, j, load_row(src, j))
        for side in (0, 1):
            if side == 0:
                q = {11 + m: aux_ref[aux + 5 + m] for m in range(5)}
                q.update({16 + m: recv(side, 3 * n + m) for m in range(3)})
                before, faces = aux_ref[aux + 11], (13, 14, 15)
            else:
                q = {j: aux_ref[aux + j] for j in range(5)}
                q.update({-1 - m: recv(side, 3 * n + m) for m in range(3)})
                before, faces = None, (-1, 0, 1)
            step = {j: q[j + 1] - q[j] for j in q if j + 1 in q}
            first = faces[0]
            fall = rise_fall(step[first - 2], step[first - 1], step[first])[1]
            cell = merid_cell(step, fall, first)
            for j in faces:
                after = merid_cell(step, cell[2], j + 1)
                flux = merid_flux(courant[j], wet[j] * wet[j + 1], q[j], q[j + 1], cell, after)
                if before is not None:
                    store_row(out, j, q[j] - (flux - before))
                cell, before = after, flux
            if side == 1:
                store_row(out, 2, q[2] - (aux_ref[aux + 10] - before))
        copies[n].start()
    for n, (ref, src, out) in enumerate(((u_ref, u_in, u_out), (v_ref, v_in, v_out))):
        base = 2 * AUX_TRACER + AUX_FLOW * n
        for j in range(2, 14):
            store_row(out, j, load_row(src, j))
        for side in (0, 1):
            edge, inward, beyond = (15, 14, 16) if side == 0 else (0, 1, -1)
            halo_wet = aux_ref[halo_at + 1 - side]
            corner = recv(side, 10)
            corner_depth = jnp.where(lane < W // 2, roll(corner, -2), roll(corner, 2))
            corner_wet = halo_wet * wet_of(corner_depth)
            masks = zonal_masks(wet[edge], halo_wet, lane)
            at = (3, 4, 5, 7, 9) if side == 0 else (0, 1, 2, 6, 8)
            lap_edge, lap_in, partial, halo_lap, halo_f = (aux_ref[base + a] for a in at)
            f, f_in = load_row(ref, edge), load_row(ref, inward)
            f_out, lap_out = recv(side, 6 + 2 * n), recv(side, 7 + 2 * n)
            across = wet[edge] * wet[beyond]
            step = across * (f_out - f)
            lap_edge = lap_edge + step
            lap_out = lap_out - step
            if n == 0:
                corner_f = corner
            else:
                corner_f = jnp.where(lane < W // 2, roll(corner, -1), roll(corner, 1))
            halo_lap = halo_lap + corner_wet * (corner_f - halo_f)
            inner_step = wet[edge] * wet[inward] * (lap_in - lap_edge)
            total = (
                zonal_lap(lap_edge, halo_lap, masks, lane)
                + inner_step
                + across * (lap_out - lap_edge)
            )
            store_row(out, edge, f - visc * total)
            store_row(out, inward, f_in - visc * (partial - inner_step))
        copies[2 + n].start()
    for copy in copies:
        copy.wait()


VMEM = pl.BlockSpec(memory_space=pltpu.VMEM)
HBM = pl.BlockSpec(memory_space=pltpu.HBM)
FLAT = (K * J, W)
AUX = 2 * AUX_TRACER + 2 * AUX_FLOW + 3


def call(kernel, in_specs, out_specs, out_shapes, flops, args, scratch=()):
    return pl.pallas_call(
        kernel,
        out_shape=[jax.ShapeDtypeStruct(s, F32) for s in out_shapes],
        in_specs=in_specs,
        out_specs=out_specs,
        scratch_shapes=list(scratch),
        cost_estimate=pl.CostEstimate(flops=flops, bytes_accessed=1 << 20, transcendentals=0),
        compiler_params=pltpu.CompilerParams(vmem_limit_bytes=32 << 20),
    )(*args)


def body(t, s, u, v, ind, lay, visc):
    t, s, u, v = (x.reshape(FLAT) for x in (t, s, u, v))
    n_lon, n_lat = lax.axis_size("lon"), lax.axis_size("lat")
    t, s, u, v, depth, own, ev, od = call(
        pack_kernel,
        [HBM] * 6,
        [VMEM] * 8,
        [FLAT] * 4 + [(J, W), (K, 5 * W), (K, 3 * W), (K, 3 * W)],
        1 << 20,
        (t, s, u, v, ind, lay),
        [pltpu.VMEM((J, W), jnp.int32)] * 2 + [pltpu.SemaphoreType.DMA((6,))],
    )
    od = lax.ppermute(od, "lon", [(i, (((i + 1) ^ 1) - 1) % n_lon) for i in range(n_lon)])
    ev = lax.all_gather(
        ev, "lon", axis_index_groups=[[i, i + 1] for i in range(0, n_lon, 2)], tiled=True
    )
    swept, edge_e, edge_o = call(
        edge_kernel,
        [VMEM] * 8,
        [VMEM] * 3,
        [(12, K, W), (SEND_ROWS, 8, W), (SEND_ROWS, 8, W)],
        1 << 20,
        (t, s, u, v, depth, own, ev, od),
    )
    pairs_e, pairs_o = [], []
    top = n_lat - 1
    for p in range(n_lon):
        for l in range(n_lat):
            pairs_e.append((p * n_lat + l, p * n_lat + (l ^ 1)))
            if 0 < l < top:
                pairs_o.append((p * n_lat + l, p * n_lat + ((l + 1) ^ 1) - 1))
        pairs_o.append((p * n_lat + top, (n_lon - 1 - p) * n_lat + top))
    got_o = lax.ppermute(edge_o, ("lon", "lat"), pairs_o)
    got_e = lax.ppermute(edge_e, ("lon", "lat"), pairs_e)
    *parts, aux = call(
        inner_kernel,
        [VMEM] * 5 + [HBM] + [VMEM] * 4,
        [VMEM] * 5,
        [FLAT] * 4 + [(AUX, K, W)],
        1 << 24,
        (t, s, u, v, depth, visc, own, ev, od, swept),
        [pltpu.SMEM((K,), F32), pltpu.SemaphoreType.DMA],
    )
    outs = call(
        finish_kernel,
        [VMEM] * 10,
        [HBM] * 4,
        [FLAT] * 4,
        1 << 22,
        (u, v, depth, *parts, aux, got_e, got_o),
        [pltpu.VMEM(FLAT, F32)] * 4 + [pltpu.SemaphoreType.DMA((4,))],
    )
    return tuple(x.reshape(K, J, W) for x in outs)


def solution(mesh):
    field, flat = P(None, "lat", "lon"), P("lat", "lon")
    return jax.shard_map(
        body,
        mesh=mesh,
        in_specs=(field, field, field, field, flat, flat, P()),
        out_specs=(field,) * 4,
        check_vma=False,
    )
```

```python
import jax
import jax.numpy as jnp
from jax import lax
from jax.experimental import pallas as pl
from jax.experimental.pallas import tpu as pltpu
from jax.sharding import PartitionSpec as P

K, J, W = 16, 16, 128
WIN = 6
SEND_ROWS = 23
F32 = jnp.float32


def lanes():
    return lax.broadcasted_iota(jnp.int32, (K, W), 1)


def levels():
    return lax.broadcasted_iota(jnp.int32, (K, W), 0).astype(F32)


def low_half(lane):
    return lane - WIN * ((lane * 43) >> 8) < WIN // 2


def roll(x, shift):
    shift %= W
    return x if shift == 0 else pltpu.roll(x, shift, 1)


def load_row(ref, j):
    return ref[pl.ds(j, K, stride=J), :]


def store_row(ref, j, value):
    ref[pl.ds(j, K, stride=J), :] = value


def depth_row(depth_ref, j):
    return jnp.broadcast_to(depth_ref[pl.ds(j, 1), :], (K, W))


def wet_of(depth):
    return jnp.where(levels() < depth, 1.0, 0.0).astype(F32)


def unpack(packed, j):
    return roll(packed, -(WIN * j + 3))


def east(x, halo, lane):
    return roll(jnp.where(lane < 1, halo, x), -1)


def west(x, halo, lane):
    return roll(jnp.where(lane == W - 1, halo, x), 1)


def minmod(a, b):
    return jnp.maximum(jnp.minimum(a, jnp.maximum(b, 0.0)), jnp.minimum(b, 0.0))


def rise_fall(before, here, after):
    rise = minmod(0.5 * here + (1.0 / 12.0) * (before - after), here)
    return rise, here - rise


def limited(fall, rise):
    return minmod(fall, rise + rise), minmod(rise, fall + fall)


def weights(c):
    size = jnp.abs(c)
    rest = 1.0 - size
    return size * rest, rest * rest


def pack_columns(rows):
    lane = lanes()
    packed = jnp.zeros((K, W), F32)
    for j, row in enumerate(rows):
        mine = (lane >= WIN * j) & (lane < WIN * j + WIN)
        packed = jnp.where(mine, roll(row, WIN * j + 3), packed)
    return packed


def pack_kernel(*refs):
    sources, (t_ref, s_ref, u_ref, v_ref, d_ref, own_ref, ev_ref, od_ref) = refs[:6], refs[6:14]
    ind_ref, lay_ref, sems = refs[14:]
    copies = [
        pltpu.make_async_copy(src, dst, sems.at[n])
        for n, (src, dst) in enumerate(zip(sources, (t_ref, s_ref, u_ref, v_ref, ind_ref, lay_ref)))
    ]
    for n in (4, 5, 0, 1, 2, 3):
        copies[n].start()
    copies[4].wait()
    copies[5].wait()
    d_ref[...] = (ind_ref[...] * lay_ref[...]).astype(F32)
    d = pack_columns([depth_row(d_ref, j) for j in range(J)])
    fields = []
    for n, ref in enumerate((t_ref, s_ref, u_ref, v_ref)):
        copies[n].wait()
        fields.append(pack_columns([load_row(ref, j) for j in range(J)]))
    fields.insert(3, d)
    for n, x in enumerate(fields):
        own_ref[:, n * W : (n + 1) * W] = x
    t, s, u, d, v = fields
    low = low_half(lanes())
    even = (lax.axis_index("lon") & 1) == 0
    for n, (a, b) in enumerate(((t, s), (u, d), (v, v))):
        to_east = jnp.where(low, a, roll(b, 3))
        to_west = jnp.where(low, roll(b, -3), a)
        at = slice(n * W, (n + 1) * W)
        ev_ref[:, at] = jnp.where(even, to_east, to_west)
        od_ref[:, at] = jnp.where(even, to_west, to_east)


def seams(own_ref, ev_ref, od_ref):
    low = low_half(lanes())
    even = (lax.axis_index("lon") & 1) == 0
    mate = pl.multiple_of(jnp.where(even, K, 0), K)
    out = []
    for n in range(5):
        at = slice((n // 2) * W, (n // 2 + 1) * W)
        ev = ev_ref[pl.ds(mate, K), at]
        od = od_ref[:, at]
        from_west = jnp.where(even, od, ev)
        from_east = jnp.where(even, ev, od)
        if n in (1, 3):
            from_west, from_east = roll(from_west, -3), roll(from_east, 3)
        own = own_ref[:, n * W : (n + 1) * W]
        out.append(
            (
                jnp.where(low, from_west, from_east),
                jnp.where(low, from_west, own),
                jnp.where(low, own, from_east),
            )
        )
    return out


def seam_flux(q, c, wet):
    step = roll(q, -1) - q
    rise, fall = rise_fall(roll(step, 1), step, roll(step, -1))
    down, up = limited(roll(fall, 1), rise)
    near, far = weights(c)
    out_right = q + (near * down + far * up)
    near, far = weights(roll(c, 1))
    out_left = q - (near * up + far * down)
    return fall, c * wet * roll(wet, -1) * jnp.where(c > 0.0, out_right, roll(out_left, -1))


class Zonal:
    def __init__(self, packs, u_ref, d_ref):
        self.packs, self.u_ref, self.d_ref = packs, u_ref, d_ref
        lane = lanes()
        third = lane - WIN * ((lane * 43) >> 8) == 2
        _, uw, ue = packs[2]
        _, dw, de = packs[3]
        ww, we = wet_of(dw), wet_of(de)
        self.fix = []
        for n in range(2):
            fall_w, flux_w = seam_flux(packs[n][1], uw, ww)
            _, flux_e = seam_flux(packs[n][2], ue, we)
            self.fix.append((jnp.where(third, flux_e, roll(fall_w, 1)), flux_w))

    def row(self, refs, j):
        lane = lanes()
        last = lane == W - 1
        u = load_row(self.u_ref, j)
        wet = wet_of(depth_row(self.d_ref, j))
        halo_wet = wet_of(unpack(self.packs[3][0], j))
        near, far = weights(u)
        near_w, far_w = weights(west(u, unpack(self.packs[2][0], j), lane))
        face = u * wet * east(wet, halo_wet, lane)
        forward = u > 0.0
        out = []
        for n, ref in enumerate(refs):
            q = load_row(ref, j)
            halo = unpack(self.packs[n][0], j)
            fix, flux_in = (unpack(x, j) for x in self.fix[n])
            right = east(q, halo, lane)
            rise, fall = rise_fall(
                q - west(q, halo, lane),
                right - q,
                roll(jnp.where(lane < 2, halo, q), -2) - right,
            )
            down, up = limited(jnp.where(lane == 0, fix, roll(fall, 1)), rise)
            flux = face * jnp.where(
                forward, q + (near * down + far * up), roll(q - (near_w * up + far_w * down), -1)
            )
            flux_west = roll(jnp.where(last, flux_in, flux), 1)
            out.append(q - (jnp.where(last, fix, flux) - flux_west))
        return out


def zonal_masks(wet, halo_wet, lane):
    return wet * east(wet, halo_wet, lane), wet * west(wet, halo_wet, lane)


def zonal_lap(f, halo, masks, lane):
    return masks[0] * (east(f, halo, lane) - f) - masks[1] * (f - west(f, halo, lane))


def seam_lap(f, wet):
    total = None
    for shift in (1, -1, WIN, -WIN):
        term = wet * roll(wet, shift) * (roll(f, shift) - f)
        total = term if total is None else total + term
    return total


def edge_kernel(
    t_ref, s_ref, u_ref, v_ref, d_ref, own_ref, ev_ref, od_ref, swept_ref, e_ref, o_ref
):
    lane = lanes()
    packs = seams(own_ref, ev_ref, od_ref)
    zonal = Zonal(packs, u_ref, d_ref)
    halves = []
    for rows in ((J - 1, J - 2, J - 3), (0, 1, 2)):
        planes = [zonal.row((t_ref, s_ref), j) for j in rows]
        for j, (t, s) in zip(rows, planes):
            swept_ref[j if j < 3 else j - 10] = t
            swept_ref[6 + (j if j < 3 else j - 10)] = s
        half = [p[0] for p in planes] + [p[1] for p in planes]
        j, inward = rows[0], rows[1]
        depth = depth_row(d_ref, j)
        halo_depth = unpack(packs[3][0], j)
        wet, halo_wet = wet_of(depth), wet_of(halo_depth)
        masks = zonal_masks(wet, halo_wet, lane)
        to_inner = wet * wet_of(depth_row(d_ref, inward))
        corner = roll(halo_depth, 2)
        corner = jnp.where(lane < W // 2, corner, roll(halo_depth, -2))
        for ref, pack, reach in ((v_ref, packs[4], 1), (u_ref, packs[2], 0)):
            halo = unpack(pack[0], j)
            f = load_row(ref, j)
            partial = zonal_lap(f, halo, masks, lane) + to_inner * (load_row(ref, inward) - f)
            half[6:6] = [f, partial]
            take = jnp.where(lane < W // 2, roll(halo, reach), roll(halo, -reach))
            corner = jnp.where((lane == reach) | (lane == W - 1 - reach), take, corner)
        halves.append((half + [corner], depth[:8]))
    lat = lax.axis_index("lat")
    even = (lat & 1) == 0
    top = lat == lax.axis_size("lat") - 1
    (north, north_d), (south, south_d) = halves
    for n, (a, b) in enumerate(zip(north, south)):
        e_ref[2 * n : 2 * n + 2] = jnp.where(even, a, b).reshape(2, 8, W)
        o_ref[2 * n : 2 * n + 2] = jnp.where(even, b, a).reshape(2, 8, W)
    e_ref[SEND_ROWS - 1] = jnp.where(even, north_d, south_d)
    o_ref[SEND_ROWS - 1] = jnp.where(even, south_d, north_d)

    @pl.when(top)
    def _():
        mirror = W - 1 - lax.broadcasted_iota(jnp.int32, (8, W), 1)
        lane8 = lax.broadcasted_iota(jnp.int32, (8, W), 1)
        for n in range(SEND_ROWS):
            x = jnp.take_along_axis(o_ref[n], mirror, axis=1)
            if 12 <= n < 20:
                x = -x
            elif 20 <= n < 22:
                x = jnp.where((lane8 < 2) | (lane8 > W - 3), -x, x)
            o_ref[n] = x


def merid_cell(step, fall_before, j):
    rise, fall = rise_fall(step[j - 1], step[j], step[j + 1])
    down, up = limited(fall_before, rise)
    return down, up, fall


def merid_flux(c, wet_pair, q, q_next, cell, cell_next):
    forward = c > 0.0
    rest = 1.0 - jnp.abs(c)
    square = rest * rest
    near = jnp.where(forward, cell[0], cell_next[1])
    far = jnp.where(forward, cell[1], cell_next[0])
    return c * wet_pair * (
        jnp.where(forward, q, q_next) + (c * rest * near + jnp.where(forward, square, -square) * far)
    )


AUX_TRACER, AUX_FLOW = 12, 10


def inner_kernel(
    t_ref,
    s_ref,
    u_ref,
    v_ref,
    d_ref,
    visc_hbm,
    own_ref,
    ev_ref,
    od_ref,
    swept_ref,
    t_out,
    s_out,
    u_out,
    v_out,
    aux_ref,
    visc_ref,
    sem,
):
    copy = pltpu.make_async_copy(visc_hbm, visc_ref, sem)
    copy.start()
    lane = lanes()
    packs = seams(own_ref, ev_ref, od_ref)
    zonal = Zonal(packs, u_ref, d_ref)
    rows = [{}, {}]
    for j in (0, 1, 2, 13, 14, 15):
        for n in range(2):
            rows[n][j] = swept_ref[6 * n + (j if j < 3 else j - 10)]
    for j in range(3, 13):
        rows[0][j], rows[1][j] = zonal.row((t_ref, s_ref), j)
    wet = [wet_of(depth_row(d_ref, j)) for j in range(J)]
    for n, out in enumerate((t_out, s_out)):
        q = rows[n]
        for at, j in enumerate((0, 1, 2, 3, 4, 11, 12, 13, 14, 15)):
            aux_ref[AUX_TRACER * n + at] = q[j]
        step = [q[j + 1] - q[j] for j in range(J - 1)]
        cell = merid_cell(step, rise_fall(step[0], step[1], step[2])[1], 2)
        before = None
        for j in range(2, 13):
            after = merid_cell(step, cell[2], j + 1)
            flux = merid_flux(load_row(v_ref, j), wet[j] * wet[j + 1], q[j], q[j + 1], cell, after)
            if j == 2:
                aux_ref[AUX_TRACER * n + 10] = flux
            else:
                store_row(out, j, q[j] - (flux - before))
            if j == 12:
                aux_ref[AUX_TRACER * n + 11] = flux
            cell, before = after, flux
    wet_w, wet_e = wet_of(packs[3][1]), wet_of(packs[3][2])
    low = low_half(lane)
    copy.wait()
    visc = viscosity(visc_ref)
    halo_wet = [wet_of(unpack(packs[3][0], j)) for j in range(J)]
    masks = [zonal_masks(wet[j], halo_wet[j], lane) for j in range(J)]
    pair = [wet[j] * wet[j + 1] for j in range(J - 1)]
    for n, (ref, pack, out) in enumerate(((u_ref, packs[2], u_out), (v_ref, packs[4], v_out))):
        base = 2 * AUX_TRACER + AUX_FLOW * n
        halo_lap = jnp.where(low, seam_lap(pack[1], wet_w), seam_lap(pack[2], wet_e))
        f = [load_row(ref, j) for j in range(J)]
        lap = []
        step = None
        for j in range(J):
            total = zonal_lap(f[j], unpack(pack[0], j), masks[j], lane)
            if step is not None:
                total = total - step
            if j < J - 1:
                step = pair[j] * (f[j + 1] - f[j])
                total = total + step
            lap.append(total)
        step = None
        for j in range(1, J - 1):
            total = zonal_lap(lap[j], unpack(halo_lap, j), masks[j], lane)
            if step is not None:
                total = total - step
            if j < J - 2:
                step = pair[j] * (lap[j + 1] - lap[j])
                total = total + step
            if j == 1:
                aux_ref[base + 2] = total
            elif j == J - 2:
                aux_ref[base + 5] = total
            else:
                store_row(out, j, f[j] - visc * total)
        aux_ref[base + 0] = lap[0]
        aux_ref[base + 1] = lap[1]
        aux_ref[base + 3] = lap[J - 1]
        aux_ref[base + 4] = lap[J - 2]
        aux_ref[base + 6] = unpack(halo_lap, 0)
        aux_ref[base + 7] = unpack(halo_lap, J - 1)
        aux_ref[base + 8] = unpack(pack[0], 0)
        aux_ref[base + 9] = unpack(pack[0], J - 1)
    aux_ref[2 * AUX_TRACER + 2 * AUX_FLOW] = halo_wet[0]
    aux_ref[2 * AUX_TRACER + 2 * AUX_FLOW + 1] = halo_wet[J - 1]
    aux_ref[2 * AUX_TRACER + 2 * AUX_FLOW + 2] = visc


def viscosity(visc_ref):
    level = lax.broadcasted_iota(jnp.int32, (K, W), 0)
    visc = jnp.zeros((K, W), F32)
    for k in range(K):
        visc = jnp.where(level == k, visc_ref[k], visc)
    return visc


def finish_kernel(
    u_ref, v_ref, d_ref, t_in, s_in, u_in, v_in, aux_ref, e_ref, o_ref, *outs
):
    finals, (t_out, s_out, u_out, v_out), sems = outs[:4], outs[4:8], outs[8]
    lane = lanes()
    copies = [
        pltpu.make_async_copy(src, dst, sems.at[n])
        for n, (src, dst) in enumerate(zip((t_out, s_out, u_out, v_out), finals))
    ]
    even = (lax.axis_index("lat") & 1) == 0
    halo_at = 2 * AUX_TRACER + 2 * AUX_FLOW
    visc = aux_ref[halo_at + 2]

    def recv(side, n):
        e, o = e_ref[2 * n : 2 * n + 2].reshape(K, W), o_ref[2 * n : 2 * n + 2].reshape(K, W)
        return jnp.where(even, e, o) if side == 0 else jnp.where(even, o, e)

    def recv_depth(side):
        e, o = e_ref[SEND_ROWS - 1], o_ref[SEND_ROWS - 1]
        x = jnp.where(even, e, o) if side == 0 else jnp.where(even, o, e)
        return jnp.concatenate([x, x], axis=0)

    wet = {j: wet_of(depth_row(d_ref, j)) for j in (0, 1, 2, 13, 14, 15)}
    wet[16], wet[-1] = wet_of(recv_depth(0)), wet_of(recv_depth(1))
    courant = {j: load_row(v_ref, j) for j in (0, 1, 13, 14, 15)}
    courant[-1] = recv(1, 8)
    for n, (src, out) in enumerate(((t_in, t_out), (s_in, s_out))):
        aux = AUX_TRACER * n
        for j in range(3, 13):
            store_row(out, j, load_row(src, j))
        for side in (0, 1):
            if side == 0:
                q = {11 + m: aux_ref[aux + 5 + m] for m in range(5)}
                q.update({16 + m: recv(side, 3 * n + m) for m in range(3)})
                before, faces = aux_ref[aux + 11], (13, 14, 15)
            else:
                q = {j: aux_ref[aux + j] for j in range(5)}
                q.update({-1 - m: recv(side, 3 * n + m) for m in range(3)})
                before, faces = None, (-1, 0, 1)
            step = {j: q[j + 1] - q[j] for j in q if j + 1 in q}
            first = faces[0]
            fall = rise_fall(step[first - 2], step[first - 1], step[first])[1]
            cell = merid_cell(step, fall, first)
            for j in faces:
                after = merid_cell(step, cell[2], j + 1)
                flux = merid_flux(courant[j], wet[j] * wet[j + 1], q[j], q[j + 1], cell, after)
                if before is not None:
                    store_row(out, j, q[j] - (flux - before))
                cell, before = after, flux
            if side == 1:
                store_row(out, 2, q[2] - (aux_ref[aux + 10] - before))
        copies[n].start()
    for n, (ref, src, out) in enumerate(((u_ref, u_in, u_out), (v_ref, v_in, v_out))):
        base = 2 * AUX_TRACER + AUX_FLOW * n
        for j in range(2, 14):
            store_row(out, j, load_row(src, j))
        for side in (0, 1):
            edge, inward, beyond = (15, 14, 16) if side == 0 else (0, 1, -1)
            halo_wet = aux_ref[halo_at + 1 - side]
            corner = recv(side, 10)
            corner_depth = jnp.where(lane < W // 2, roll(corner, -2), roll(corner, 2))
            corner_wet = halo_wet * wet_of(corner_depth)
            masks = zonal_masks(wet[edge], halo_wet, lane)
            at = (3, 4, 5, 7, 9) if side == 0 else (0, 1, 2, 6, 8)
            lap_edge, lap_in, partial, halo_lap, halo_f = (aux_ref[base + a] for a in at)
            f, f_in = load_row(ref, edge), load_row(ref, inward)
            f_out, lap_out = recv(side, 6 + 2 * n), recv(side, 7 + 2 * n)
            across = wet[edge] * wet[beyond]
            step = across * (f_out - f)
            lap_edge = lap_edge + step
            lap_out = lap_out - step
            if n == 0:
                corner_f = corner
            else:
                corner_f = jnp.where(lane < W // 2, roll(corner, -1), roll(corner, 1))
            halo_lap = halo_lap + corner_wet * (corner_f - halo_f)
            inner_step = wet[edge] * wet[inward] * (lap_in - lap_edge)
            total = (
                zonal_lap(lap_edge, halo_lap, masks, lane)
                + inner_step
                + across * (lap_out - lap_edge)
            )
            store_row(out, edge, f - visc * total)
            store_row(out, inward, f_in - visc * (partial - inner_step))
        copies[2 + n].start()
    for copy in copies:
        copy.wait()


VMEM = pl.BlockSpec(memory_space=pltpu.VMEM)
HBM = pl.BlockSpec(memory_space=pltpu.HBM)
FLAT = (K * J, W)
AUX = 2 * AUX_TRACER + 2 * AUX_FLOW + 3


def call(kernel, in_specs, out_specs, out_shapes, flops, args, scratch=()):
    return pl.pallas_call(
        kernel,
        out_shape=[jax.ShapeDtypeStruct(s, F32) for s in out_shapes],
        in_specs=in_specs,
        out_specs=out_specs,
        scratch_shapes=list(scratch),
        cost_estimate=pl.CostEstimate(flops=flops, bytes_accessed=1 << 20, transcendentals=0),
        compiler_params=pltpu.CompilerParams(vmem_limit_bytes=32 << 20),
    )(*args)


def body(t, s, u, v, ind, lay, visc):
    t, s, u, v = (x.reshape(FLAT) for x in (t, s, u, v))
    n_lon, n_lat = lax.axis_size("lon"), lax.axis_size("lat")
    t, s, u, v, depth, own, ev, od = call(
        pack_kernel,
        [HBM] * 6,
        [VMEM] * 8,
        [FLAT] * 4 + [(J, W), (K, 5 * W), (K, 3 * W), (K, 3 * W)],
        1 << 20,
        [pltpu.with_memory_space_constraint(x, pltpu.HBM) for x in (t, s, u, v, ind, lay)],
        [pltpu.VMEM((J, W), jnp.int32)] * 2 + [pltpu.SemaphoreType.DMA((6,))],
    )
    od = lax.ppermute(od, "lon", [(i, (((i + 1) ^ 1) - 1) % n_lon) for i in range(n_lon)])
    ev = lax.all_gather(
        ev, "lon", axis_index_groups=[[i, i + 1] for i in range(0, n_lon, 2)], tiled=True
    )
    swept, edge_e, edge_o = call(
        edge_kernel,
        [VMEM] * 8,
        [VMEM] * 3,
        [(12, K, W), (SEND_ROWS, 8, W), (SEND_ROWS, 8, W)],
        1 << 20,
        (t, s, u, v, depth, own, ev, od),
    )
    pairs_e, pairs_o = [], []
    top = n_lat - 1
    for p in range(n_lon):
        for l in range(n_lat):
            pairs_e.append((p * n_lat + l, p * n_lat + (l ^ 1)))
            if 0 < l < top:
                pairs_o.append((p * n_lat + l, p * n_lat + ((l + 1) ^ 1) - 1))
        pairs_o.append((p * n_lat + top, (n_lon - 1 - p) * n_lat + top))
    got_e = lax.ppermute(edge_e, ("lon", "lat"), pairs_e)
    got_o = lax.ppermute(edge_o, ("lon", "lat"), pairs_o)
    *parts, aux = call(
        inner_kernel,
        [VMEM] * 5 + [HBM] + [VMEM] * 4,
        [VMEM] * 5,
        [FLAT] * 4 + [(AUX, K, W)],
        1 << 24,
        (t, s, u, v, depth, pltpu.with_memory_space_constraint(visc, pltpu.HBM), own, ev, od, swept),
        [pltpu.SMEM((K,), F32), pltpu.SemaphoreType.DMA],
    )
    outs = call(
        finish_kernel,
        [VMEM] * 10,
        [HBM] * 4,
        [FLAT] * 4,
        1 << 22,
        (u, v, depth, *parts, aux, got_e, got_o),
        [pltpu.VMEM(FLAT, F32)] * 4 + [pltpu.SemaphoreType.DMA((4,))],
    )
    return tuple(x.reshape(K, J, W) for x in outs)


def solution(mesh):
    field, flat = P(None, "lat", "lon"), P("lat", "lon")
    return jax.shard_map(
        body,
        mesh=mesh,
        in_specs=(field, field, field, field, flat, flat, P()),
        out_specs=(field,) * 4,
        check_vma=False,
    )
```

```python
import jax
import jax.numpy as jnp
from jax import lax
from jax.experimental import pallas as pl
from jax.experimental.pallas import tpu as pltpu
from jax.sharding import PartitionSpec as P

K, J, W = 16, 16, 128
WIN = 6
PHASE = (0, 3, 0, 3, 0)
SEND_ROWS = 21
F32 = jnp.float32


def lanes():
    return lax.broadcasted_iota(jnp.int32, (K, W), 1)


def levels():
    return lax.broadcasted_iota(jnp.int32, (K, W), 0).astype(F32)


def low_half(lane):
    return lane - WIN * ((lane * 43) >> 8) < WIN // 2


def roll(x, shift):
    shift %= W
    return x if shift == 0 else pltpu.roll(x, shift, 1)


def load_row(ref, j):
    return ref[pl.ds(j, K, stride=J), :]


def store_row(ref, j, value):
    ref[pl.ds(j, K, stride=J), :] = value


def depth_row(depth_ref, j):
    return jnp.broadcast_to(depth_ref[pl.ds(j, 1), :], (K, W))


def wet_of(depth):
    return jnp.where(levels() < depth, 1.0, 0.0).astype(F32)


def unpack(packed, j):
    return roll(packed, -(WIN * j + 3))


def east(x, halo, lane):
    return roll(jnp.where(lane < 1, halo, x), -1)


def west(x, halo, lane):
    return roll(jnp.where(lane == W - 1, halo, x), 1)


def minmod(a, b):
    return jnp.maximum(jnp.minimum(a, jnp.maximum(b, 0.0)), jnp.minimum(b, 0.0))


def rise_fall(before, here, after):
    rise = minmod(0.5 * here + (1.0 / 12.0) * (before - after), here)
    return rise, here - rise


def limited(fall, rise):
    return minmod(fall, rise + rise), minmod(rise, fall + fall)


def weights(c):
    size = jnp.abs(c)
    rest = 1.0 - size
    return size * rest, rest * rest


def pack_columns(rows, phase):
    lane = lanes()
    packed = jnp.zeros((K, W), F32)
    for j, row in enumerate(rows):
        first = WIN * j + phase
        packed = jnp.where((lane >= first) & (lane < first + WIN), roll(row, first + 3), packed)
    return packed


def pack_kernel(*refs):
    sources, (t_ref, s_ref, u_ref, v_ref, d_ref, own_ref, ev_ref, od_ref) = refs[:6], refs[6:14]
    ind_ref, lay_ref, sems = refs[14:]
    copies = [
        pltpu.make_async_copy(src, dst, sems.at[n])
        for n, (src, dst) in enumerate(zip(sources, (t_ref, s_ref, u_ref, v_ref, ind_ref, lay_ref)))
    ]
    for n in (4, 5, 0, 1, 2, 3):
        copies[n].start()
    copies[4].wait()
    copies[5].wait()
    d_ref[...] = (ind_ref[...] * lay_ref[...]).astype(F32)
    d = pack_columns([depth_row(d_ref, j) for j in range(J)], 3)
    fields = []
    for n, ref in enumerate((t_ref, s_ref, u_ref, v_ref)):
        copies[n].wait()
        fields.append(pack_columns([load_row(ref, j) for j in range(J)], 3 if n == 1 else 0))
    fields.insert(3, d)
    for n, x in enumerate(fields):
        own_ref[:, n * W : (n + 1) * W] = x
    t, s, u, d, v = fields
    low = low_half(lanes())
    even = (lax.axis_index("lon") & 1) == 0
    for n, (a, b) in enumerate(((t, s), (u, d), (v, v))):
        to_east = jnp.where(low, a, b)
        to_west = jnp.where(low, b, a)
        at = slice(n * W, (n + 1) * W)
        ev_ref[:, at] = jnp.where(even, to_east, to_west)
        od_ref[:, at] = jnp.where(even, to_west, to_east)


def arrived(ev_ref, od_ref, n):
    even = (lax.axis_index("lon") & 1) == 0
    mate = pl.multiple_of(jnp.where(even, K, 0), K)
    at = slice((n // 2) * W, (n // 2 + 1) * W)
    ev = ev_ref[pl.ds(mate, K), at]
    od = od_ref[:, at]
    return jnp.where(even, od, ev), jnp.where(even, ev, od)


def seams(own_ref, ev_ref, od_ref):
    low = low_half(lanes())
    out = []
    for n in range(5):
        from_west, from_east = arrived(ev_ref, od_ref, n)
        own = own_ref[:, n * W : (n + 1) * W]
        if PHASE[n]:
            from_west, from_east, own = (roll(x, -3) for x in (from_west, from_east, own))
        out.append(
            (
                jnp.where(low, from_west, from_east),
                jnp.where(low, from_west, own),
                jnp.where(low, own, from_east),
            )
        )
    return out


def seam_flux(q, c, wet):
    step = roll(q, -1) - q
    rise, fall = rise_fall(roll(step, 1), step, roll(step, -1))
    down, up = limited(roll(fall, 1), rise)
    near, far = weights(c)
    out_right = q + (near * down + far * up)
    near, far = weights(roll(c, 1))
    out_left = q - (near * up + far * down)
    return fall, c * wet * roll(wet, -1) * jnp.where(c > 0.0, out_right, roll(out_left, -1))


def in_step(walks):
    out = [None] * len(walks)
    live = list(range(len(walks)))
    while live:
        for n in tuple(live):
            try:
                next(walks[n])
            except StopIteration as end:
                out[n] = end.value
                live.remove(n)
    return out


class Zonal:
    def __init__(self, packs, u_ref, d_ref):
        self.packs, self.u_ref, self.d_ref = packs, u_ref, d_ref
        lane = lanes()
        third = lane - WIN * ((lane * 43) >> 8) == 2
        _, uw, ue = packs[2]
        _, dw, de = packs[3]
        ww, we = wet_of(dw), wet_of(de)
        self.fix = []
        for n in range(2):
            fall_w, flux_w = seam_flux(packs[n][1], uw, ww)
            _, flux_e = seam_flux(packs[n][2], ue, we)
            self.fix.append((jnp.where(third, flux_e, roll(fall_w, 1)), flux_w))

    def row(self, refs, j):
        lane = lanes()
        last = lane == W - 1
        u = load_row(self.u_ref, j)
        wet = wet_of(depth_row(self.d_ref, j))
        halo_wet = unpack(self.packs[3][0], j)
        halo_u = unpack(self.packs[2][0], j)
        halos = [unpack(self.packs[n][0], j) for n in range(2)]
        fixes = [[unpack(x, j) for x in self.fix[n]] for n in range(2)]
        q = [load_row(ref, j) for ref in refs]
        yield
        halo_wet = wet_of(halo_wet)
        right = [east(q[n], halos[n], lane) for n in range(2)]
        left = [west(q[n], halos[n], lane) for n in range(2)]
        beyond = [roll(jnp.where(lane < 2, halos[n], q[n]), -2) for n in range(2)]
        u_west = west(u, halo_u, lane)
        wet_east = east(wet, halo_wet, lane)
        yield
        edges = [rise_fall(q[n] - left[n], right[n] - q[n], beyond[n] - right[n]) for n in range(2)]
        falls = [roll(edges[n][1], 1) for n in range(2)]
        yield
        near, far = weights(u)
        near_w, far_w = weights(u_west)
        face = u * wet * wet_east
        forward = u > 0.0
        cells = [
            limited(jnp.where(lane == 0, fixes[n][0], falls[n]), edges[n][0]) for n in range(2)
        ]
        from_right = [roll(q[n] - (near_w * cells[n][1] + far_w * cells[n][0]), -1) for n in range(2)]
        yield
        flux = [
            face * jnp.where(forward, q[n] + (near * cells[n][0] + far * cells[n][1]), from_right[n])
            for n in range(2)
        ]
        before = [roll(jnp.where(last, fixes[n][1], flux[n]), 1) for n in range(2)]
        yield
        return [q[n] - (jnp.where(last, fixes[n][0], flux[n]) - before[n]) for n in range(2)]


def zonal_masks(wet, halo_wet, lane):
    return wet * east(wet, halo_wet, lane), wet * west(wet, halo_wet, lane)


def zonal_lap(f, halo, masks, lane):
    return masks[0] * (east(f, halo, lane) - f) - masks[1] * (f - west(f, halo, lane))


def seam_lap(f, wet):
    total = None
    for shift in (1, -1, WIN, -WIN):
        term = wet * roll(wet, shift) * (roll(f, shift) - f)
        total = term if total is None else total + term
    return total


def edge_kernel(
    t_ref, s_ref, u_ref, v_ref, d_ref, own_ref, ev_ref, od_ref, swept_ref, e_ref, o_ref
):
    lane = lanes()
    lane8, sub8 = lane[:8], lax.broadcasted_iota(jnp.int32, (8, W), 0)
    packs = seams(own_ref, ev_ref, od_ref)
    zonal = Zonal(packs, u_ref, d_ref)
    packs = [p[0] for p in packs]
    wet = {j: wet_of(depth_row(d_ref, j)) for j in (0, 1, 2, 13, 14, 15)}
    halo_wet = {j: wet_of(unpack(packs[3], j)) for j in (0, 15)}
    halves = []
    all_rows = (15, 14, 13, 0, 1, 2)
    swept = []
    for at in range(0, 6, 6):
        swept += in_step([zonal.row((t_ref, s_ref), j) for j in all_rows[at : at + 6]])
    planes_of = (swept[:3], swept[3:])
    for side, rows in enumerate(((J - 1, J - 2, J - 3), (0, 1, 2))):
        planes = planes_of[side]
        for j, (t, s) in zip(rows, planes):
            swept_ref[j if j < 3 else j - 10] = t
            swept_ref[6 + (j if j < 3 else j - 10)] = s
        half = [p[0] for p in planes] + [p[1] for p in planes]
        j, inward = rows[0], rows[1]
        masks = zonal_masks(wet[j], halo_wet[j], lane)
        to_inner = wet[j] * wet[inward]
        for ref, pack in ((u_ref, packs[2]), (v_ref, packs[4])):
            f = load_row(ref, j)
            partial = zonal_lap(f, unpack(pack, j), masks, lane) + to_inner * (load_row(ref, inward) - f)
            half += [f, partial]
        depth = depth_row(d_ref, j)[:8]
        corner = jnp.where(sub8 < 4, depth, roll(depth, W // 2))
        for at, (pack, top) in enumerate(
            ((packs[2], 0), (packs[4], 0), (packs[2], 8), (packs[4], 8), (packs[3], 0))
        ):
            home = -(WIN * j + 3)
            part = pack[top : top + 8]
            corner = jnp.where(lane8 == at, roll(part, home + at), corner)
            corner = jnp.where(lane8 == W - 1 - at, roll(part, home - at), corner)
        halves.append((half, corner))
    lat = lax.axis_index("lat")
    even = (lat & 1) == 0
    (north, north_c), (south, south_c) = halves
    for n, (a, b) in enumerate(zip(north, south)):
        e_ref[2 * n : 2 * n + 2] = jnp.where(even, a, b).reshape(2, 8, W)
        o_ref[2 * n : 2 * n + 2] = jnp.where(even, b, a).reshape(2, 8, W)
    e_ref[SEND_ROWS - 1] = jnp.where(even, north_c, south_c)
    o_ref[SEND_ROWS - 1] = jnp.where(even, south_c, north_c)

    @pl.when(lat == lax.axis_size("lat") - 1)
    def _():
        for n in range(SEND_ROWS):
            x = jnp.take_along_axis(o_ref[n], W - 1 - lane8, axis=1)
            if 12 <= n < 20:
                x = -x
            elif n == 20:
                x = jnp.where((lane8 < 4) | (lane8 > W - 5), -x, x)
            o_ref[n] = x


def merid_cell(step, fall_before, j):
    rise, fall = rise_fall(step[j - 1], step[j], step[j + 1])
    down, up = limited(fall_before, rise)
    return down, up, fall


def merid_flux(c, wet_pair, q, q_next, cell, cell_next):
    forward = c > 0.0
    rest = 1.0 - jnp.abs(c)
    square = rest * rest
    near = jnp.where(forward, cell[0], cell_next[1])
    far = jnp.where(forward, cell[1], cell_next[0])
    return c * wet_pair * (
        jnp.where(forward, q, q_next) + (c * rest * near + jnp.where(forward, square, -square) * far)
    )


AUX_TRACER, AUX_FLOW = 12, 10


def inner_kernel(
    t_ref,
    s_ref,
    u_ref,
    v_ref,
    d_ref,
    visc_hbm,
    own_ref,
    ev_ref,
    od_ref,
    swept_ref,
    t_out,
    s_out,
    u_out,
    v_out,
    aux_ref,
    visc_ref,
    sem,
):
    copy = pltpu.make_async_copy(visc_hbm, visc_ref, sem)
    copy.start()
    lane = lanes()
    packs = seams(own_ref, ev_ref, od_ref)
    zonal = Zonal(packs, u_ref, d_ref)
    rows = [{}, {}]
    for j in (0, 1, 2, 13, 14, 15):
        for n in range(2):
            rows[n][j] = swept_ref[6 * n + (j if j < 3 else j - 10)]
    for at in range(3, 13, 3):
        group = range(at, min(at + 3, 13))
        for j, (t, s) in zip(group, in_step([zonal.row((t_ref, s_ref), j) for j in group])):
            rows[0][j], rows[1][j] = t, s
    wet = [wet_of(depth_row(d_ref, j)) for j in range(J)]
    for n, out in enumerate((t_out, s_out)):
        q = rows[n]
        for at, j in enumerate((0, 1, 2, 3, 4, 11, 12, 13, 14, 15)):
            aux_ref[AUX_TRACER * n + at] = q[j]
        step = [q[j + 1] - q[j] for j in range(J - 1)]
        cell = merid_cell(step, rise_fall(step[0], step[1], step[2])[1], 2)
        before = None
        for j in range(2, 13):
            after = merid_cell(step, cell[2], j + 1)
            flux = merid_flux(load_row(v_ref, j), wet[j] * wet[j + 1], q[j], q[j + 1], cell, after)
            if j == 2:
                aux_ref[AUX_TRACER * n + 10] = flux
            else:
                store_row(out, j, q[j] - (flux - before))
            if j == 12:
                aux_ref[AUX_TRACER * n + 11] = flux
            cell, before = after, flux
    wet_w, wet_e = wet_of(packs[3][1]), wet_of(packs[3][2])
    low = low_half(lane)
    copy.wait()
    visc = viscosity(visc_ref)
    halo_wet = [wet_of(unpack(packs[3][0], j)) for j in range(J)]
    masks = [zonal_masks(wet[j], halo_wet[j], lane) for j in range(J)]
    pair = [wet[j] * wet[j + 1] for j in range(J - 1)]
    for n, (ref, pack, out) in enumerate(((u_ref, packs[2], u_out), (v_ref, packs[4], v_out))):
        base = 2 * AUX_TRACER + AUX_FLOW * n
        halo_lap = jnp.where(low, seam_lap(pack[1], wet_w), seam_lap(pack[2], wet_e))
        f = [load_row(ref, j) for j in range(J)]
        lap = []
        step = None
        for j in range(J):
            total = zonal_lap(f[j], unpack(pack[0], j), masks[j], lane)
            if step is not None:
                total = total - step
            if j < J - 1:
                step = pair[j] * (f[j + 1] - f[j])
                total = total + step
            lap.append(total)
        step = None
        for j in range(1, J - 1):
            total = zonal_lap(lap[j], unpack(halo_lap, j), masks[j], lane)
            if step is not None:
                total = total - step
            if j < J - 2:
                step = pair[j] * (lap[j + 1] - lap[j])
                total = total + step
            if j == 1:
                aux_ref[base + 2] = total
            elif j == J - 2:
                aux_ref[base + 5] = total
            else:
                store_row(out, j, f[j] - visc * total)
        aux_ref[base + 0] = lap[0]
        aux_ref[base + 1] = lap[1]
        aux_ref[base + 3] = lap[J - 1]
        aux_ref[base + 4] = lap[J - 2]
        aux_ref[base + 6] = unpack(halo_lap, 0)
        aux_ref[base + 7] = unpack(halo_lap, J - 1)
        aux_ref[base + 8] = unpack(pack[0], 0)
        aux_ref[base + 9] = unpack(pack[0], J - 1)
    aux_ref[2 * AUX_TRACER + 2 * AUX_FLOW] = halo_wet[0]
    aux_ref[2 * AUX_TRACER + 2 * AUX_FLOW + 1] = halo_wet[J - 1]
    aux_ref[2 * AUX_TRACER + 2 * AUX_FLOW + 2] = visc


def viscosity(visc_ref):
    level = lax.broadcasted_iota(jnp.int32, (K, W), 0)
    visc = jnp.zeros((K, W), F32)
    for k in range(K):
        visc = jnp.where(level == k, visc_ref[k], visc)
    return visc


def finish_kernel(
    u_ref, v_ref, d_ref, _t, _s, _u, _v, aux_ref, e_ref, o_ref, *outs
):
    finals, (t_out, s_out, u_out, v_out), sems = outs[:4], outs[4:8], outs[8]
    lane = lanes()
    copies = [
        pltpu.make_async_copy(src, dst, sems.at[n])
        for n, (src, dst) in enumerate(zip((t_out, s_out, u_out, v_out), finals))
    ]
    even = (lax.axis_index("lat") & 1) == 0
    halo_at = 2 * AUX_TRACER + 2 * AUX_FLOW
    visc = aux_ref[halo_at + 2]

    def recv(side, n):
        e, o = e_ref[2 * n : 2 * n + 2].reshape(K, W), o_ref[2 * n : 2 * n + 2].reshape(K, W)
        return jnp.where(even, e, o) if side == 0 else jnp.where(even, o, e)

    wet = {j: wet_of(depth_row(d_ref, j)) for j in (0, 1, 2, 13, 14, 15)}
    corner_u, corner_v, corner_wet = [], [], []
    for side in (0, 1):
        e, o = e_ref[SEND_ROWS - 1], o_ref[SEND_ROWS - 1]
        tile = jnp.where(even, e, o) if side == 0 else jnp.where(even, o, e)
        lane8 = lane[:8]
        inside = (lane8 > 4) & (lane8 < W - 5)
        row = jnp.where(inside[:1], tile[:1], roll(tile, W // 2)[4:5])
        wet[16 if side == 0 else -1] = wet_of(jnp.broadcast_to(row, (K, W)))
        part = [tile] + [
            jnp.where(lane8 < W // 2, roll(tile, -m), roll(tile, m)) for m in range(1, 5)
        ]
        corner_u.append(jnp.concatenate([part[0], part[2]], axis=0))
        corner_v.append(jnp.concatenate([part[1], part[3]], axis=0))
        corner_wet.append(wet_of(jnp.concatenate([part[4], part[4]], axis=0)))
    courant = {j: load_row(v_ref, j) for j in (0, 1, 13, 14, 15)}
    courant[-1] = recv(1, 8)
    for n, out in enumerate((t_out, s_out)):
        aux = AUX_TRACER * n
        for side in (0, 1):
            if side == 0:
                q = {11 + m: aux_ref[aux + 5 + m] for m in range(5)}
                q.update({16 + m: recv(side, 3 * n + m) for m in range(3)})
                before, faces = aux_ref[aux + 11], (13, 14, 15)
            else:
                q = {j: aux_ref[aux + j] for j in range(5)}
                q.update({-1 - m: recv(side, 3 * n + m) for m in range(3)})
                before, faces = None, (-1, 0, 1)
            step = {j: q[j + 1] - q[j] for j in q if j + 1 in q}
            first = faces[0]
            fall = rise_fall(step[first - 2], step[first - 1], step[first])[1]
            cell = merid_cell(step, fall, first)
            for j in faces:
                after = merid_cell(step, cell[2], j + 1)
                flux = merid_flux(courant[j], wet[j] * wet[j + 1], q[j], q[j + 1], cell, after)
                if before is not None:
                    store_row(out, j, q[j] - (flux - before))
                cell, before = after, flux
            if side == 1:
                store_row(out, 2, q[2] - (aux_ref[aux + 10] - before))
        copies[n].start()
    for n, (ref, out) in enumerate(((u_ref, u_out), (v_ref, v_out))):
        base = 2 * AUX_TRACER + AUX_FLOW * n
        for side in (0, 1):
            edge, inward, beyond = (15, 14, 16) if side == 0 else (0, 1, -1)
            halo_wet = aux_ref[halo_at + 1 - side]
            masks = zonal_masks(wet[edge], halo_wet, lane)
            at = (3, 4, 5, 7, 9) if side == 0 else (0, 1, 2, 6, 8)
            lap_edge, lap_in, partial, halo_lap, halo_f = (aux_ref[base + a] for a in at)
            f, f_in = load_row(ref, edge), load_row(ref, inward)
            f_out, lap_out = recv(side, 6 + 2 * n), recv(side, 7 + 2 * n)
            across = wet[edge] * wet[beyond]
            step = across * (f_out - f)
            lap_edge = lap_edge + step
            lap_out = lap_out - step
            corner_f = (corner_u, corner_v)[n][side]
            halo_lap = halo_lap + halo_wet * corner_wet[side] * (corner_f - halo_f)
            inner_step = wet[edge] * wet[inward] * (lap_in - lap_edge)
            total = (
                zonal_lap(lap_edge, halo_lap, masks, lane)
                + inner_step
                + across * (lap_out - lap_edge)
            )
            store_row(out, edge, f - visc * total)
            store_row(out, inward, f_in - visc * (partial - inner_step))
        copies[2 + n].start()
    for copy in copies:
        copy.wait()


VMEM = pl.BlockSpec(memory_space=pltpu.VMEM)
HBM = pl.BlockSpec(memory_space=pltpu.HBM)
FLAT = (K * J, W)
AUX = 2 * AUX_TRACER + 2 * AUX_FLOW + 3


def call(kernel, in_specs, out_specs, out_shapes, flops, args, scratch=(), aliases=()):
    return pl.pallas_call(
        kernel,
        out_shape=[jax.ShapeDtypeStruct(s, F32) for s in out_shapes],
        in_specs=in_specs,
        out_specs=out_specs,
        scratch_shapes=list(scratch),
        input_output_aliases=dict(aliases),
        cost_estimate=pl.CostEstimate(flops=flops, bytes_accessed=1 << 20, transcendentals=0),
        compiler_params=pltpu.CompilerParams(vmem_limit_bytes=32 << 20),
    )(*args)


def body(t, s, u, v, ind, lay, visc):
    t, s, u, v = (x.reshape(FLAT) for x in (t, s, u, v))
    n_lon, n_lat = lax.axis_size("lon"), lax.axis_size("lat")
    t, s, u, v, depth, own, ev, od = call(
        pack_kernel,
        [HBM] * 6,
        [VMEM] * 8,
        [FLAT] * 4 + [(J, W), (K, 5 * W), (K, 3 * W), (K, 3 * W)],
        1 << 20,
        [pltpu.with_memory_space_constraint(x, pltpu.HBM) for x in (t, s, u, v, ind, lay)],
        [pltpu.VMEM((J, W), jnp.int32)] * 2 + [pltpu.SemaphoreType.DMA((6,))],
    )
    od = lax.ppermute(od, "lon", [(i, (((i + 1) ^ 1) - 1) % n_lon) for i in range(n_lon)])
    ev = lax.all_gather(
        ev, "lon", axis_index_groups=[[i, i + 1] for i in range(0, n_lon, 2)], tiled=True
    )
    swept, edge_e, edge_o = call(
        edge_kernel,
        [VMEM] * 8,
        [VMEM] * 3,
        [(12, K, W), (SEND_ROWS, 8, W), (SEND_ROWS, 8, W)],
        1 << 20,
        (t, s, u, v, depth, own, ev, od),
    )
    pairs_e, pairs_o = [], []
    top = n_lat - 1
    for p in range(n_lon):
        for l in range(n_lat):
            pairs_e.append((p * n_lat + l, p * n_lat + (l ^ 1)))
            if 0 < l < top:
                pairs_o.append((p * n_lat + l, p * n_lat + ((l + 1) ^ 1) - 1))
        pairs_o.append((p * n_lat + top, (n_lon - 1 - p) * n_lat + top))
    got_e = lax.ppermute(edge_e, ("lon", "lat"), pairs_e)
    got_o = lax.ppermute(edge_o, ("lon", "lat"), pairs_o)
    *parts, aux = call(
        inner_kernel,
        [VMEM] * 5 + [HBM] + [VMEM] * 4,
        [VMEM] * 5,
        [FLAT] * 4 + [(AUX, K, W)],
        1 << 24,
        (t, s, u, v, depth, pltpu.with_memory_space_constraint(visc, pltpu.HBM), own, ev, od, swept),
        [pltpu.SMEM((K,), F32), pltpu.SemaphoreType.DMA],
    )
    outs = call(
        finish_kernel,
        [VMEM] * 10,
        [HBM] * 4 + [VMEM] * 4,
        [FLAT] * 8,
        1 << 22,
        (u, v, depth, *parts, aux, got_e, got_o),
        [pltpu.SemaphoreType.DMA((4,))],
        {3: 4, 4: 5, 5: 6, 6: 7},
    )
    return tuple(x.reshape(K, J, W) for x in outs[:4])


def solution(mesh):
    field, flat = P(None, "lat", "lon"), P("lat", "lon")
    return jax.shard_map(
        body,
        mesh=mesh,
        in_specs=(field, field, field, field, flat, flat, P()),
        out_specs=(field,) * 4,
        check_vma=False,
    )
```

```python
import functools

import jax
import jax.numpy as jnp
from jax import lax
from jax.experimental import pallas as pl
from jax.experimental.pallas import tpu as pltpu
from jax.sharding import PartitionSpec as P

K, J, W = 16, 16, 128
WIN = 6
PHASE = (0, 3, 0, 3, 0)
SEND_ROWS = 21
F32 = jnp.float32


def lanes():
    return lax.broadcasted_iota(jnp.int32, (K, W), 1)


def levels():
    return lax.broadcasted_iota(jnp.int32, (K, W), 0).astype(F32)


def low_half(lane):
    return lane - WIN * ((lane * 43) >> 8) < WIN // 2


def roll(x, shift):
    shift %= W
    return x if shift == 0 else pltpu.roll(x, shift, 1)


def load_row(ref, j):
    return ref[pl.ds(j, K, stride=J), :]


def store_row(ref, j, value):
    ref[pl.ds(j, K, stride=J), :] = value


def depth_row(depth_ref, j):
    return jnp.broadcast_to(depth_ref[pl.ds(j, 1), :], (K, W))


def wet_of(depth):
    return jnp.where(levels() < depth, 1.0, 0.0).astype(F32)


def unpack(packed, j):
    return roll(packed, -(WIN * j + 3))


def east(x, halo, lane):
    return roll(jnp.where(lane < 1, halo, x), -1)


def west(x, halo, lane):
    return roll(jnp.where(lane == W - 1, halo, x), 1)


def minmod(a, b):
    return jnp.maximum(jnp.minimum(a, jnp.maximum(b, 0.0)), jnp.minimum(b, 0.0))


def rise_fall(before, here, after):
    rise = minmod(0.5 * here + (1.0 / 12.0) * (before - after), here)
    return rise, here - rise


def limited(fall, rise):
    return minmod(fall, rise + rise), minmod(rise, fall + fall)


def weights(c):
    size = jnp.abs(c)
    rest = 1.0 - size
    return size * rest, rest * rest


def pack_columns(rows, phase):
    lane = lanes()
    packed = jnp.zeros((K, W), F32)
    for j, row in enumerate(rows):
        first = WIN * j + phase
        packed = jnp.where((lane >= first) & (lane < first + WIN), roll(row, first + 3), packed)
    return packed


def pack_kernel(*refs):
    sources, (t_ref, s_ref, u_ref, v_ref, d_ref, own_ref, ev_ref, od_ref) = refs[:6], refs[6:14]
    ind_ref, lay_ref, sems = refs[14:]
    copies = [
        pltpu.make_async_copy(src, dst, sems.at[n])
        for n, (src, dst) in enumerate(zip(sources, (t_ref, s_ref, u_ref, v_ref, ind_ref, lay_ref)))
    ]
    for n in (4, 5, 0, 1, 2, 3):
        copies[n].start()
    copies[4].wait()
    copies[5].wait()
    d_ref[...] = (ind_ref[...] * lay_ref[...]).astype(F32)
    d = pack_columns([depth_row(d_ref, j) for j in range(J)], 3)
    fields = []
    for n, ref in enumerate((t_ref, s_ref, u_ref, v_ref)):
        copies[n].wait()
        fields.append(pack_columns([load_row(ref, j) for j in range(J)], 3 if n == 1 else 0))
    fields.insert(3, d)
    for n, x in enumerate(fields):
        own_ref[:, n * W : (n + 1) * W] = x
    t, s, u, d, v = fields
    low = low_half(lanes())
    even = (lax.axis_index("lon") & 1) == 0
    for n, (a, b) in enumerate(((t, s), (u, d), (v, v))):
        to_east = jnp.where(low, a, b)
        to_west = jnp.where(low, b, a)
        at = slice(n * W, (n + 1) * W)
        ev_ref[:, at] = jnp.where(even, to_east, to_west)
        od_ref[:, at] = jnp.where(even, to_west, to_east)


def arrived(ev_ref, od_ref, n):
    even = (lax.axis_index("lon") & 1) == 0
    mate = pl.multiple_of(jnp.where(even, K, 0), K)
    at = slice((n // 2) * W, (n // 2 + 1) * W)
    ev = ev_ref[pl.ds(mate, K), at]
    od = od_ref[:, at]
    return jnp.where(even, od, ev), jnp.where(even, ev, od)


def seams(own_ref, ev_ref, od_ref):
    low = low_half(lanes())
    out = []
    for n in range(5):
        from_west, from_east = arrived(ev_ref, od_ref, n)
        own = own_ref[:, n * W : (n + 1) * W]
        if PHASE[n]:
            from_west, from_east, own = (roll(x, -3) for x in (from_west, from_east, own))
        out.append(
            (
                jnp.where(low, from_west, from_east),
                jnp.where(low, from_west, own),
                jnp.where(low, own, from_east),
            )
        )
    return out


def seam_flux(q, c, wet):
    step = roll(q, -1) - q
    rise, fall = rise_fall(roll(step, 1), step, roll(step, -1))
    down, up = limited(roll(fall, 1), rise)
    near, far = weights(c)
    out_right = q + (near * down + far * up)
    near, far = weights(roll(c, 1))
    out_left = q - (near * up + far * down)
    return fall, c * wet * roll(wet, -1) * jnp.where(c > 0.0, out_right, roll(out_left, -1))


def in_step(walks):
    out = [None] * len(walks)
    live = list(range(len(walks)))
    while live:
        for n in tuple(live):
            try:
                next(walks[n])
            except StopIteration as end:
                out[n] = end.value
                live.remove(n)
    return out


class Zonal:
    def __init__(self, packs, u_ref, d_ref):
        self.packs, self.u_ref, self.d_ref = packs, u_ref, d_ref
        lane = lanes()
        third = lane - WIN * ((lane * 43) >> 8) == 2
        _, uw, ue = packs[2]
        _, dw, de = packs[3]
        ww, we = wet_of(dw), wet_of(de)
        self.fix = []
        for n in range(2):
            fall_w, flux_w = seam_flux(packs[n][1], uw, ww)
            _, flux_e = seam_flux(packs[n][2], ue, we)
            self.fix.append((jnp.where(third, flux_e, roll(fall_w, 1)), flux_w))

    def row(self, refs, j):
        lane = lanes()
        last = lane == W - 1
        u = load_row(self.u_ref, j)
        wet = wet_of(depth_row(self.d_ref, j))
        halo_wet = unpack(self.packs[3][0], j)
        halo_u = unpack(self.packs[2][0], j)
        halos = [unpack(self.packs[n][0], j) for n in range(2)]
        fixes = [[unpack(x, j) for x in self.fix[n]] for n in range(2)]
        q = [load_row(ref, j) for ref in refs]
        yield
        halo_wet = wet_of(halo_wet)
        right = [east(q[n], halos[n], lane) for n in range(2)]
        left = [west(q[n], halos[n], lane) for n in range(2)]
        beyond = [roll(jnp.where(lane < 2, halos[n], q[n]), -2) for n in range(2)]
        u_west = west(u, halo_u, lane)
        wet_east = east(wet, halo_wet, lane)
        yield
        edges = [rise_fall(q[n] - left[n], right[n] - q[n], beyond[n] - right[n]) for n in range(2)]
        falls = [roll(edges[n][1], 1) for n in range(2)]
        yield
        near, far = weights(u)
        near_w, far_w = weights(u_west)
        face = u * wet * wet_east
        forward = u > 0.0
        cells = [
            limited(jnp.where(lane == 0, fixes[n][0], falls[n]), edges[n][0]) for n in range(2)
        ]
        from_right = [roll(q[n] - (near_w * cells[n][1] + far_w * cells[n][0]), -1) for n in range(2)]
        yield
        flux = [
            face * jnp.where(forward, q[n] + (near * cells[n][0] + far * cells[n][1]), from_right[n])
            for n in range(2)
        ]
        before = [roll(jnp.where(last, fixes[n][1], flux[n]), 1) for n in range(2)]
        yield
        return [q[n] - (jnp.where(last, fixes[n][0], flux[n]) - before[n]) for n in range(2)]


def zonal_masks(wet, halo_wet, lane):
    return wet * east(wet, halo_wet, lane), wet * west(wet, halo_wet, lane)


def zonal_lap(f, halo, masks, lane):
    return masks[0] * (east(f, halo, lane) - f) - masks[1] * (f - west(f, halo, lane))


def seam_lap(f, wet):
    total = None
    for shift in (1, -1, WIN, -WIN):
        term = wet * roll(wet, shift) * (roll(f, shift) - f)
        total = term if total is None else total + term
    return total


def edge_kernel(
    t_ref, s_ref, u_ref, v_ref, d_ref, own_ref, ev_ref, od_ref, swept_ref, e_ref, o_ref
):
    lane = lanes()
    lane8, sub8 = lane[:8], lax.broadcasted_iota(jnp.int32, (8, W), 0)
    packs = seams(own_ref, ev_ref, od_ref)
    zonal = Zonal(packs, u_ref, d_ref)
    packs = [p[0] for p in packs]
    wet = {j: wet_of(depth_row(d_ref, j)) for j in (0, 1, 2, 13, 14, 15)}
    halo_wet = {j: wet_of(unpack(packs[3], j)) for j in (0, 15)}
    halves = []
    all_rows = (15, 14, 13, 0, 1, 2)
    swept = []
    for at in range(0, 6, 6):
        swept += in_step([zonal.row((t_ref, s_ref), j) for j in all_rows[at : at + 6]])
    planes_of = (swept[:3], swept[3:])
    for side, rows in enumerate(((J - 1, J - 2, J - 3), (0, 1, 2))):
        planes = planes_of[side]
        for j, (t, s) in zip(rows, planes):
            swept_ref[j if j < 3 else j - 10] = t
            swept_ref[6 + (j if j < 3 else j - 10)] = s
        half = [p[0] for p in planes] + [p[1] for p in planes]
        j, inward = rows[0], rows[1]
        masks = zonal_masks(wet[j], halo_wet[j], lane)
        to_inner = wet[j] * wet[inward]
        for ref, pack in ((u_ref, packs[2]), (v_ref, packs[4])):
            f = load_row(ref, j)
            partial = zonal_lap(f, unpack(pack, j), masks, lane) + to_inner * (load_row(ref, inward) - f)
            half += [f, partial]
        depth = depth_row(d_ref, j)[:8]
        corner = jnp.where(sub8 < 4, depth, roll(depth, W // 2))
        for at, (pack, top) in enumerate(
            ((packs[2], 0), (packs[4], 0), (packs[2], 8), (packs[4], 8), (packs[3], 0))
        ):
            home = -(WIN * j + 3)
            part = pack[top : top + 8]
            corner = jnp.where(lane8 == at, roll(part, home + at), corner)
            corner = jnp.where(lane8 == W - 1 - at, roll(part, home - at), corner)
        halves.append((half, corner))
    lat = lax.axis_index("lat")
    even = (lat & 1) == 0
    (north, north_c), (south, south_c) = halves
    for n, (a, b) in enumerate(zip(north, south)):
        e_ref[2 * n : 2 * n + 2] = jnp.where(even, a, b).reshape(2, 8, W)
        o_ref[2 * n : 2 * n + 2] = jnp.where(even, b, a).reshape(2, 8, W)
    e_ref[SEND_ROWS - 1] = jnp.where(even, north_c, south_c)
    o_ref[SEND_ROWS - 1] = jnp.where(even, south_c, north_c)

    @pl.when(lat == lax.axis_size("lat") - 1)
    def _():
        for n in range(SEND_ROWS):
            x = jnp.take_along_axis(o_ref[n], W - 1 - lane8, axis=1)
            if 12 <= n < 20:
                x = -x
            elif n == 20:
                x = jnp.where((lane8 < 4) | (lane8 > W - 5), -x, x)
            o_ref[n] = x


def merid_cell(step, fall_before, j):
    rise, fall = rise_fall(step[j - 1], step[j], step[j + 1])
    down, up = limited(fall_before, rise)
    return down, up, fall


def merid_flux(c, wet_pair, q, q_next, cell, cell_next):
    forward = c > 0.0
    rest = 1.0 - jnp.abs(c)
    square = rest * rest
    near = jnp.where(forward, cell[0], cell_next[1])
    far = jnp.where(forward, cell[1], cell_next[0])
    return c * wet_pair * (
        jnp.where(forward, q, q_next) + (c * rest * near + jnp.where(forward, square, -square) * far)
    )


AUX_TRACER, AUX_FLOW = 12, 10


def inner_kernel(
    t_ref,
    s_ref,
    u_ref,
    v_ref,
    d_ref,
    visc_hbm,
    own_ref,
    ev_ref,
    od_ref,
    swept_ref,
    t_out,
    s_out,
    u_out,
    v_out,
    aux_ref,
    visc_ref,
    sem,
):
    copy = pltpu.make_async_copy(visc_hbm, visc_ref, sem)
    copy.start()
    lane = lanes()
    packs = seams(own_ref, ev_ref, od_ref)
    zonal = Zonal(packs, u_ref, d_ref)
    rows = [{}, {}]
    for j in (0, 1, 2, 13, 14, 15):
        for n in range(2):
            rows[n][j] = swept_ref[6 * n + (j if j < 3 else j - 10)]
    for at in range(3, 13, 3):
        group = range(at, min(at + 3, 13))
        for j, (t, s) in zip(group, in_step([zonal.row((t_ref, s_ref), j) for j in group])):
            rows[0][j], rows[1][j] = t, s
    wet = [wet_of(depth_row(d_ref, j)) for j in range(J)]
    for n, out in enumerate((t_out, s_out)):
        q = rows[n]
        for at, j in enumerate((0, 1, 2, 3, 4, 11, 12, 13, 14, 15)):
            aux_ref[AUX_TRACER * n + at] = q[j]
        step = [q[j + 1] - q[j] for j in range(J - 1)]
        cell = merid_cell(step, rise_fall(step[0], step[1], step[2])[1], 2)
        before = None
        for j in range(2, 13):
            after = merid_cell(step, cell[2], j + 1)
            flux = merid_flux(load_row(v_ref, j), wet[j] * wet[j + 1], q[j], q[j + 1], cell, after)
            if j == 2:
                aux_ref[AUX_TRACER * n + 10] = flux
            else:
                store_row(out, j, q[j] - (flux - before))
            if j == 12:
                aux_ref[AUX_TRACER * n + 11] = flux
            cell, before = after, flux
    wet_w, wet_e = wet_of(packs[3][1]), wet_of(packs[3][2])
    low = low_half(lane)
    copy.wait()
    visc = viscosity(visc_ref)
    halo_wet = [wet_of(unpack(packs[3][0], j)) for j in range(J)]
    masks = [zonal_masks(wet[j], halo_wet[j], lane) for j in range(J)]
    pair = [wet[j] * wet[j + 1] for j in range(J - 1)]
    for n, (ref, pack, out) in enumerate(((u_ref, packs[2], u_out), (v_ref, packs[4], v_out))):
        base = 2 * AUX_TRACER + AUX_FLOW * n
        halo_lap = jnp.where(low, seam_lap(pack[1], wet_w), seam_lap(pack[2], wet_e))
        f = [load_row(ref, j) for j in range(J)]
        lap = []
        step = None
        for j in range(J):
            total = zonal_lap(f[j], unpack(pack[0], j), masks[j], lane)
            if step is not None:
                total = total - step
            if j < J - 1:
                step = pair[j] * (f[j + 1] - f[j])
                total = total + step
            lap.append(total)
        step = None
        for j in range(1, J - 1):
            total = zonal_lap(lap[j], unpack(halo_lap, j), masks[j], lane)
            if step is not None:
                total = total - step
            if j < J - 2:
                step = pair[j] * (lap[j + 1] - lap[j])
                total = total + step
            if j == 1:
                aux_ref[base + 2] = total
            elif j == J - 2:
                aux_ref[base + 5] = total
            else:
                store_row(out, j, f[j] - visc * total)
        aux_ref[base + 0] = lap[0]
        aux_ref[base + 1] = lap[1]
        aux_ref[base + 3] = lap[J - 1]
        aux_ref[base + 4] = lap[J - 2]
        aux_ref[base + 6] = unpack(halo_lap, 0)
        aux_ref[base + 7] = unpack(halo_lap, J - 1)
        aux_ref[base + 8] = unpack(pack[0], 0)
        aux_ref[base + 9] = unpack(pack[0], J - 1)
    aux_ref[2 * AUX_TRACER + 2 * AUX_FLOW] = halo_wet[0]
    aux_ref[2 * AUX_TRACER + 2 * AUX_FLOW + 1] = halo_wet[J - 1]
    aux_ref[2 * AUX_TRACER + 2 * AUX_FLOW + 2] = visc


def viscosity(visc_ref):
    level = lax.broadcasted_iota(jnp.int32, (K, W), 0)
    visc = jnp.zeros((K, W), F32)
    for k in range(K):
        visc = jnp.where(level == k, visc_ref[k], visc)
    return visc


def finish_side(side, got_ref, u_ref, v_ref, d_ref, aux_ref, outs, finals, sems):
    lane = lanes()
    t_out, s_out, u_out, v_out = outs
    half = pl.ds(8 * (1 - side), 8)
    copies = [
        pltpu.make_async_copy(
            src.reshape(K, J, W).at[:, half], dst.reshape(K, J, W).at[:, half], sems.at[n]
        )
        for n, (src, dst) in enumerate(zip(outs, finals))
    ]
    halo_at = 2 * AUX_TRACER + 2 * AUX_FLOW
    visc = aux_ref[halo_at + 2]

    def recv(n):
        return got_ref[2 * n : 2 * n + 2].reshape(K, W)

    faces = (13, 14, 15) if side == 0 else (-1, 0, 1)
    edge, inward, beyond = (15, 14, 16) if side == 0 else (0, 1, -1)
    wet = {j: wet_of(depth_row(d_ref, j)) for j in ((13, 14, 15) if side == 0 else (0, 1, 2))}
    tile = got_ref[SEND_ROWS - 1]
    lane8 = lane[:8]
    inside = (lane8 > 4) & (lane8 < W - 5)
    row = jnp.where(inside[:1], tile[:1], roll(tile, W // 2)[4:5])
    wet[beyond] = wet_of(jnp.broadcast_to(row, (K, W)))
    part = [tile] + [
        jnp.where(lane8 < W // 2, roll(tile, -m), roll(tile, m)) for m in range(1, 5)
    ]
    corner_flow = [jnp.concatenate([part[n], part[n + 2]], axis=0) for n in range(2)]
    corner_wet = wet_of(jnp.concatenate([part[4], part[4]], axis=0))
    courant = {j: recv(8) if j < 0 else load_row(v_ref, j) for j in faces}
    for n, out in enumerate((t_out, s_out)):
        aux = AUX_TRACER * n
        if side == 0:
            q = {11 + m: aux_ref[aux + 5 + m] for m in range(5)}
            q.update({16 + m: recv(3 * n + m) for m in range(3)})
            before = aux_ref[aux + 11]
        else:
            q = {j: aux_ref[aux + j] for j in range(5)}
            q.update({-1 - m: recv(3 * n + m) for m in range(3)})
            before = None
        step = {j: q[j + 1] - q[j] for j in q if j + 1 in q}
        first = faces[0]
        fall = rise_fall(step[first - 2], step[first - 1], step[first])[1]
        cell = merid_cell(step, fall, first)
        for j in faces:
            after = merid_cell(step, cell[2], j + 1)
            flux = merid_flux(courant[j], wet[j] * wet[j + 1], q[j], q[j + 1], cell, after)
            if before is not None:
                store_row(out, j, q[j] - (flux - before))
            cell, before = after, flux
        if side == 1:
            store_row(out, 2, q[2] - (aux_ref[aux + 10] - before))
        copies[n].start()
    halo_wet = aux_ref[halo_at + 1 - side]
    masks = zonal_masks(wet[edge], halo_wet, lane)
    across = wet[edge] * wet[beyond]
    for n, (ref, out) in enumerate(((u_ref, u_out), (v_ref, v_out))):
        base = 2 * AUX_TRACER + AUX_FLOW * n
        at = (3, 4, 5, 7, 9) if side == 0 else (0, 1, 2, 6, 8)
        lap_edge, lap_in, partial, halo_lap, halo_f = (aux_ref[base + a] for a in at)
        f, f_in = load_row(ref, edge), load_row(ref, inward)
        f_out, lap_out = recv(6 + 2 * n), recv(7 + 2 * n)
        step = across * (f_out - f)
        lap_edge = lap_edge + step
        lap_out = lap_out - step
        halo_lap = halo_lap + halo_wet * corner_wet * (corner_flow[n] - halo_f)
        inner_step = wet[edge] * wet[inward] * (lap_in - lap_edge)
        total = (
            zonal_lap(lap_edge, halo_lap, masks, lane)
            + inner_step
            + across * (lap_out - lap_edge)
        )
        store_row(out, edge, f - visc * total)
        store_row(out, inward, f_in - visc * (partial - inner_step))
        copies[2 + n].start()
    for copy in copies:
        copy.wait()


def finish_kernel(north_if_even, *refs):
    u_ref, v_ref, d_ref, aux_ref, got_ref = refs[:5]
    finals, outs, sems = refs[-9:-5], refs[-5:-1], refs[-1]
    even = (lax.axis_index("lat") & 1) == 0

    @pl.when(even)
    def _():
        side = 0 if north_if_even else 1
        finish_side(side, got_ref, u_ref, v_ref, d_ref, aux_ref, outs, finals, sems)

    @pl.when(jnp.logical_not(even))
    def _():
        side = 1 if north_if_even else 0
        finish_side(side, got_ref, u_ref, v_ref, d_ref, aux_ref, outs, finals, sems)


VMEM = pl.BlockSpec(memory_space=pltpu.VMEM)
HBM = pl.BlockSpec(memory_space=pltpu.HBM)
FLAT = (K * J, W)
AUX = 2 * AUX_TRACER + 2 * AUX_FLOW + 3


def call(kernel, in_specs, out_specs, out_shapes, flops, args, scratch=(), aliases=()):
    return pl.pallas_call(
        kernel,
        out_shape=[jax.ShapeDtypeStruct(s, F32) for s in out_shapes],
        in_specs=in_specs,
        out_specs=out_specs,
        scratch_shapes=list(scratch),
        input_output_aliases=dict(aliases),
        cost_estimate=pl.CostEstimate(flops=flops, bytes_accessed=1 << 20, transcendentals=0),
        compiler_params=pltpu.CompilerParams(vmem_limit_bytes=32 << 20),
    )(*args)


def body(t, s, u, v, ind, lay, visc):
    t, s, u, v = (x.reshape(FLAT) for x in (t, s, u, v))
    n_lon, n_lat = lax.axis_size("lon"), lax.axis_size("lat")
    t, s, u, v, depth, own, ev, od = call(
        pack_kernel,
        [HBM] * 6,
        [VMEM] * 8,
        [FLAT] * 4 + [(J, W), (K, 5 * W), (K, 3 * W), (K, 3 * W)],
        1 << 20,
        [pltpu.with_memory_space_constraint(x, pltpu.HBM) for x in (t, s, u, v, ind, lay)],
        [pltpu.VMEM((J, W), jnp.int32)] * 2 + [pltpu.SemaphoreType.DMA((6,))],
    )
    od = lax.ppermute(od, "lon", [(i, (((i + 1) ^ 1) - 1) % n_lon) for i in range(n_lon)])
    ev = lax.all_gather(
        ev, "lon", axis_index_groups=[[i, i + 1] for i in range(0, n_lon, 2)], tiled=True
    )
    swept, edge_e, edge_o = call(
        edge_kernel,
        [VMEM] * 8,
        [VMEM] * 3,
        [(12, K, W), (SEND_ROWS, 8, W), (SEND_ROWS, 8, W)],
        1 << 20,
        (t, s, u, v, depth, own, ev, od),
    )
    pairs_e, pairs_o = [], []
    top = n_lat - 1
    for p in range(n_lon):
        for l in range(n_lat):
            pairs_e.append((p * n_lat + l, p * n_lat + (l ^ 1)))
            if 0 < l < top:
                pairs_o.append((p * n_lat + l, p * n_lat + ((l + 1) ^ 1) - 1))
        pairs_o.append((p * n_lat + top, (n_lon - 1 - p) * n_lat + top))
    got_e = lax.ppermute(edge_e, ("lon", "lat"), pairs_e)
    got_o = lax.ppermute(edge_o, ("lon", "lat"), pairs_o)
    *parts, aux = call(
        inner_kernel,
        [VMEM] * 5 + [HBM] + [VMEM] * 4,
        [VMEM] * 5,
        [FLAT] * 4 + [(AUX, K, W)],
        1 << 24,
        (t, s, u, v, depth, pltpu.with_memory_space_constraint(visc, pltpu.HBM), own, ev, od, swept),
        [pltpu.SMEM((K,), F32), pltpu.SemaphoreType.DMA],
    )
    flow = (u, v, depth, aux)
    outs = call(
        functools.partial(finish_kernel, True),
        [VMEM] * 9,
        [HBM] * 4 + [VMEM] * 4,
        [FLAT] * 8,
        1 << 21,
        (*flow, got_e, *parts),
        [pltpu.SemaphoreType.DMA((4,))],
        {5: 4, 6: 5, 7: 6, 8: 7},
    )
    outs = call(
        functools.partial(finish_kernel, False),
        [VMEM] * 5 + [HBM] * 4 + [VMEM] * 4,
        [HBM] * 4 + [VMEM] * 4,
        [FLAT] * 8,
        1 << 21,
        (*flow, got_o, *outs),
        [pltpu.SemaphoreType.DMA((4,))],
        {5 + n: n for n in range(8)},
    )
    return tuple(x.reshape(K, J, W) for x in outs[:4])


def solution(mesh):
    field, flat = P(None, "lat", "lon"), P("lat", "lon")
    return jax.shard_map(
        body,
        mesh=mesh,
        in_specs=(field, field, field, field, flat, flat, P()),
        out_specs=(field,) * 4,
        check_vma=False,
    )
```

```python
import functools

import jax
import jax.numpy as jnp
from jax import lax
from jax.experimental import pallas as pl
from jax.experimental.pallas import tpu as pltpu
from jax.sharding import PartitionSpec as P

K, J, W = 16, 16, 128
WIN = 6
PHASE = (0, 3, 0, 3, 0)
SEND_ROWS = 21
F32 = jnp.float32


def lanes():
    return lax.broadcasted_iota(jnp.int32, (K, W), 1)


def levels():
    return lax.broadcasted_iota(jnp.int32, (K, W), 0).astype(F32)


def low_half(lane):
    return lane - WIN * ((lane * 43) >> 8) < WIN // 2


def roll(x, shift):
    shift %= W
    return x if shift == 0 else pltpu.roll(x, shift, 1)


def load_row(ref, j):
    return ref[pl.ds(j, K, stride=J), :]


def store_row(ref, j, value):
    ref[pl.ds(j, K, stride=J), :] = value


def depth_row(depth_ref, j):
    return jnp.broadcast_to(depth_ref[pl.ds(j, 1), :], (K, W))


def wet_of(depth):
    return jnp.where(levels() < depth, 1.0, 0.0).astype(F32)


def unpack(packed, j):
    return roll(packed, -(WIN * j + 3))


def east(x, halo, lane):
    return roll(jnp.where(lane < 1, halo, x), -1)


def west(x, halo, lane):
    return roll(jnp.where(lane == W - 1, halo, x), 1)


def minmod(a, b):
    return jnp.maximum(jnp.minimum(a, jnp.maximum(b, 0.0)), jnp.minimum(b, 0.0))


def rise_fall(before, here, after):
    rise = minmod(0.5 * here + (1.0 / 12.0) * (before - after), here)
    return rise, here - rise


def limited(fall, rise):
    return minmod(fall, rise + rise), minmod(rise, fall + fall)


def weights(c):
    size = jnp.abs(c)
    rest = 1.0 - size
    return size * rest, rest * rest


def pack_columns(rows, phase):
    lane = lanes()
    packed = jnp.zeros((K, W), F32)
    moved = [roll(row, WIN * j + phase + 3) for j, row in enumerate(rows)]
    for j, row in enumerate(moved):
        first = WIN * j + phase
        packed = jnp.where((lane >= first) & (lane < first + WIN), row, packed)
    return packed


def pack_kernel(*refs):
    sources, (t_ref, s_ref, u_ref, v_ref, d_ref, own_ref, ev_ref, od_ref) = refs[:6], refs[6:14]
    ind_ref, lay_ref, sems = refs[14:]
    copies = [
        pltpu.make_async_copy(src, dst, sems.at[n])
        for n, (src, dst) in enumerate(zip(sources, (t_ref, s_ref, u_ref, v_ref, ind_ref, lay_ref)))
    ]
    for n in (4, 5, 0, 1, 2, 3):
        copies[n].start()
    copies[4].wait()
    copies[5].wait()
    d_ref[...] = (ind_ref[...] * lay_ref[...]).astype(F32)
    d = pack_columns([depth_row(d_ref, j) for j in range(J)], 3)
    fields = []
    for n, ref in enumerate((t_ref, s_ref, u_ref, v_ref)):
        copies[n].wait()
        fields.append(pack_columns([load_row(ref, j) for j in range(J)], 3 if n == 1 else 0))
    fields.insert(3, d)
    for n, x in enumerate(fields):
        own_ref[:, n * W : (n + 1) * W] = x
    t, s, u, d, v = fields
    low = low_half(lanes())
    even = (lax.axis_index("lon") & 1) == 0
    for n, (a, b) in enumerate(((t, s), (u, d), (v, v))):
        to_east = jnp.where(low, a, b)
        to_west = jnp.where(low, b, a)
        at = slice(n * W, (n + 1) * W)
        ev_ref[:, at] = jnp.where(even, to_east, to_west)
        od_ref[:, at] = jnp.where(even, to_west, to_east)


def arrived(ev_ref, od_ref, n):
    even = (lax.axis_index("lon") & 1) == 0
    mate = pl.multiple_of(jnp.where(even, K, 0), K)
    at = slice((n // 2) * W, (n // 2 + 1) * W)
    ev = ev_ref[pl.ds(mate, K), at]
    od = od_ref[:, at]
    return jnp.where(even, od, ev), jnp.where(even, ev, od)


def seams(own_ref, ev_ref, od_ref):
    low = low_half(lanes())
    out = []
    for n in range(5):
        from_west, from_east = arrived(ev_ref, od_ref, n)
        own = own_ref[:, n * W : (n + 1) * W]
        if PHASE[n]:
            from_west, from_east, own = (roll(x, -3) for x in (from_west, from_east, own))
        out.append(
            (
                jnp.where(low, from_west, from_east),
                jnp.where(low, from_west, own),
                jnp.where(low, own, from_east),
            )
        )
    return out


def in_step(walks):
    out = [None] * len(walks)
    live = list(range(len(walks)))
    while live:
        for n in tuple(live):
            try:
                next(walks[n])
            except StopIteration as end:
                out[n] = end.value
                live.remove(n)
    return out


class Zonal:
    def __init__(self, packs, u_ref, d_ref):
        self.packs, self.u_ref, self.d_ref = packs, u_ref, d_ref
        self.flux = {}
        self.fall = {}

    def seam_walks(self):
        return [self.seam(n, side) for n in range(2) for side in (1, 2)]

    def seam(self, n, side):
        q, c, wet = self.packs[n][side], self.packs[2][side], wet_of(self.packs[3][side])
        q_next, c_west, wet_next = roll(q, -1), roll(c, 1), roll(wet, -1)
        yield
        step = q_next - q
        before, after = roll(step, 1), roll(step, -1)
        yield
        rise, fall = rise_fall(before, step, after)
        fall_before = roll(fall, 1)
        yield
        down, up = limited(fall_before, rise)
        near, far = weights(c_west)
        from_right = roll(q - (near * up + far * down), -1)
        yield
        near, far = weights(c)
        self.flux[n, side] = c * wet * wet_next * jnp.where(
            c > 0.0, q + (near * down + far * up), from_right
        )
        self.fall[n, side] = fall_before

    def fixes(self, n):
        lane = lanes()
        third = lane - WIN * ((lane * 43) >> 8) == 2
        return jnp.where(third, self.flux[n, 2], self.fall[n, 1]), self.flux[n, 1]

    def row(self, refs, j):
        lane = lanes()
        last = lane == W - 1
        u = load_row(self.u_ref, j)
        wet = wet_of(depth_row(self.d_ref, j))
        halo_wet = unpack(self.packs[3][0], j)
        halo_u = unpack(self.packs[2][0], j)
        halos = [unpack(self.packs[n][0], j) for n in range(2)]
        q = [load_row(ref, j) for ref in refs]
        yield
        halo_wet = wet_of(halo_wet)
        right = [east(q[n], halos[n], lane) for n in range(2)]
        left = [west(q[n], halos[n], lane) for n in range(2)]
        beyond = [roll(jnp.where(lane < 2, halos[n], q[n]), -2) for n in range(2)]
        u_west = west(u, halo_u, lane)
        wet_east = east(wet, halo_wet, lane)
        yield
        edges = [rise_fall(q[n] - left[n], right[n] - q[n], beyond[n] - right[n]) for n in range(2)]
        falls = [roll(edges[n][1], 1) for n in range(2)]
        yield
        near, far = weights(u)
        near_w, far_w = weights(u_west)
        face = u * wet * wet_east
        while (1, 2) not in self.flux:
            yield
        fixes = [[unpack(x, j) for x in self.fixes(n)] for n in range(2)]
        yield
        forward = u > 0.0
        cells = [
            limited(jnp.where(lane == 0, fixes[n][0], falls[n]), edges[n][0]) for n in range(2)
        ]
        from_right = [roll(q[n] - (near_w * cells[n][1] + far_w * cells[n][0]), -1) for n in range(2)]
        yield
        flux = [
            face * jnp.where(forward, q[n] + (near * cells[n][0] + far * cells[n][1]), from_right[n])
            for n in range(2)
        ]
        before = [roll(jnp.where(last, fixes[n][1], flux[n]), 1) for n in range(2)]
        yield
        return [q[n] - (jnp.where(last, fixes[n][0], flux[n]) - before[n]) for n in range(2)]


def zonal_masks(wet, halo_wet, lane):
    return wet * east(wet, halo_wet, lane), wet * west(wet, halo_wet, lane)


def zonal_lap(f, halo, masks, lane):
    return masks[0] * (east(f, halo, lane) - f) - masks[1] * (f - west(f, halo, lane))


def seam_lap(f, wet):
    total = None
    for shift in (1, -1, WIN, -WIN):
        term = wet * roll(wet, shift) * (roll(f, shift) - f)
        total = term if total is None else total + term
    return total


def edge_kernel(
    t_ref, s_ref, u_ref, v_ref, d_ref, own_ref, ev_ref, od_ref, swept_ref, e_ref, o_ref
):
    lane = lanes()
    lane8, sub8 = lane[:8], lax.broadcasted_iota(jnp.int32, (8, W), 0)
    packs = seams(own_ref, ev_ref, od_ref)
    zonal = Zonal(packs, u_ref, d_ref)
    packs = [p[0] for p in packs]
    wet = {j: wet_of(depth_row(d_ref, j)) for j in (0, 1, 2, 13, 14, 15)}
    all_rows = (15, 14, 13, 0, 1, 2)

    def partial_lap(ref, pack, j, inward):
        f = load_row(ref, j)
        halo, dry = unpack(pack, j), unpack(packs[3], j)
        yield
        right, left = east(f, halo, lane), west(f, halo, lane)
        dry = wet_of(dry)
        wet_r, wet_l = east(wet[j], dry, lane), west(wet[j], dry, lane)
        yield
        return wet[j] * (
            wet_r * (right - f)
            + wet_l * (left - f)
            + wet[inward] * (load_row(ref, inward) - f)
        )

    def corner_tile(j):
        depth = depth_row(d_ref, j)[:8]
        far = roll(depth, W // 2)
        parts = []
        for at, (pack, top) in enumerate(
            ((packs[2], 0), (packs[4], 0), (packs[2], 8), (packs[4], 8), (packs[3], 0))
        ):
            home = -(WIN * j + 3)
            part = pack[top : top + 8]
            parts += [(at, roll(part, home + at)), (W - 1 - at, roll(part, home - at))]
        yield
        corner = jnp.where(sub8 < 4, depth, far)
        for at, part in parts:
            corner = jnp.where(lane8 == at, part, corner)
        return corner

    sides = ((J - 1, J - 2), (0, 1))
    flows = ((u_ref, packs[2]), (v_ref, packs[4]))
    seam_walks = zonal.seam_walks()
    done = in_step(
        seam_walks
        + [zonal.row((t_ref, s_ref), j) for j in all_rows]
        + [partial_lap(*flow, *rows) for rows in sides for flow in flows]
        + [corner_tile(rows[0]) for rows in sides]
    )[len(seam_walks) :]
    halves = []
    for side, (edge, _) in enumerate(sides):
        planes = done[3 * side : 3 * side + 3]
        for j, (t, s) in zip(all_rows[3 * side : 3 * side + 3], planes):
            swept_ref[j if j < 3 else j - 10] = t
            swept_ref[6 + (j if j < 3 else j - 10)] = s
        half = [p[0] for p in planes] + [p[1] for p in planes]
        for n, (ref, _) in enumerate(flows):
            half += [load_row(ref, edge), done[6 + 2 * side + n]]
        halves.append((half, done[10 + side]))
    lat = lax.axis_index("lat")
    even = (lat & 1) == 0
    (north, north_c), (south, south_c) = halves
    for n, (a, b) in enumerate(zip(north, south)):
        e_ref[2 * n : 2 * n + 2] = jnp.where(even, a, b).reshape(2, 8, W)
        o_ref[2 * n : 2 * n + 2] = jnp.where(even, b, a).reshape(2, 8, W)
    e_ref[SEND_ROWS - 1] = jnp.where(even, north_c, south_c)
    o_ref[SEND_ROWS - 1] = jnp.where(even, south_c, north_c)

    @pl.when(lat == lax.axis_size("lat") - 1)
    def _():
        for n in range(SEND_ROWS):
            x = jnp.take_along_axis(o_ref[n], W - 1 - lane8, axis=1)
            if 12 <= n < 20:
                x = -x
            elif n == 20:
                x = jnp.where((lane8 < 4) | (lane8 > W - 5), -x, x)
            o_ref[n] = x


def merid_cell(step, fall_before, j):
    rise, fall = rise_fall(step[j - 1], step[j], step[j + 1])
    down, up = limited(fall_before, rise)
    return down, up, fall


def merid_flux(c, wet_pair, q, q_next, cell, cell_next):
    forward = c > 0.0
    rest = 1.0 - jnp.abs(c)
    square = rest * rest
    near = jnp.where(forward, cell[0], cell_next[1])
    far = jnp.where(forward, cell[1], cell_next[0])
    return c * wet_pair * (
        jnp.where(forward, q, q_next) + (c * rest * near + jnp.where(forward, square, -square) * far)
    )


AUX_TRACER, AUX_FLOW = 12, 10


def inner_kernel(
    t_ref,
    s_ref,
    u_ref,
    v_ref,
    d_ref,
    visc_hbm,
    own_ref,
    ev_ref,
    od_ref,
    swept_ref,
    t_out,
    s_out,
    u_out,
    v_out,
    aux_ref,
    visc_ref,
    sem,
    mask_ref,
    lap_ref,
):
    copy = pltpu.make_async_copy(visc_hbm, visc_ref, sem)
    copy.start()
    lane = lanes()
    packs = seams(own_ref, ev_ref, od_ref)
    zonal = Zonal(packs, u_ref, d_ref)
    rows = [{}, {}]
    for j in (0, 1, 2, 13, 14, 15):
        for n in range(2):
            rows[n][j] = swept_ref[6 * n + (j if j < 3 else j - 10)]
    in_step(zonal.seam_walks())
    for at in range(3, 13, 10):
        group = range(at, min(at + 10, 13))
        for j, (t, s) in zip(group, in_step([zonal.row((t_ref, s_ref), j) for j in group])):
            rows[0][j], rows[1][j] = t, s
    wet = [wet_of(depth_row(d_ref, j)) for j in range(J)]
    for n, out in enumerate((t_out, s_out)):
        q = rows[n]
        for at, j in enumerate((0, 1, 2, 3, 4, 11, 12, 13, 14, 15)):
            aux_ref[AUX_TRACER * n + at] = q[j]
        step = [q[j + 1] - q[j] for j in range(J - 1)]
        cell = merid_cell(step, rise_fall(step[0], step[1], step[2])[1], 2)
        before = None
        for j in range(2, 13):
            after = merid_cell(step, cell[2], j + 1)
            flux = merid_flux(load_row(v_ref, j), wet[j] * wet[j + 1], q[j], q[j + 1], cell, after)
            if j == 2:
                aux_ref[AUX_TRACER * n + 10] = flux
            else:
                store_row(out, j, q[j] - (flux - before))
            if j == 12:
                aux_ref[AUX_TRACER * n + 11] = flux
            cell, before = after, flux
    wet_w, wet_e = wet_of(packs[3][1]), wet_of(packs[3][2])
    low = low_half(lane)
    halo_wet = {}

    def mask_row(j):
        halo = unpack(packs[3][0], j)
        yield
        halo = wet_of(halo)
        if j in (0, J - 1):
            halo_wet[j] = halo
        right, left = east(wet[j], halo, lane), west(wet[j], halo, lane)
        yield
        mask_ref[j] = wet[j] * right
        mask_ref[J + j] = wet[j] * left
        if j < J - 1:
            mask_ref[2 * J + j] = wet[j] * wet[j + 1]

    def lap_row(n, packed, load, j, first, last):
        here = load(n, j)
        halo = unpack(packed, j)
        yield
        right, left = east(here, halo, lane), west(here, halo, lane)
        yield
        total = mask_ref[j] * (right - here) - mask_ref[J + j] * (here - left)
        if j > first:
            total = total - mask_ref[2 * J + j - 1] * (here - load(n, j - 1))
        if j < last:
            total = total + mask_ref[2 * J + j] * (load(n, j + 1) - here)
        return total

    def walk(makers):
        for at in range(0, len(makers), 16):
            in_step([m() for m in makers[at : at + 16]])

    walk([functools.partial(mask_row, j) for j in range(J)])
    flows = ((u_ref, packs[2], u_out), (v_ref, packs[4], v_out))

    def inner(n, j):
        lap_ref[J * n + j] = yield from lap_row(n, flows[n][1][0], lambda n, j: load_row(flows[n][0], j), j, 0, J - 1)

    walk([functools.partial(inner, n, j) for j in range(J) for n in range(2)])
    halo_laps = [
        jnp.where(low, seam_lap(pack[1], wet_w), seam_lap(pack[2], wet_e)) for _, pack, _ in flows
    ]
    copy.wait()
    visc = viscosity(visc_ref)

    def outer(n, j):
        total = yield from lap_row(n, halo_laps[n], lambda n, j: lap_ref[J * n + j], j, 1, J - 2)
        base = 2 * AUX_TRACER + AUX_FLOW * n
        if j == 1:
            aux_ref[base + 2] = total
        elif j == J - 2:
            aux_ref[base + 5] = total
        else:
            store_row(flows[n][2], j, load_row(flows[n][0], j) - visc * total)

    walk([functools.partial(outer, n, j) for j in range(1, J - 1) for n in range(2)])
    for n, (_, pack, _) in enumerate(flows):
        base = 2 * AUX_TRACER + AUX_FLOW * n
        aux_ref[base + 0] = lap_ref[J * n]
        aux_ref[base + 1] = lap_ref[J * n + 1]
        aux_ref[base + 3] = lap_ref[J * n + J - 1]
        aux_ref[base + 4] = lap_ref[J * n + J - 2]
        aux_ref[base + 6] = unpack(halo_laps[n], 0)
        aux_ref[base + 7] = unpack(halo_laps[n], J - 1)
        aux_ref[base + 8] = unpack(pack[0], 0)
        aux_ref[base + 9] = unpack(pack[0], J - 1)
    aux_ref[2 * AUX_TRACER + 2 * AUX_FLOW] = halo_wet[0]
    aux_ref[2 * AUX_TRACER + 2 * AUX_FLOW + 1] = halo_wet[J - 1]
    aux_ref[2 * AUX_TRACER + 2 * AUX_FLOW + 2] = visc


def viscosity(visc_ref):
    level = lax.broadcasted_iota(jnp.int32, (K, W), 0)
    visc = jnp.zeros((K, W), F32)
    for k in range(K):
        visc = jnp.where(level == k, visc_ref[k], visc)
    return visc


def finish_side(side, got_ref, u_ref, v_ref, d_ref, aux_ref, outs, finals, sems):
    lane = lanes()
    t_out, s_out, u_out, v_out = outs
    half = pl.ds(8 * (1 - side), 8)
    copies = [
        pltpu.make_async_copy(
            src.reshape(K, J, W).at[:, half], dst.reshape(K, J, W).at[:, half], sems.at[n]
        )
        for n, (src, dst) in enumerate(zip(outs, finals))
    ]
    halo_at = 2 * AUX_TRACER + 2 * AUX_FLOW
    visc = aux_ref[halo_at + 2]

    def recv(n):
        return got_ref[2 * n : 2 * n + 2].reshape(K, W)

    faces = (13, 14, 15) if side == 0 else (-1, 0, 1)
    edge, inward, beyond = (15, 14, 16) if side == 0 else (0, 1, -1)
    wet = {j: wet_of(depth_row(d_ref, j)) for j in ((13, 14, 15) if side == 0 else (0, 1, 2))}
    tile = got_ref[SEND_ROWS - 1]
    lane8 = lane[:8]
    inside = (lane8 > 4) & (lane8 < W - 5)
    row = jnp.where(inside[:1], tile[:1], roll(tile, W // 2)[4:5])
    wet[beyond] = wet_of(jnp.broadcast_to(row, (K, W)))
    part = [tile] + [
        jnp.where(lane8 < W // 2, roll(tile, -m), roll(tile, m)) for m in range(1, 5)
    ]
    corner_flow = [jnp.concatenate([part[n], part[n + 2]], axis=0) for n in range(2)]
    corner_wet = wet_of(jnp.concatenate([part[4], part[4]], axis=0))
    courant = {j: recv(8) if j < 0 else load_row(v_ref, j) for j in faces}
    for n, out in enumerate((t_out, s_out)):
        aux = AUX_TRACER * n
        if side == 0:
            q = {11 + m: aux_ref[aux + 5 + m] for m in range(5)}
            q.update({16 + m: recv(3 * n + m) for m in range(3)})
            before = aux_ref[aux + 11]
        else:
            q = {j: aux_ref[aux + j] for j in range(5)}
            q.update({-1 - m: recv(3 * n + m) for m in range(3)})
            before = None
        step = {j: q[j + 1] - q[j] for j in q if j + 1 in q}
        first = faces[0]
        fall = rise_fall(step[first - 2], step[first - 1], step[first])[1]
        cell = merid_cell(step, fall, first)
        for j in faces:
            after = merid_cell(step, cell[2], j + 1)
            flux = merid_flux(courant[j], wet[j] * wet[j + 1], q[j], q[j + 1], cell, after)
            if before is not None:
                store_row(out, j, q[j] - (flux - before))
            cell, before = after, flux
        if side == 1:
            store_row(out, 2, q[2] - (aux_ref[aux + 10] - before))
        copies[n].start()
    halo_wet = aux_ref[halo_at + 1 - side]
    masks = zonal_masks(wet[edge], halo_wet, lane)
    across = wet[edge] * wet[beyond]
    for n, (ref, out) in enumerate(((u_ref, u_out), (v_ref, v_out))):
        base = 2 * AUX_TRACER + AUX_FLOW * n
        at = (3, 4, 5, 7, 9) if side == 0 else (0, 1, 2, 6, 8)
        lap_edge, lap_in, partial, halo_lap, halo_f = (aux_ref[base + a] for a in at)
        f, f_in = load_row(ref, edge), load_row(ref, inward)
        f_out, lap_out = recv(6 + 2 * n), recv(7 + 2 * n)
        step = across * (f_out - f)
        lap_edge = lap_edge + step
        lap_out = lap_out - step
        halo_lap = halo_lap + halo_wet * corner_wet * (corner_flow[n] - halo_f)
        inner_step = wet[edge] * wet[inward] * (lap_in - lap_edge)
        total = (
            zonal_lap(lap_edge, halo_lap, masks, lane)
            + inner_step
            + across * (lap_out - lap_edge)
        )
        store_row(out, edge, f - visc * total)
        store_row(out, inward, f_in - visc * (partial - inner_step))
        copies[2 + n].start()
    for copy in copies:
        copy.wait()


def finish_kernel(north_if_even, *refs):
    u_ref, v_ref, d_ref, aux_ref, got_ref = refs[:5]
    finals, outs, sems = refs[-9:-5], refs[-5:-1], refs[-1]
    even = (lax.axis_index("lat") & 1) == 0

    @pl.when(even)
    def _():
        side = 0 if north_if_even else 1
        finish_side(side, got_ref, u_ref, v_ref, d_ref, aux_ref, outs, finals, sems)

    @pl.when(jnp.logical_not(even))
    def _():
        side = 1 if north_if_even else 0
        finish_side(side, got_ref, u_ref, v_ref, d_ref, aux_ref, outs, finals, sems)


VMEM = pl.BlockSpec(memory_space=pltpu.VMEM)
HBM = pl.BlockSpec(memory_space=pltpu.HBM)
FLAT = (K * J, W)
AUX = 2 * AUX_TRACER + 2 * AUX_FLOW + 3


def call(kernel, in_specs, out_specs, out_shapes, flops, args, scratch=(), aliases=()):
    return pl.pallas_call(
        kernel,
        out_shape=[jax.ShapeDtypeStruct(s, F32) for s in out_shapes],
        in_specs=in_specs,
        out_specs=out_specs,
        scratch_shapes=list(scratch),
        input_output_aliases=dict(aliases),
        cost_estimate=pl.CostEstimate(flops=flops, bytes_accessed=1 << 20, transcendentals=0),
        compiler_params=pltpu.CompilerParams(vmem_limit_bytes=32 << 20),
    )(*args)


def body(t, s, u, v, ind, lay, visc):
    t, s, u, v = (x.reshape(FLAT) for x in (t, s, u, v))
    n_lon, n_lat = lax.axis_size("lon"), lax.axis_size("lat")
    t, s, u, v, depth, own, ev, od = call(
        pack_kernel,
        [HBM] * 6,
        [VMEM] * 8,
        [FLAT] * 4 + [(J, W), (K, 5 * W), (K, 3 * W), (K, 3 * W)],
        1 << 20,
        [pltpu.with_memory_space_constraint(x, pltpu.HBM) for x in (t, s, u, v, ind, lay)],
        [pltpu.VMEM((J, W), jnp.int32)] * 2 + [pltpu.SemaphoreType.DMA((6,))],
    )
    od = lax.ppermute(od, "lon", [(i, (((i + 1) ^ 1) - 1) % n_lon) for i in range(n_lon)])
    ev = lax.all_gather(
        ev, "lon", axis_index_groups=[[i, i + 1] for i in range(0, n_lon, 2)], tiled=True
    )
    swept, edge_e, edge_o = call(
        edge_kernel,
        [VMEM] * 8,
        [VMEM] * 3,
        [(12, K, W), (SEND_ROWS, 8, W), (SEND_ROWS, 8, W)],
        1 << 20,
        (t, s, u, v, depth, own, ev, od),
    )
    pairs_e, pairs_o = [], []
    top = n_lat - 1
    for p in range(n_lon):
        for l in range(n_lat):
            pairs_e.append((p * n_lat + l, p * n_lat + (l ^ 1)))
            if 0 < l < top:
                pairs_o.append((p * n_lat + l, p * n_lat + ((l + 1) ^ 1) - 1))
        pairs_o.append((p * n_lat + top, (n_lon - 1 - p) * n_lat + top))
    got_e = lax.ppermute(edge_e, ("lon", "lat"), pairs_e)
    got_o = lax.ppermute(edge_o, ("lon", "lat"), pairs_o)
    *parts, aux = call(
        inner_kernel,
        [VMEM] * 5 + [HBM] + [VMEM] * 4,
        [VMEM] * 5,
        [FLAT] * 4 + [(AUX, K, W)],
        1 << 24,
        (t, s, u, v, depth, pltpu.with_memory_space_constraint(visc, pltpu.HBM), own, ev, od, swept),
        [
            pltpu.SMEM((K,), F32),
            pltpu.SemaphoreType.DMA,
            pltpu.VMEM((3 * J, K, W), F32),
            pltpu.VMEM((2 * J, K, W), F32),
        ],
    )
    flow = (u, v, depth, aux)
    outs = call(
        functools.partial(finish_kernel, True),
        [VMEM] * 9,
        [HBM] * 4 + [VMEM] * 4,
        [FLAT] * 8,
        1 << 21,
        (*flow, got_e, *parts),
        [pltpu.SemaphoreType.DMA((4,))],
        {5: 4, 6: 5, 7: 6, 8: 7},
    )
    outs = call(
        functools.partial(finish_kernel, False),
        [VMEM] * 5 + [HBM] * 4 + [VMEM] * 4,
        [HBM] * 4 + [VMEM] * 4,
        [FLAT] * 8,
        1 << 21,
        (*flow, got_o, *outs),
        [pltpu.SemaphoreType.DMA((4,))],
        {5 + n: n for n in range(8)},
    )
    return tuple(x.reshape(K, J, W) for x in outs[:4])


def solution(mesh):
    field, flat = P(None, "lat", "lon"), P("lat", "lon")
    return jax.shard_map(
        body,
        mesh=mesh,
        in_specs=(field, field, field, field, flat, flat, P()),
        out_specs=(field,) * 4,
        check_vma=False,
    )
```

```python
import functools

import jax
import jax.numpy as jnp
from jax import lax
from jax.experimental import pallas as pl
from jax.experimental.pallas import tpu as pltpu
from jax.sharding import PartitionSpec as P

K, J, W = 16, 16, 128
WIN = 6
PHASE = (0, 3, 0, 3, 0)
SEND_ROWS = 21
F32 = jnp.float32


def lanes():
    return lax.broadcasted_iota(jnp.int32, (K, W), 1)


def levels():
    return lax.broadcasted_iota(jnp.int32, (K, W), 0).astype(F32)


def low_half(lane):
    return lane - WIN * ((lane * 43) >> 8) < WIN // 2


def roll(x, shift):
    shift %= W
    return x if shift == 0 else pltpu.roll(x, shift, 1)


def load_row(ref, j):
    return ref[pl.ds(j, K, stride=J), :]


def store_row(ref, j, value):
    ref[pl.ds(j, K, stride=J), :] = value


def depth_row(depth_ref, j):
    return jnp.broadcast_to(depth_ref[pl.ds(j, 1), :], (K, W))


def wet_of(depth):
    return jnp.where(levels() < depth, 1.0, 0.0).astype(F32)


def unpack(packed, j):
    return roll(packed, -(WIN * j + 3))


def east(x, halo, lane):
    return roll(jnp.where(lane < 1, halo, x), -1)


def west(x, halo, lane):
    return roll(jnp.where(lane == W - 1, halo, x), 1)


def minmod(a, b):
    return jnp.maximum(jnp.minimum(a, jnp.maximum(b, 0.0)), jnp.minimum(b, 0.0))


def rise_fall(before, here, after):
    rise = minmod(0.5 * here + (1.0 / 12.0) * (before - after), here)
    return rise, here - rise


def limited(fall, rise):
    return minmod(fall, rise + rise), minmod(rise, fall + fall)


def weights(c):
    size = jnp.abs(c)
    rest = 1.0 - size
    return size * rest, rest * rest


def pack_columns(rows, phase):
    lane = lanes()
    packed = jnp.zeros((K, W), F32)
    moved = [roll(row, WIN * j + phase + 3) for j, row in enumerate(rows)]
    for j, row in enumerate(moved):
        first = WIN * j + phase
        packed = jnp.where((lane >= first) & (lane < first + WIN), row, packed)
    return packed


def pack_kernel(*refs):
    sources, (t_ref, s_ref, u_ref, v_ref, d_ref, own_ref, ev_ref, od_ref) = refs[:6], refs[6:14]
    ind_ref, lay_ref, sems = refs[14:]
    copies = [
        pltpu.make_async_copy(src, dst, sems.at[n])
        for n, (src, dst) in enumerate(zip(sources, (t_ref, s_ref, u_ref, v_ref, ind_ref, lay_ref)))
    ]
    for n in (4, 5, 0, 1, 2, 3):
        copies[n].start()
    copies[4].wait()
    copies[5].wait()
    d_ref[...] = (ind_ref[...] * lay_ref[...]).astype(F32)
    d = pack_columns([depth_row(d_ref, j) for j in range(J)], 3)
    fields = []
    for n, ref in enumerate((t_ref, s_ref, u_ref, v_ref)):
        copies[n].wait()
        fields.append(pack_columns([load_row(ref, j) for j in range(J)], 3 if n == 1 else 0))
    fields.insert(3, d)
    for n, x in enumerate(fields):
        own_ref[:, n * W : (n + 1) * W] = x
    t, s, u, d, v = fields
    low = low_half(lanes())
    even = (lax.axis_index("lon") & 1) == 0
    for n, (a, b) in enumerate(((t, s), (u, d), (v, v))):
        to_east = jnp.where(low, a, b)
        to_west = jnp.where(low, b, a)
        at = slice(n * W, (n + 1) * W)
        ev_ref[:, at] = jnp.where(even, to_east, to_west)
        od_ref[:, at] = jnp.where(even, to_west, to_east)


def arrived(ev_ref, od_ref, n):
    even = (lax.axis_index("lon") & 1) == 0
    mate = pl.multiple_of(jnp.where(even, K, 0), K)
    at = slice((n // 2) * W, (n // 2 + 1) * W)
    ev = ev_ref[pl.ds(mate, K), at]
    od = od_ref[:, at]
    return jnp.where(even, od, ev), jnp.where(even, ev, od)


def seams(own_ref, ev_ref, od_ref):
    low = low_half(lanes())
    out = []
    for n in range(5):
        from_west, from_east = arrived(ev_ref, od_ref, n)
        own = own_ref[:, n * W : (n + 1) * W]
        if PHASE[n]:
            from_west, from_east, own = (roll(x, -3) for x in (from_west, from_east, own))
        out.append(
            (
                jnp.where(low, from_west, from_east),
                jnp.where(low, from_west, own),
                jnp.where(low, own, from_east),
            )
        )
    return out


def in_step(walks):
    out = [None] * len(walks)
    live = list(range(len(walks)))
    while live:
        for n in tuple(live):
            try:
                next(walks[n])
            except StopIteration as end:
                out[n] = end.value
                live.remove(n)
    return out


class Zonal:
    def __init__(self, packs, u_ref, d_ref):
        self.packs, self.u_ref, self.d_ref = packs, u_ref, d_ref
        self.flux = {}
        self.fall = {}

    def seam_walks(self):
        return [self.seam(n, side) for n in range(2) for side in (1, 2)]

    def seam(self, n, side):
        q, c, wet = self.packs[n][side], self.packs[2][side], wet_of(self.packs[3][side])
        q_next, c_west, wet_next = roll(q, -1), roll(c, 1), roll(wet, -1)
        yield
        step = q_next - q
        before, after = roll(step, 1), roll(step, -1)
        yield
        rise, fall = rise_fall(before, step, after)
        fall_before = roll(fall, 1)
        yield
        down, up = limited(fall_before, rise)
        near, far = weights(c_west)
        from_right = roll(q - (near * up + far * down), -1)
        yield
        near, far = weights(c)
        self.flux[n, side] = c * wet * wet_next * jnp.where(
            c > 0.0, q + (near * down + far * up), from_right
        )
        self.fall[n, side] = fall_before

    def fixes(self, n):
        lane = lanes()
        third = lane - WIN * ((lane * 43) >> 8) == 2
        return jnp.where(third, self.flux[n, 2], self.fall[n, 1]), self.flux[n, 1]

    def row(self, refs, j):
        lane = lanes()
        last = lane == W - 1
        u = load_row(self.u_ref, j)
        wet = wet_of(depth_row(self.d_ref, j))
        halo_wet = unpack(self.packs[3][0], j)
        halo_u = unpack(self.packs[2][0], j)
        halos = [unpack(self.packs[n][0], j) for n in range(2)]
        q = [load_row(ref, j) for ref in refs]
        yield
        halo_wet = wet_of(halo_wet)
        right = [east(q[n], halos[n], lane) for n in range(2)]
        left = [west(q[n], halos[n], lane) for n in range(2)]
        beyond = [roll(jnp.where(lane < 2, halos[n], q[n]), -2) for n in range(2)]
        u_west = west(u, halo_u, lane)
        wet_east = east(wet, halo_wet, lane)
        yield
        edges = [rise_fall(q[n] - left[n], right[n] - q[n], beyond[n] - right[n]) for n in range(2)]
        falls = [roll(edges[n][1], 1) for n in range(2)]
        yield
        near, far = weights(u)
        near_w, far_w = weights(u_west)
        face = u * wet * wet_east
        while (1, 2) not in self.flux:
            yield
        fixes = [[unpack(x, j) for x in self.fixes(n)] for n in range(2)]
        yield
        forward = u > 0.0
        cells = [
            limited(jnp.where(lane == 0, fixes[n][0], falls[n]), edges[n][0]) for n in range(2)
        ]
        from_right = [roll(q[n] - (near_w * cells[n][1] + far_w * cells[n][0]), -1) for n in range(2)]
        yield
        flux = [
            face * jnp.where(forward, q[n] + (near * cells[n][0] + far * cells[n][1]), from_right[n])
            for n in range(2)
        ]
        before = [roll(jnp.where(last, fixes[n][1], flux[n]), 1) for n in range(2)]
        yield
        return [q[n] - (jnp.where(last, fixes[n][0], flux[n]) - before[n]) for n in range(2)]


def zonal_masks(wet, halo_wet, lane):
    return wet * east(wet, halo_wet, lane), wet * west(wet, halo_wet, lane)


def zonal_lap(f, halo, masks, lane):
    return masks[0] * (east(f, halo, lane) - f) - masks[1] * (f - west(f, halo, lane))


def seam_lap(f, wet):
    total = None
    for shift in (1, -1, WIN, -WIN):
        term = wet * roll(wet, shift) * (roll(f, shift) - f)
        total = term if total is None else total + term
    return total


def edge_kernel(
    t_ref, s_ref, u_ref, v_ref, d_ref, own_ref, ev_ref, od_ref, swept_ref, e_ref, o_ref
):
    lane = lanes()
    lane8, sub8 = lane[:8], lax.broadcasted_iota(jnp.int32, (8, W), 0)
    packs = seams(own_ref, ev_ref, od_ref)
    zonal = Zonal(packs, u_ref, d_ref)
    packs = [p[0] for p in packs]
    wet = {j: wet_of(depth_row(d_ref, j)) for j in (0, 1, 2, 13, 14, 15)}
    all_rows = (15, 14, 13, 0, 1, 2)

    def partial_lap(ref, pack, j, inward):
        f = load_row(ref, j)
        halo, dry = unpack(pack, j), unpack(packs[3], j)
        yield
        right, left = east(f, halo, lane), west(f, halo, lane)
        dry = wet_of(dry)
        wet_r, wet_l = east(wet[j], dry, lane), west(wet[j], dry, lane)
        yield
        return wet[j] * (
            wet_r * (right - f)
            + wet_l * (left - f)
            + wet[inward] * (load_row(ref, inward) - f)
        )

    def corner_tile(j):
        depth = depth_row(d_ref, j)[:8]
        far = roll(depth, W // 2)
        parts = []
        for at, (pack, top) in enumerate(
            ((packs[2], 0), (packs[4], 0), (packs[2], 8), (packs[4], 8), (packs[3], 0))
        ):
            home = -(WIN * j + 3)
            part = pack[top : top + 8]
            parts += [(at, roll(part, home + at)), (W - 1 - at, roll(part, home - at))]
        yield
        corner = jnp.where(sub8 < 4, depth, far)
        for at, part in parts:
            corner = jnp.where(lane8 == at, part, corner)
        return corner

    sides = ((J - 1, J - 2), (0, 1))
    flows = ((u_ref, packs[2]), (v_ref, packs[4]))
    seam_walks = zonal.seam_walks()
    done = in_step(
        seam_walks
        + [zonal.row((t_ref, s_ref), j) for j in all_rows]
        + [partial_lap(*flow, *rows) for rows in sides for flow in flows]
        + [corner_tile(rows[0]) for rows in sides]
    )[len(seam_walks) :]
    halves = []
    for side, (edge, _) in enumerate(sides):
        planes = done[3 * side : 3 * side + 3]
        for j, (t, s) in zip(all_rows[3 * side : 3 * side + 3], planes):
            swept_ref[j if j < 3 else j - 10] = t
            swept_ref[6 + (j if j < 3 else j - 10)] = s
        half = [p[0] for p in planes] + [p[1] for p in planes]
        for n, (ref, _) in enumerate(flows):
            half += [load_row(ref, edge), done[6 + 2 * side + n]]
        halves.append((half, done[10 + side]))
    lat = lax.axis_index("lat")
    even = (lat & 1) == 0
    (north, north_c), (south, south_c) = halves
    for n, (a, b) in enumerate(zip(north, south)):
        e_ref[2 * n : 2 * n + 2] = jnp.where(even, a, b).reshape(2, 8, W)
        o_ref[2 * n : 2 * n + 2] = jnp.where(even, b, a).reshape(2, 8, W)
    e_ref[SEND_ROWS - 1] = jnp.where(even, north_c, south_c)
    o_ref[SEND_ROWS - 1] = jnp.where(even, south_c, north_c)

    @pl.when(lat == lax.axis_size("lat") - 1)
    def _():
        for n in range(SEND_ROWS):
            x = jnp.take_along_axis(o_ref[n], W - 1 - lane8, axis=1)
            if 12 <= n < 20:
                x = -x
            elif n == 20:
                x = jnp.where((lane8 < 4) | (lane8 > W - 5), -x, x)
            o_ref[n] = x


def merid_cell(step, fall_before, j):
    rise, fall = rise_fall(step[j - 1], step[j], step[j + 1])
    down, up = limited(fall_before, rise)
    return down, up, fall


def merid_flux(c, wet_pair, q, q_next, cell, cell_next):
    forward = c > 0.0
    rest = 1.0 - jnp.abs(c)
    square = rest * rest
    near = jnp.where(forward, cell[0], cell_next[1])
    far = jnp.where(forward, cell[1], cell_next[0])
    return c * wet_pair * (
        jnp.where(forward, q, q_next) + (c * rest * near + jnp.where(forward, square, -square) * far)
    )


AUX_TRACER, AUX_FLOW = 12, 10


def inner_kernel(
    t_ref,
    s_ref,
    u_ref,
    v_ref,
    d_ref,
    visc_hbm,
    own_ref,
    ev_ref,
    od_ref,
    swept_ref,
    t_out,
    s_out,
    u_out,
    v_out,
    aux_ref,
    visc_ref,
    sem,
    mask_ref,
    lap_ref,
):
    copy = pltpu.make_async_copy(visc_hbm, visc_ref, sem)
    copy.start()
    lane = lanes()
    packs = seams(own_ref, ev_ref, od_ref)
    zonal = Zonal(packs, u_ref, d_ref)
    rows = [{}, {}]
    for j in (0, 1, 2, 13, 14, 15):
        for n in range(2):
            rows[n][j] = swept_ref[6 * n + (j if j < 3 else j - 10)]
    in_step(zonal.seam_walks())
    for at in range(3, 13, 10):
        group = range(at, min(at + 10, 13))
        for j, (t, s) in zip(group, in_step([zonal.row((t_ref, s_ref), j) for j in group])):
            rows[0][j], rows[1][j] = t, s
    wet = [wet_of(depth_row(d_ref, j)) for j in range(J)]
    for n, out in enumerate((t_out, s_out)):
        q = rows[n]
        for at, j in enumerate((0, 1, 2, 3, 4, 11, 12, 13, 14, 15)):
            aux_ref[AUX_TRACER * n + at] = q[j]
        step = [q[j + 1] - q[j] for j in range(J - 1)]
        cell = merid_cell(step, rise_fall(step[0], step[1], step[2])[1], 2)
        before = None
        for j in range(2, 13):
            after = merid_cell(step, cell[2], j + 1)
            flux = merid_flux(load_row(v_ref, j), wet[j] * wet[j + 1], q[j], q[j + 1], cell, after)
            if j == 2:
                aux_ref[AUX_TRACER * n + 10] = flux
            else:
                store_row(out, j, q[j] - (flux - before))
            if j == 12:
                aux_ref[AUX_TRACER * n + 11] = flux
            cell, before = after, flux
    wet_w, wet_e = wet_of(packs[3][1]), wet_of(packs[3][2])
    low = low_half(lane)
    halo_wet = {}

    def mask_row(j):
        halo = unpack(packs[3][0], j)
        yield
        halo = wet_of(halo)
        if j in (0, J - 1):
            halo_wet[j] = halo
        right, left = east(wet[j], halo, lane), west(wet[j], halo, lane)
        yield
        mask_ref[j] = wet[j] * right
        mask_ref[J + j] = wet[j] * left
        if j < J - 1:
            mask_ref[2 * J + j] = wet[j] * wet[j + 1]

    def lap_row(n, packed, load, j, first, last):
        here = load(n, j)
        halo = unpack(packed, j)
        yield
        right, left = east(here, halo, lane), west(here, halo, lane)
        yield
        total = mask_ref[j] * (right - here) - mask_ref[J + j] * (here - left)
        if j > first:
            total = total - mask_ref[2 * J + j - 1] * (here - load(n, j - 1))
        if j < last:
            total = total + mask_ref[2 * J + j] * (load(n, j + 1) - here)
        return total

    def walk(makers):
        for at in range(0, len(makers), 16):
            in_step([m() for m in makers[at : at + 16]])

    walk([functools.partial(mask_row, j) for j in range(J)])
    flows = ((u_ref, packs[2], u_out), (v_ref, packs[4], v_out))

    def inner(n, j):
        lap_ref[J * n + j] = yield from lap_row(n, flows[n][1][0], lambda n, j: load_row(flows[n][0], j), j, 0, J - 1)

    walk([functools.partial(inner, n, j) for j in range(J) for n in range(2)])
    halo_laps = [
        jnp.where(low, seam_lap(pack[1], wet_w), seam_lap(pack[2], wet_e)) for _, pack, _ in flows
    ]
    copy.wait()
    visc = viscosity(visc_ref)

    def outer(n, j):
        total = yield from lap_row(n, halo_laps[n], lambda n, j: lap_ref[J * n + j], j, 1, J - 2)
        base = 2 * AUX_TRACER + AUX_FLOW * n
        if j == 1:
            aux_ref[base + 2] = total
        elif j == J - 2:
            aux_ref[base + 5] = total
        else:
            store_row(flows[n][2], j, load_row(flows[n][0], j) - visc * total)

    walk([functools.partial(outer, n, j) for j in range(1, J - 1) for n in range(2)])
    for n, (_, pack, _) in enumerate(flows):
        base = 2 * AUX_TRACER + AUX_FLOW * n
        aux_ref[base + 0] = lap_ref[J * n]
        aux_ref[base + 1] = lap_ref[J * n + 1]
        aux_ref[base + 3] = lap_ref[J * n + J - 1]
        aux_ref[base + 4] = lap_ref[J * n + J - 2]
        aux_ref[base + 6] = unpack(halo_laps[n], 0)
        aux_ref[base + 7] = unpack(halo_laps[n], J - 1)
        aux_ref[base + 8] = unpack(pack[0], 0)
        aux_ref[base + 9] = unpack(pack[0], J - 1)
    aux_ref[2 * AUX_TRACER + 2 * AUX_FLOW] = halo_wet[0]
    aux_ref[2 * AUX_TRACER + 2 * AUX_FLOW + 1] = halo_wet[J - 1]
    aux_ref[2 * AUX_TRACER + 2 * AUX_FLOW + 2] = visc


def viscosity(visc_ref):
    level = lax.broadcasted_iota(jnp.int32, (K, W), 0)
    visc = jnp.zeros((K, W), F32)
    for k in range(K):
        visc = jnp.where(level == k, visc_ref[k], visc)
    return visc


def finish_side(side, got_ref, u_ref, v_ref, d_ref, aux_ref, outs, finals, sems):
    lane = lanes()
    t_out, s_out, u_out, v_out = outs
    half = pl.ds(8 * (1 - side), 8)
    copies = [
        pltpu.make_async_copy(
            src.reshape(K, J, W).at[:, half], dst.reshape(K, J, W).at[:, half], sems.at[4 * side + n]
        )
        for n, (src, dst) in enumerate(zip(outs, finals))
    ]
    halo_at = 2 * AUX_TRACER + 2 * AUX_FLOW
    visc = aux_ref[halo_at + 2]

    def recv(n):
        return got_ref[2 * n : 2 * n + 2].reshape(K, W)

    faces = (13, 14, 15) if side == 0 else (-1, 0, 1)
    edge, inward, beyond = (15, 14, 16) if side == 0 else (0, 1, -1)
    wet = {j: wet_of(depth_row(d_ref, j)) for j in ((13, 14, 15) if side == 0 else (0, 1, 2))}
    tile = got_ref[SEND_ROWS - 1]
    lane8 = lane[:8]
    inside = (lane8 > 4) & (lane8 < W - 5)
    row = jnp.where(inside[:1], tile[:1], roll(tile, W // 2)[4:5])
    wet[beyond] = wet_of(jnp.broadcast_to(row, (K, W)))
    part = [tile] + [
        jnp.where(lane8 < W // 2, roll(tile, -m), roll(tile, m)) for m in range(1, 5)
    ]
    corner_flow = [jnp.concatenate([part[n], part[n + 2]], axis=0) for n in range(2)]
    corner_wet = wet_of(jnp.concatenate([part[4], part[4]], axis=0))
    courant = {j: recv(8) if j < 0 else load_row(v_ref, j) for j in faces}
    for n, out in enumerate((t_out, s_out)):
        aux = AUX_TRACER * n
        if side == 0:
            q = {11 + m: aux_ref[aux + 5 + m] for m in range(5)}
            q.update({16 + m: recv(3 * n + m) for m in range(3)})
            before = aux_ref[aux + 11]
        else:
            q = {j: aux_ref[aux + j] for j in range(5)}
            q.update({-1 - m: recv(3 * n + m) for m in range(3)})
            before = None
        step = {j: q[j + 1] - q[j] for j in q if j + 1 in q}
        first = faces[0]
        fall = rise_fall(step[first - 2], step[first - 1], step[first])[1]
        cell = merid_cell(step, fall, first)
        for j in faces:
            after = merid_cell(step, cell[2], j + 1)
            flux = merid_flux(courant[j], wet[j] * wet[j + 1], q[j], q[j + 1], cell, after)
            if before is not None:
                store_row(out, j, q[j] - (flux - before))
            cell, before = after, flux
        if side == 1:
            store_row(out, 2, q[2] - (aux_ref[aux + 10] - before))
        copies[n].start()
    halo_wet = aux_ref[halo_at + 1 - side]
    masks = zonal_masks(wet[edge], halo_wet, lane)
    across = wet[edge] * wet[beyond]
    for n, (ref, out) in enumerate(((u_ref, u_out), (v_ref, v_out))):
        base = 2 * AUX_TRACER + AUX_FLOW * n
        at = (3, 4, 5, 7, 9) if side == 0 else (0, 1, 2, 6, 8)
        lap_edge, lap_in, partial, halo_lap, halo_f = (aux_ref[base + a] for a in at)
        f, f_in = load_row(ref, edge), load_row(ref, inward)
        f_out, lap_out = recv(6 + 2 * n), recv(7 + 2 * n)
        step = across * (f_out - f)
        lap_edge = lap_edge + step
        lap_out = lap_out - step
        halo_lap = halo_lap + halo_wet * corner_wet * (corner_flow[n] - halo_f)
        inner_step = wet[edge] * wet[inward] * (lap_in - lap_edge)
        total = (
            zonal_lap(lap_edge, halo_lap, masks, lane)
            + inner_step
            + across * (lap_out - lap_edge)
        )
        store_row(out, edge, f - visc * total)
        store_row(out, inward, f_in - visc * (partial - inner_step))
        copies[2 + n].start()
    return copies


def first_kernel(u_ref, v_ref, d_ref, aux_ref, even_ref, o_ref, *refs):
    fixed = (u_ref, v_ref, d_ref, aux_ref, refs[-5:-1], refs[-9:-5], refs[-1])
    lat = lax.axis_index("lat")
    even = (lat & 1) == 0
    top = lat == lax.axis_size("lat") - 1

    @pl.when(even)
    def _():
        copies = finish_side(0, even_ref, *fixed) + finish_side(1, o_ref, *fixed)
        for copy in copies:
            copy.wait()

    @pl.when(jnp.logical_not(even | top))
    def _():
        for copy in finish_side(0, o_ref, *fixed):
            copy.wait()


def last_kernel(u_ref, v_ref, d_ref, aux_ref, odd_ref, f_ref, o_ref, *refs):
    fixed = (u_ref, v_ref, d_ref, aux_ref, refs[-5:-1], refs[-9:-5], refs[-1])
    lat = lax.axis_index("lat")
    odd = (lat & 1) == 1
    top = lat == lax.axis_size("lat") - 1

    @pl.when(odd & jnp.logical_not(top))
    def _():
        for copy in finish_side(1, odd_ref, *fixed):
            copy.wait()

    low_lon = lax.axis_index("lon") < lax.axis_size("lon") // 2
    for mine, seam_ref in ((low_lon, o_ref), (jnp.logical_not(low_lon), f_ref)):

        @pl.when(top & mine)
        def _(seam_ref=seam_ref):
            copies = finish_side(1, odd_ref, *fixed) + finish_side(0, seam_ref, *fixed)
            for copy in copies:
                copy.wait()


VMEM = pl.BlockSpec(memory_space=pltpu.VMEM)
HBM = pl.BlockSpec(memory_space=pltpu.HBM)
FLAT = (K * J, W)
AUX = 2 * AUX_TRACER + 2 * AUX_FLOW + 3


def call(kernel, in_specs, out_specs, out_shapes, flops, args, scratch=(), aliases=()):
    return pl.pallas_call(
        kernel,
        out_shape=[jax.ShapeDtypeStruct(s, F32) for s in out_shapes],
        in_specs=in_specs,
        out_specs=out_specs,
        scratch_shapes=list(scratch),
        input_output_aliases=dict(aliases),
        cost_estimate=pl.CostEstimate(flops=flops, bytes_accessed=1 << 20, transcendentals=0),
        compiler_params=pltpu.CompilerParams(vmem_limit_bytes=32 << 20),
    )(*args)


def body(t, s, u, v, ind, lay, visc):
    t, s, u, v = (x.reshape(FLAT) for x in (t, s, u, v))
    n_lon, n_lat = lax.axis_size("lon"), lax.axis_size("lat")
    t, s, u, v, depth, own, ev, od = call(
        pack_kernel,
        [HBM] * 6,
        [VMEM] * 8,
        [FLAT] * 4 + [(J, W), (K, 5 * W), (K, 3 * W), (K, 3 * W)],
        1 << 20,
        [pltpu.with_memory_space_constraint(x, pltpu.HBM) for x in (t, s, u, v, ind, lay)],
        [pltpu.VMEM((J, W), jnp.int32)] * 2 + [pltpu.SemaphoreType.DMA((6,))],
    )
    od = lax.ppermute(od, "lon", [(i, (((i + 1) ^ 1) - 1) % n_lon) for i in range(n_lon)])
    ev = lax.all_gather(
        ev, "lon", axis_index_groups=[[i, i + 1] for i in range(0, n_lon, 2)], tiled=True
    )
    swept, edge_e, edge_o = call(
        edge_kernel,
        [VMEM] * 8,
        [VMEM] * 3,
        [(12, K, W), (SEND_ROWS, 8, W), (SEND_ROWS, 8, W)],
        1 << 20,
        (t, s, u, v, depth, own, ev, od),
    )
    to_even, to_odd, pairs_o, pairs_f = [], [], [], []
    top = n_lat - 1
    for p in range(n_lon):
        for l in range(n_lat):
            (to_even if l & 1 else to_odd).append((p * n_lat + l, p * n_lat + (l ^ 1)))
            if 0 < l < top:
                pairs_o.append((p * n_lat + l, p * n_lat + ((l + 1) ^ 1) - 1))
        across = (p * n_lat + top, (n_lon - 1 - p) * n_lat + top)
        (pairs_f if p < n_lon // 2 else pairs_o).append(across)
    got_even = lax.ppermute(edge_e, ("lon", "lat"), to_even)
    got_o = lax.ppermute(edge_o, ("lon", "lat"), pairs_o)
    got_odd = lax.ppermute(edge_e, ("lon", "lat"), to_odd)
    got_f = lax.ppermute(edge_o, ("lon", "lat"), pairs_f)
    *parts, aux = call(
        inner_kernel,
        [VMEM] * 5 + [HBM] + [VMEM] * 4,
        [VMEM] * 5,
        [FLAT] * 4 + [(AUX, K, W)],
        1 << 24,
        (t, s, u, v, depth, pltpu.with_memory_space_constraint(visc, pltpu.HBM), own, ev, od, swept),
        [
            pltpu.SMEM((K,), F32),
            pltpu.SemaphoreType.DMA,
            pltpu.VMEM((3 * J, K, W), F32),
            pltpu.VMEM((2 * J, K, W), F32),
        ],
    )
    flow = (u, v, depth, aux)
    outs = call(
        first_kernel,
        [VMEM] * 10,
        [HBM] * 4 + [VMEM] * 4,
        [FLAT] * 8,
        1 << 21,
        (*flow, got_even, got_o, *parts),
        [pltpu.SemaphoreType.DMA((8,))],
        {6 + n: 4 + n for n in range(4)},
    )
    outs = call(
        last_kernel,
        [VMEM] * 7 + [HBM] * 4 + [VMEM] * 4,
        [HBM] * 4 + [VMEM] * 4,
        [FLAT] * 8,
        1 << 21,
        (*flow, got_odd, got_f, got_o, *outs),
        [pltpu.SemaphoreType.DMA((8,))],
        {7 + n: n for n in range(8)},
    )
    return tuple(x.reshape(K, J, W) for x in outs[:4])


def solution(mesh):
    field, flat = P(None, "lat", "lon"), P("lat", "lon")
    return jax.shard_map(
        body,
        mesh=mesh,
        in_specs=(field, field, field, field, flat, flat, P()),
        out_specs=(field,) * 4,
        check_vma=False,
    )
```

```python
import functools

import jax
import jax.numpy as jnp
from jax import lax
from jax.experimental import pallas as pl
from jax.experimental.pallas import tpu as pltpu
from jax.sharding import PartitionSpec as P

K, J, W = 16, 16, 128
WIN = 6
PHASE = (0, 3, 0, 3, 0)
SEND_ROWS = 21
F32 = jnp.float32


def lanes():
    return lax.broadcasted_iota(jnp.int32, (K, W), 1)


def levels():
    return lax.broadcasted_iota(jnp.int32, (K, W), 0).astype(F32)


def low_half(lane):
    return lane - WIN * ((lane * 43) >> 8) < WIN // 2


def roll(x, shift):
    shift %= W
    return x if shift == 0 else pltpu.roll(x, shift, 1)


def load_row(ref, j):
    return ref[pl.ds(j, K, stride=J), :]


def store_row(ref, j, value):
    ref[pl.ds(j, K, stride=J), :] = value


def depth_row(depth_ref, j):
    return jnp.broadcast_to(depth_ref[pl.ds(j, 1), :], (K, W))


def wet_of(depth):
    return jnp.where(levels() < depth, 1.0, 0.0).astype(F32)


def unpack(packed, j):
    return roll(packed, -(WIN * j + 3))


def east(x, halo, lane):
    return roll(jnp.where(lane < 1, halo, x), -1)


def west(x, halo, lane):
    return roll(jnp.where(lane == W - 1, halo, x), 1)


def minmod(a, b):
    return jnp.maximum(jnp.minimum(a, jnp.maximum(b, 0.0)), jnp.minimum(b, 0.0))


def rise_fall(before, here, after):
    rise = minmod(0.5 * here + (1.0 / 12.0) * (before - after), here)
    return rise, here - rise


def limited(fall, rise):
    return minmod(fall, rise + rise), minmod(rise, fall + fall)


def weights(c):
    size = jnp.abs(c)
    rest = 1.0 - size
    return size * rest, rest * rest


def pack_columns(rows, phase):
    lane = lanes()
    packed = jnp.zeros((K, W), F32)
    moved = [roll(row, WIN * j + phase + 3) for j, row in enumerate(rows)]
    for j, row in enumerate(moved):
        first = WIN * j + phase
        packed = jnp.where((lane >= first) & (lane < first + WIN), row, packed)
    return packed


def pack_kernel(*refs):
    sources, (t_ref, s_ref, u_ref, v_ref, d_ref, own_ref, ev_ref, od_ref) = refs[:6], refs[6:14]
    ind_ref, lay_ref, sems = refs[14:]
    copies = [
        pltpu.make_async_copy(src, dst, sems.at[n])
        for n, (src, dst) in enumerate(zip(sources, (t_ref, s_ref, u_ref, v_ref, ind_ref, lay_ref)))
    ]
    for n in (4, 5, 0, 1, 2, 3):
        copies[n].start()
    copies[4].wait()
    copies[5].wait()
    d_ref[...] = (ind_ref[...] * lay_ref[...]).astype(F32)
    d = pack_columns([depth_row(d_ref, j) for j in range(J)], 3)
    fields = []
    for n, ref in enumerate((t_ref, s_ref, u_ref, v_ref)):
        copies[n].wait()
        fields.append(pack_columns([load_row(ref, j) for j in range(J)], 3 if n == 1 else 0))
    fields.insert(3, d)
    for n, x in enumerate(fields):
        own_ref[:, n * W : (n + 1) * W] = x
    t, s, u, d, v = fields
    low = low_half(lanes())
    even = (lax.axis_index("lon") & 1) == 0
    for n, (a, b) in enumerate(((t, s), (u, d), (v, v))):
        to_east = jnp.where(low, a, b)
        to_west = jnp.where(low, b, a)
        at = slice(n * W, (n + 1) * W)
        ev_ref[:, at] = jnp.where(even, to_east, to_west)
        od_ref[:, at] = jnp.where(even, to_west, to_east)


def arrived(ev_ref, od_ref, n):
    even = (lax.axis_index("lon") & 1) == 0
    mate = pl.multiple_of(jnp.where(even, K, 0), K)
    at = slice((n // 2) * W, (n // 2 + 1) * W)
    ev = ev_ref[pl.ds(mate, K), at]
    od = od_ref[:, at]
    return jnp.where(even, od, ev), jnp.where(even, ev, od)


def seams(own_ref, ev_ref, od_ref):
    low = low_half(lanes())
    out = []
    for n in range(5):
        from_west, from_east = arrived(ev_ref, od_ref, n)
        own = own_ref[:, n * W : (n + 1) * W]
        if PHASE[n]:
            from_west, from_east, own = (roll(x, -3) for x in (from_west, from_east, own))
        out.append(
            (
                jnp.where(low, from_west, from_east),
                jnp.where(low, from_west, own),
                jnp.where(low, own, from_east),
            )
        )
    return out


def in_step(walks):
    out = [None] * len(walks)
    live = list(range(len(walks)))
    while live:
        for n in tuple(live):
            try:
                next(walks[n])
            except StopIteration as end:
                out[n] = end.value
                live.remove(n)
    return out


class Zonal:
    def __init__(self, packs, u_ref, d_ref):
        self.packs, self.u_ref, self.d_ref = packs, u_ref, d_ref
        self.flux = {}
        self.fall = {}

    def seam_walks(self):
        return [self.seam(n, side) for n in range(2) for side in (1, 2)]

    def seam(self, n, side):
        q, c, wet = self.packs[n][side], self.packs[2][side], wet_of(self.packs[3][side])
        q_next, c_west, wet_next = roll(q, -1), roll(c, 1), roll(wet, -1)
        yield
        step = q_next - q
        before, after = roll(step, 1), roll(step, -1)
        yield
        rise, fall = rise_fall(before, step, after)
        fall_before = roll(fall, 1)
        yield
        down, up = limited(fall_before, rise)
        near, far = weights(c_west)
        from_right = roll(q - (near * up + far * down), -1)
        yield
        near, far = weights(c)
        self.flux[n, side] = c * wet * wet_next * jnp.where(
            c > 0.0, q + (near * down + far * up), from_right
        )
        self.fall[n, side] = fall_before

    def fixes(self, n):
        lane = lanes()
        third = lane - WIN * ((lane * 43) >> 8) == 2
        return jnp.where(third, self.flux[n, 2], self.fall[n, 1]), self.flux[n, 1]

    def row(self, refs, j):
        lane = lanes()
        last = lane == W - 1
        u = load_row(self.u_ref, j)
        wet = wet_of(depth_row(self.d_ref, j))
        halo_wet = unpack(self.packs[3][0], j)
        halo_u = unpack(self.packs[2][0], j)
        halos = [unpack(self.packs[n][0], j) for n in range(2)]
        q = [load_row(ref, j) for ref in refs]
        yield
        halo_wet = wet_of(halo_wet)
        right = [east(q[n], halos[n], lane) for n in range(2)]
        left = [west(q[n], halos[n], lane) for n in range(2)]
        beyond = [roll(jnp.where(lane < 2, halos[n], q[n]), -2) for n in range(2)]
        u_west = west(u, halo_u, lane)
        wet_east = east(wet, halo_wet, lane)
        yield
        edges = [rise_fall(q[n] - left[n], right[n] - q[n], beyond[n] - right[n]) for n in range(2)]
        falls = [roll(edges[n][1], 1) for n in range(2)]
        yield
        near, far = weights(u)
        near_w, far_w = weights(u_west)
        face = u * wet * wet_east
        while (1, 2) not in self.flux:
            yield
        fixes = [[unpack(x, j) for x in self.fixes(n)] for n in range(2)]
        yield
        forward = u > 0.0
        cells = [
            limited(jnp.where(lane == 0, fixes[n][0], falls[n]), edges[n][0]) for n in range(2)
        ]
        from_right = [roll(q[n] - (near_w * cells[n][1] + far_w * cells[n][0]), -1) for n in range(2)]
        yield
        flux = [
            face * jnp.where(forward, q[n] + (near * cells[n][0] + far * cells[n][1]), from_right[n])
            for n in range(2)
        ]
        before = [roll(jnp.where(last, fixes[n][1], flux[n]), 1) for n in range(2)]
        yield
        return [q[n] - (jnp.where(last, fixes[n][0], flux[n]) - before[n]) for n in range(2)]


def zonal_masks(wet, halo_wet, lane):
    return wet * east(wet, halo_wet, lane), wet * west(wet, halo_wet, lane)


def zonal_lap(f, halo, masks, lane):
    return masks[0] * (east(f, halo, lane) - f) - masks[1] * (f - west(f, halo, lane))


def seam_lap(f, wet):
    total = None
    for shift in (1, -1, WIN, -WIN):
        term = wet * roll(wet, shift) * (roll(f, shift) - f)
        total = term if total is None else total + term
    return total


def edge_kernel(
    t_ref, s_ref, u_ref, v_ref, d_ref, own_ref, ev_ref, od_ref, swept_ref, e_ref, o_ref, a_ref, f_ref
):
    lane = lanes()
    lane8, sub8 = lane[:8], lax.broadcasted_iota(jnp.int32, (8, W), 0)
    packs = seams(own_ref, ev_ref, od_ref)
    zonal = Zonal(packs, u_ref, d_ref)
    packs = [p[0] for p in packs]
    wet = {j: wet_of(depth_row(d_ref, j)) for j in (0, 1, 2, 13, 14, 15)}
    all_rows = (15, 14, 13, 0, 1, 2)

    def partial_lap(ref, pack, j, inward):
        f = load_row(ref, j)
        halo, dry = unpack(pack, j), unpack(packs[3], j)
        yield
        right, left = east(f, halo, lane), west(f, halo, lane)
        dry = wet_of(dry)
        wet_r, wet_l = east(wet[j], dry, lane), west(wet[j], dry, lane)
        yield
        return wet[j] * (
            wet_r * (right - f)
            + wet_l * (left - f)
            + wet[inward] * (load_row(ref, inward) - f)
        )

    def corner_tile(j):
        depth = depth_row(d_ref, j)[:8]
        far = roll(depth, W // 2)
        parts = []
        for at, (pack, top) in enumerate(
            ((packs[2], 0), (packs[4], 0), (packs[2], 8), (packs[4], 8), (packs[3], 0))
        ):
            home = -(WIN * j + 3)
            part = pack[top : top + 8]
            parts += [(at, roll(part, home + at)), (W - 1 - at, roll(part, home - at))]
        yield
        corner = jnp.where(sub8 < 4, depth, far)
        for at, part in parts:
            corner = jnp.where(lane8 == at, part, corner)
        return corner

    sides = ((J - 1, J - 2), (0, 1))
    flows = ((u_ref, packs[2]), (v_ref, packs[4]))
    seam_walks = zonal.seam_walks()
    done = in_step(
        seam_walks
        + [zonal.row((t_ref, s_ref), j) for j in all_rows]
        + [partial_lap(*flow, *rows) for rows in sides for flow in flows]
        + [corner_tile(rows[0]) for rows in sides]
    )[len(seam_walks) :]
    halves = []
    for side, (edge, _) in enumerate(sides):
        planes = done[3 * side : 3 * side + 3]
        for j, (t, s) in zip(all_rows[3 * side : 3 * side + 3], planes):
            swept_ref[j if j < 3 else j - 10] = t
            swept_ref[6 + (j if j < 3 else j - 10)] = s
        half = [p[0] for p in planes] + [p[1] for p in planes]
        for n, (ref, _) in enumerate(flows):
            half += [load_row(ref, edge), done[6 + 2 * side + n]]
        halves.append((half, done[10 + side]))
    lat = lax.axis_index("lat")
    even = (lat & 1) == 0
    (north, north_c), (south, south_c) = halves
    for n, (a, b) in enumerate(zip(north, south)):
        e_ref[2 * n : 2 * n + 2] = jnp.where(even, a, b).reshape(2, 8, W)
        o_ref[2 * n : 2 * n + 2] = jnp.where(even, b, a).reshape(2, 8, W)
    e_ref[SEND_ROWS - 1] = jnp.where(even, north_c, south_c)
    o_ref[SEND_ROWS - 1] = jnp.where(even, south_c, north_c)

    @pl.when(lat == lax.axis_size("lat") - 1)
    def _():
        for n in range(SEND_ROWS):
            x = jnp.take_along_axis(o_ref[n], W - 1 - lane8, axis=1)
            if 12 <= n < 20:
                x = -x
            elif n == 20:
                x = jnp.where((lane8 < 4) | (lane8 > W - 5), -x, x)
            o_ref[n] = x

    late = (lat == lax.axis_size("lat") - 1) & seam_first()

    @pl.when(late)
    def _():
        a_ref[...] = o_ref[...]
        f_ref[...] = e_ref[...]

    @pl.when(jnp.logical_not(late))
    def _():
        a_ref[...] = e_ref[...]
        f_ref[...] = o_ref[...]


def low_longitude():
    return lax.axis_index("lon") < lax.axis_size("lon") // 2


def seam_first():
    return jnp.logical_not(low_longitude()) & (lax.axis_index("lon") < lax.axis_size("lon") - 1)


def merid_cell(step, fall_before, j):
    rise, fall = rise_fall(step[j - 1], step[j], step[j + 1])
    down, up = limited(fall_before, rise)
    return down, up, fall


def merid_flux(c, wet_pair, q, q_next, cell, cell_next):
    forward = c > 0.0
    rest = 1.0 - jnp.abs(c)
    square = rest * rest
    near = jnp.where(forward, cell[0], cell_next[1])
    far = jnp.where(forward, cell[1], cell_next[0])
    return c * wet_pair * (
        jnp.where(forward, q, q_next) + (c * rest * near + jnp.where(forward, square, -square) * far)
    )


AUX_TRACER, AUX_FLOW = 12, 10


def inner_kernel(
    t_ref,
    s_ref,
    u_ref,
    v_ref,
    d_ref,
    visc_hbm,
    own_ref,
    ev_ref,
    od_ref,
    swept_ref,
    t_out,
    s_out,
    u_out,
    v_out,
    aux_ref,
    visc_ref,
    sem,
    mask_ref,
    lap_ref,
):
    copy = pltpu.make_async_copy(visc_hbm, visc_ref, sem)
    copy.start()
    lane = lanes()
    packs = seams(own_ref, ev_ref, od_ref)
    zonal = Zonal(packs, u_ref, d_ref)
    rows = [{}, {}]
    for j in (0, 1, 2, 13, 14, 15):
        for n in range(2):
            rows[n][j] = swept_ref[6 * n + (j if j < 3 else j - 10)]
    in_step(zonal.seam_walks())
    for at in range(3, 13, 10):
        group = range(at, min(at + 10, 13))
        for j, (t, s) in zip(group, in_step([zonal.row((t_ref, s_ref), j) for j in group])):
            rows[0][j], rows[1][j] = t, s
    wet = [wet_of(depth_row(d_ref, j)) for j in range(J)]
    for n, out in enumerate((t_out, s_out)):
        q = rows[n]
        for at, j in enumerate((0, 1, 2, 3, 4, 11, 12, 13, 14, 15)):
            aux_ref[AUX_TRACER * n + at] = q[j]
        step = [q[j + 1] - q[j] for j in range(J - 1)]
        cell = merid_cell(step, rise_fall(step[0], step[1], step[2])[1], 2)
        before = None
        for j in range(2, 13):
            after = merid_cell(step, cell[2], j + 1)
            flux = merid_flux(load_row(v_ref, j), wet[j] * wet[j + 1], q[j], q[j + 1], cell, after)
            if j == 2:
                aux_ref[AUX_TRACER * n + 10] = flux
            else:
                store_row(out, j, q[j] - (flux - before))
            if j == 12:
                aux_ref[AUX_TRACER * n + 11] = flux
            cell, before = after, flux
    wet_w, wet_e = wet_of(packs[3][1]), wet_of(packs[3][2])
    low = low_half(lane)
    halo_wet = {}

    def mask_row(j):
        halo = unpack(packs[3][0], j)
        yield
        halo = wet_of(halo)
        if j in (0, J - 1):
            halo_wet[j] = halo
        right, left = east(wet[j], halo, lane), west(wet[j], halo, lane)
        yield
        mask_ref[j] = wet[j] * right
        mask_ref[J + j] = wet[j] * left
        if j < J - 1:
            mask_ref[2 * J + j] = wet[j] * wet[j + 1]

    def lap_row(n, packed, load, j, first, last):
        here = load(n, j)
        halo = unpack(packed, j)
        yield
        right, left = east(here, halo, lane), west(here, halo, lane)
        yield
        total = mask_ref[j] * (right - here) - mask_ref[J + j] * (here - left)
        if j > first:
            total = total - mask_ref[2 * J + j - 1] * (here - load(n, j - 1))
        if j < last:
            total = total + mask_ref[2 * J + j] * (load(n, j + 1) - here)
        return total

    def walk(makers):
        for at in range(0, len(makers), 16):
            in_step([m() for m in makers[at : at + 16]])

    walk([functools.partial(mask_row, j) for j in range(J)])
    flows = ((u_ref, packs[2], u_out), (v_ref, packs[4], v_out))

    def inner(n, j):
        lap_ref[J * n + j] = yield from lap_row(n, flows[n][1][0], lambda n, j: load_row(flows[n][0], j), j, 0, J - 1)

    walk([functools.partial(inner, n, j) for j in range(J) for n in range(2)])
    halo_laps = [
        jnp.where(low, seam_lap(pack[1], wet_w), seam_lap(pack[2], wet_e)) for _, pack, _ in flows
    ]
    copy.wait()
    visc = viscosity(visc_ref)

    def outer(n, j):
        total = yield from lap_row(n, halo_laps[n], lambda n, j: lap_ref[J * n + j], j, 1, J - 2)
        base = 2 * AUX_TRACER + AUX_FLOW * n
        if j == 1:
            aux_ref[base + 2] = total
        elif j == J - 2:
            aux_ref[base + 5] = total
        else:
            store_row(flows[n][2], j, load_row(flows[n][0], j) - visc * total)

    walk([functools.partial(outer, n, j) for j in range(1, J - 1) for n in range(2)])
    for n, (_, pack, _) in enumerate(flows):
        base = 2 * AUX_TRACER + AUX_FLOW * n
        aux_ref[base + 0] = lap_ref[J * n]
        aux_ref[base + 1] = lap_ref[J * n + 1]
        aux_ref[base + 3] = lap_ref[J * n + J - 1]
        aux_ref[base + 4] = lap_ref[J * n + J - 2]
        aux_ref[base + 6] = unpack(halo_laps[n], 0)
        aux_ref[base + 7] = unpack(halo_laps[n], J - 1)
        aux_ref[base + 8] = unpack(pack[0], 0)
        aux_ref[base + 9] = unpack(pack[0], J - 1)
    aux_ref[2 * AUX_TRACER + 2 * AUX_FLOW] = halo_wet[0]
    aux_ref[2 * AUX_TRACER + 2 * AUX_FLOW + 1] = halo_wet[J - 1]
    aux_ref[2 * AUX_TRACER + 2 * AUX_FLOW + 2] = visc


def viscosity(visc_ref):
    level = lax.broadcasted_iota(jnp.int32, (K, W), 0)
    visc = jnp.zeros((K, W), F32)
    for k in range(K):
        visc = jnp.where(level == k, visc_ref[k], visc)
    return visc


def finish_side(side, got_ref, u_ref, v_ref, d_ref, aux_ref, outs, finals, sems):
    lane = lanes()
    t_out, s_out, u_out, v_out = outs
    half = pl.ds(8 * (1 - side), 8)
    copies = [
        pltpu.make_async_copy(
            src.reshape(K, J, W).at[:, half], dst.reshape(K, J, W).at[:, half], sems.at[4 * side + n]
        )
        for n, (src, dst) in enumerate(zip(outs, finals))
    ]
    halo_at = 2 * AUX_TRACER + 2 * AUX_FLOW
    visc = aux_ref[halo_at + 2]

    def recv(n):
        return got_ref[2 * n : 2 * n + 2].reshape(K, W)

    faces = (13, 14, 15) if side == 0 else (-1, 0, 1)
    edge, inward, beyond = (15, 14, 16) if side == 0 else (0, 1, -1)
    wet = {j: wet_of(depth_row(d_ref, j)) for j in ((13, 14, 15) if side == 0 else (0, 1, 2))}
    tile = got_ref[SEND_ROWS - 1]
    lane8 = lane[:8]
    inside = (lane8 > 4) & (lane8 < W - 5)
    row = jnp.where(inside[:1], tile[:1], roll(tile, W // 2)[4:5])
    wet[beyond] = wet_of(jnp.broadcast_to(row, (K, W)))
    part = [tile] + [
        jnp.where(lane8 < W // 2, roll(tile, -m), roll(tile, m)) for m in range(1, 5)
    ]
    corner_flow = [jnp.concatenate([part[n], part[n + 2]], axis=0) for n in range(2)]
    corner_wet = wet_of(jnp.concatenate([part[4], part[4]], axis=0))
    courant = {j: recv(8) if j < 0 else load_row(v_ref, j) for j in faces}
    for n, out in enumerate((t_out, s_out)):
        aux = AUX_TRACER * n
        if side == 0:
            q = {11 + m: aux_ref[aux + 5 + m] for m in range(5)}
            q.update({16 + m: recv(3 * n + m) for m in range(3)})
            before = aux_ref[aux + 11]
        else:
            q = {j: aux_ref[aux + j] for j in range(5)}
            q.update({-1 - m: recv(3 * n + m) for m in range(3)})
            before = None
        step = {j: q[j + 1] - q[j] for j in q if j + 1 in q}
        first = faces[0]
        fall = rise_fall(step[first - 2], step[first - 1], step[first])[1]
        cell = merid_cell(step, fall, first)
        for j in faces:
            after = merid_cell(step, cell[2], j + 1)
            flux = merid_flux(courant[j], wet[j] * wet[j + 1], q[j], q[j + 1], cell, after)
            if before is not None:
                store_row(out, j, q[j] - (flux - before))
            cell, before = after, flux
        if side == 1:
            store_row(out, 2, q[2] - (aux_ref[aux + 10] - before))
        copies[n].start()
    halo_wet = aux_ref[halo_at + 1 - side]
    masks = zonal_masks(wet[edge], halo_wet, lane)
    across = wet[edge] * wet[beyond]
    for n, (ref, out) in enumerate(((u_ref, u_out), (v_ref, v_out))):
        base = 2 * AUX_TRACER + AUX_FLOW * n
        at = (3, 4, 5, 7, 9) if side == 0 else (0, 1, 2, 6, 8)
        lap_edge, lap_in, partial, halo_lap, halo_f = (aux_ref[base + a] for a in at)
        f, f_in = load_row(ref, edge), load_row(ref, inward)
        f_out, lap_out = recv(6 + 2 * n), recv(7 + 2 * n)
        step = across * (f_out - f)
        lap_edge = lap_edge + step
        lap_out = lap_out - step
        halo_lap = halo_lap + halo_wet * corner_wet * (corner_flow[n] - halo_f)
        inner_step = wet[edge] * wet[inward] * (lap_in - lap_edge)
        total = (
            zonal_lap(lap_edge, halo_lap, masks, lane)
            + inner_step
            + across * (lap_out - lap_edge)
        )
        store_row(out, edge, f - visc * total)
        store_row(out, inward, f_in - visc * (partial - inner_step))
        copies[2 + n].start()
    return copies


def at_once(copies):
    for copy in copies:
        copy.wait()


def first_kernel(u_ref, v_ref, d_ref, aux_ref, even_ref, o_ref, *refs):
    fixed = (u_ref, v_ref, d_ref, aux_ref, refs[-5:-1], refs[-9:-5], refs[-1])
    lat = lax.axis_index("lat")
    top = lax.axis_size("lat") - 1
    even = (lat & 1) == 0
    late = (lat == top - 1) & seam_first()

    @pl.when(even & jnp.logical_not(late))
    def _():
        at_once(finish_side(0, even_ref, *fixed) + finish_side(1, o_ref, *fixed))

    @pl.when(late)
    def _():
        at_once(finish_side(1, o_ref, *fixed))

    @pl.when(jnp.logical_not(even | (lat == top)))
    def _():
        at_once(finish_side(0, o_ref, *fixed))


def last_kernel(u_ref, v_ref, d_ref, aux_ref, odd_ref, f_ref, even_ref, o_ref, *refs):
    fixed = (u_ref, v_ref, d_ref, aux_ref, refs[-5:-1], refs[-9:-5], refs[-1])
    lat = lax.axis_index("lat")
    top = lax.axis_size("lat") - 1
    low = low_longitude()
    high = jnp.logical_not(low)

    @pl.when(((lat & 1) == 1) & (lat != top))
    def _():
        at_once(finish_side(1, odd_ref, *fixed))

    first = lax.axis_index("lon") == 0

    @pl.when((lat == top) & low & jnp.logical_not(first))
    def _():
        at_once(finish_side(1, odd_ref, *fixed) + finish_side(0, even_ref, *fixed))

    @pl.when((lat == top) & first)
    def _():
        at_once(finish_side(1, odd_ref, *fixed) + finish_side(0, o_ref, *fixed))

    @pl.when((lat == top) & high)
    def _():
        at_once(finish_side(1, odd_ref, *fixed) + finish_side(0, f_ref, *fixed))

    @pl.when((lat == top - 1) & seam_first())
    def _():
        at_once(finish_side(0, f_ref, *fixed))


VMEM = pl.BlockSpec(memory_space=pltpu.VMEM)
HBM = pl.BlockSpec(memory_space=pltpu.HBM)
FLAT = (K * J, W)
AUX = 2 * AUX_TRACER + 2 * AUX_FLOW + 3


def call(kernel, in_specs, out_specs, out_shapes, flops, args, scratch=(), aliases=()):
    return pl.pallas_call(
        kernel,
        out_shape=[jax.ShapeDtypeStruct(s, F32) for s in out_shapes],
        in_specs=in_specs,
        out_specs=out_specs,
        scratch_shapes=list(scratch),
        input_output_aliases=dict(aliases),
        cost_estimate=pl.CostEstimate(flops=flops, bytes_accessed=1 << 20, transcendentals=0),
        compiler_params=pltpu.CompilerParams(vmem_limit_bytes=32 << 20),
    )(*args)


def body(t, s, u, v, ind, lay, visc):
    t, s, u, v = (x.reshape(FLAT) for x in (t, s, u, v))
    n_lon, n_lat = lax.axis_size("lon"), lax.axis_size("lat")
    t, s, u, v, depth, own, ev, od = call(
        pack_kernel,
        [HBM] * 6,
        [VMEM] * 8,
        [FLAT] * 4 + [(J, W), (K, 5 * W), (K, 3 * W), (K, 3 * W)],
        1 << 20,
        [pltpu.with_memory_space_constraint(x, pltpu.HBM) for x in (t, s, u, v, ind, lay)],
        [pltpu.VMEM((J, W), jnp.int32)] * 2 + [pltpu.SemaphoreType.DMA((6,))],
    )
    od = lax.ppermute(od, "lon", [(i, (((i + 1) ^ 1) - 1) % n_lon) for i in range(n_lon)])
    ev = lax.all_gather(
        ev, "lon", axis_index_groups=[[i, i + 1] for i in range(0, n_lon, 2)], tiled=True
    )
    swept, edge_e, edge_o, edge_a, edge_f = call(
        edge_kernel,
        [VMEM] * 8,
        [VMEM] * 5,
        [(12, K, W)] + [(SEND_ROWS, 8, W)] * 4,
        1 << 20,
        (t, s, u, v, depth, own, ev, od),
    )
    to_even, to_odd, pairs_o, last = [], [], [], []
    top = n_lat - 1
    for p in range(n_lon):
        low = p < n_lon // 2
        ahead = not low and p < n_lon - 1
        for l in range(n_lat):
            pair = (p * n_lat + l, p * n_lat + (l ^ 1))
            if l & 1:
                (last if ahead and l == top else to_even).append(pair)
            else:
                to_odd.append(pair)
            if 0 < l < top:
                pairs_o.append((p * n_lat + l, p * n_lat + ((l + 1) ^ 1) - 1))
        across = (p * n_lat + top, (n_lon - 1 - p) * n_lat + top)
        (last if low else to_even if ahead else pairs_o).append(across)
    got_even = lax.ppermute(edge_a, ("lon", "lat"), to_even)
    got_o = lax.ppermute(edge_o, ("lon", "lat"), pairs_o)
    got_odd = lax.ppermute(edge_e, ("lon", "lat"), to_odd)
    got_f = lax.ppermute(edge_f, ("lon", "lat"), last)
    *parts, aux = call(
        inner_kernel,
        [VMEM] * 5 + [HBM] + [VMEM] * 4,
        [VMEM] * 5,
        [FLAT] * 4 + [(AUX, K, W)],
        1 << 24,
        (t, s, u, v, depth, pltpu.with_memory_space_constraint(visc, pltpu.HBM), own, ev, od, swept),
        [
            pltpu.SMEM((K,), F32),
            pltpu.SemaphoreType.DMA,
            pltpu.VMEM((3 * J, K, W), F32),
            pltpu.VMEM((2 * J, K, W), F32),
        ],
    )
    flow = (u, v, depth, aux)
    outs = call(
        first_kernel,
        [VMEM] * 10,
        [HBM] * 4 + [VMEM] * 4,
        [FLAT] * 8,
        1 << 21,
        (*flow, got_even, got_o, *parts),
        [pltpu.SemaphoreType.DMA((8,))],
        {6 + n: 4 + n for n in range(4)},
    )
    outs = call(
        last_kernel,
        [VMEM] * 8 + [HBM] * 4 + [VMEM] * 4,
        [HBM] * 4 + [VMEM] * 4,
        [FLAT] * 8,
        1 << 21,
        (*flow, got_odd, got_f, got_even, got_o, *outs),
        [pltpu.SemaphoreType.DMA((8,))],
        {8 + n: n for n in range(8)},
    )
    return tuple(x.reshape(K, J, W) for x in outs[:4])


def solution(mesh):
    field, flat = P(None, "lat", "lon"), P("lat", "lon")
    return jax.shard_map(
        body,
        mesh=mesh,
        in_specs=(field, field, field, field, flat, flat, P()),
        out_specs=(field,) * 4,
        check_vma=False,
    )
```

```python
import functools

import jax
import jax.numpy as jnp
from jax import lax
from jax.experimental import pallas as pl
from jax.experimental.pallas import tpu as pltpu
from jax.sharding import PartitionSpec as P

K, J, W = 16, 16, 128
WIN = 6
PHASE = (0, 3, 0, 3, 0)
SEND_ROWS = 21
F32 = jnp.float32


def lanes():
    return lax.broadcasted_iota(jnp.int32, (K, W), 1)


def levels():
    return lax.broadcasted_iota(jnp.int32, (K, W), 0).astype(F32)


def low_half(lane):
    return lane - WIN * ((lane * 43) >> 8) < WIN // 2


def roll(x, shift):
    shift %= W
    return x if shift == 0 else pltpu.roll(x, shift, 1)


def load_row(ref, j):
    return ref[pl.ds(j, K, stride=J), :]


def store_row(ref, j, value):
    ref[pl.ds(j, K, stride=J), :] = value


def depth_row(depth_ref, j):
    return jnp.broadcast_to(depth_ref[pl.ds(j, 1), :], (K, W))


def wet_of(depth):
    return jnp.where(levels() < depth, 1.0, 0.0).astype(F32)


def unpack(packed, j):
    return roll(packed, -(WIN * j + 3))


def east(x, halo, lane):
    return roll(jnp.where(lane < 1, halo, x), -1)


def west(x, halo, lane):
    return roll(jnp.where(lane == W - 1, halo, x), 1)


def minmod(a, b):
    return jnp.maximum(jnp.minimum(a, jnp.maximum(b, 0.0)), jnp.minimum(b, 0.0))


def rise_fall(before, here, after):
    rise = minmod(0.5 * here + (1.0 / 12.0) * (before - after), here)
    return rise, here - rise


def limited(fall, rise):
    return minmod(fall, rise + rise), minmod(rise, fall + fall)


def weights(c):
    size = jnp.abs(c)
    rest = 1.0 - size
    return size * rest, rest * rest


def pack_columns(rows, phase):
    lane = lanes()
    packed = jnp.zeros((K, W), F32)
    moved = [roll(row, WIN * j + phase + 3) for j, row in enumerate(rows)]
    for j, row in enumerate(moved):
        first = WIN * j + phase
        packed = jnp.where((lane >= first) & (lane < first + WIN), row, packed)
    return packed


def pack_kernel(*refs):
    sources, (t_ref, s_ref, u_ref, v_ref, d_ref, own_ref, ev_ref, od_ref) = refs[:6], refs[6:14]
    ind_ref, lay_ref, sems = refs[14:]
    copies = [
        pltpu.make_async_copy(src, dst, sems.at[n])
        for n, (src, dst) in enumerate(zip(sources, (t_ref, s_ref, u_ref, v_ref, ind_ref, lay_ref)))
    ]
    for n in (4, 5, 0, 1, 2, 3):
        copies[n].start()
    copies[4].wait()
    copies[5].wait()
    d_ref[...] = (ind_ref[...] * lay_ref[...]).astype(F32)
    d = pack_columns([depth_row(d_ref, j) for j in range(J)], 3)
    fields = []
    for n, ref in enumerate((t_ref, s_ref, u_ref, v_ref)):
        copies[n].wait()
        fields.append(pack_columns([load_row(ref, j) for j in range(J)], 3 if n == 1 else 0))
    fields.insert(3, d)
    for n, x in enumerate(fields):
        own_ref[:, n * W : (n + 1) * W] = x
    t, s, u, d, v = fields
    low = low_half(lanes())
    even = (lax.axis_index("lon") & 1) == 0
    for n, (a, b) in enumerate(((t, s), (u, d), (v, v))):
        to_east = jnp.where(low, a, b)
        to_west = jnp.where(low, b, a)
        at = slice(n * W, (n + 1) * W)
        ev_ref[:, at] = jnp.where(even, to_east, to_west)
        od_ref[:, at] = jnp.where(even, to_west, to_east)


def arrived(ev_ref, od_ref, n):
    even = (lax.axis_index("lon") & 1) == 0
    mate = pl.multiple_of(jnp.where(even, K, 0), K)
    at = slice((n // 2) * W, (n // 2 + 1) * W)
    ev = ev_ref[pl.ds(mate, K), at]
    od = od_ref[:, at]
    return jnp.where(even, od, ev), jnp.where(even, ev, od)


def seams(own_ref, ev_ref, od_ref):
    low = low_half(lanes())
    out = []
    for n in range(5):
        from_west, from_east = arrived(ev_ref, od_ref, n)
        own = own_ref[:, n * W : (n + 1) * W]
        if PHASE[n]:
            from_west, from_east, own = (roll(x, -3) for x in (from_west, from_east, own))
        out.append(
            (
                jnp.where(low, from_west, from_east),
                jnp.where(low, from_west, own),
                jnp.where(low, own, from_east),
            )
        )
    return out


def in_step(walks):
    out = [None] * len(walks)
    live = list(range(len(walks)))
    while live:
        for n in tuple(live):
            try:
                next(walks[n])
            except StopIteration as end:
                out[n] = end.value
                live.remove(n)
    return out


class Zonal:
    def __init__(self, packs, u_ref, d_ref):
        self.packs, self.u_ref, self.d_ref = packs, u_ref, d_ref
        self.flux = {}
        self.fall = {}

    def seam_walks(self):
        return [self.seam(n, side) for n in range(2) for side in (1, 2)]

    def seam(self, n, side):
        q, c, wet = self.packs[n][side], self.packs[2][side], wet_of(self.packs[3][side])
        q_next, c_west, wet_next = roll(q, -1), roll(c, 1), roll(wet, -1)
        yield
        step = q_next - q
        before, after = roll(step, 1), roll(step, -1)
        yield
        rise, fall = rise_fall(before, step, after)
        fall_before = roll(fall, 1)
        yield
        down, up = limited(fall_before, rise)
        near, far = weights(c_west)
        from_right = roll(q - (near * up + far * down), -1)
        yield
        near, far = weights(c)
        self.flux[n, side] = c * wet * wet_next * jnp.where(
            c > 0.0, q + (near * down + far * up), from_right
        )
        self.fall[n, side] = fall_before

    def fixes(self, n):
        lane = lanes()
        third = lane - WIN * ((lane * 43) >> 8) == 2
        return jnp.where(third, self.flux[n, 2], self.fall[n, 1]), self.flux[n, 1]

    def row(self, refs, j):
        lane = lanes()
        last = lane == W - 1
        u = load_row(self.u_ref, j)
        wet = wet_of(depth_row(self.d_ref, j))
        halo_wet = unpack(self.packs[3][0], j)
        halo_u = unpack(self.packs[2][0], j)
        halos = [unpack(self.packs[n][0], j) for n in range(2)]
        q = [load_row(ref, j) for ref in refs]
        yield
        halo_wet = wet_of(halo_wet)
        right = [east(q[n], halos[n], lane) for n in range(2)]
        left = [west(q[n], halos[n], lane) for n in range(2)]
        beyond = [roll(jnp.where(lane < 2, halos[n], q[n]), -2) for n in range(2)]
        u_west = west(u, halo_u, lane)
        wet_east = east(wet, halo_wet, lane)
        yield
        edges = [rise_fall(q[n] - left[n], right[n] - q[n], beyond[n] - right[n]) for n in range(2)]
        falls = [roll(edges[n][1], 1) for n in range(2)]
        yield
        near, far = weights(u)
        near_w, far_w = weights(u_west)
        face = u * wet * wet_east
        while (1, 2) not in self.flux:
            yield
        fixes = [[unpack(x, j) for x in self.fixes(n)] for n in range(2)]
        yield
        forward = u > 0.0
        cells = [
            limited(jnp.where(lane == 0, fixes[n][0], falls[n]), edges[n][0]) for n in range(2)
        ]
        from_right = [roll(q[n] - (near_w * cells[n][1] + far_w * cells[n][0]), -1) for n in range(2)]
        yield
        flux = [
            face * jnp.where(forward, q[n] + (near * cells[n][0] + far * cells[n][1]), from_right[n])
            for n in range(2)
        ]
        before = [roll(jnp.where(last, fixes[n][1], flux[n]), 1) for n in range(2)]
        yield
        return [q[n] - (jnp.where(last, fixes[n][0], flux[n]) - before[n]) for n in range(2)]


def zonal_masks(wet, halo_wet, lane):
    return wet * east(wet, halo_wet, lane), wet * west(wet, halo_wet, lane)


def zonal_lap(f, halo, masks, lane):
    return masks[0] * (east(f, halo, lane) - f) - masks[1] * (f - west(f, halo, lane))


def seam_lap(f, wet):
    total = None
    for shift in (1, -1, WIN, -WIN):
        term = wet * roll(wet, shift) * (roll(f, shift) - f)
        total = term if total is None else total + term
    return total


def edge_kernel(
    t_ref, s_ref, u_ref, v_ref, d_ref, own_ref, ev_ref, od_ref, swept_ref, e_ref, o_ref, a_ref, f_ref
):
    lane = lanes()
    lane8, sub8 = lane[:8], lax.broadcasted_iota(jnp.int32, (8, W), 0)
    packs = seams(own_ref, ev_ref, od_ref)
    zonal = Zonal(packs, u_ref, d_ref)
    packs = [p[0] for p in packs]
    wet = {j: wet_of(depth_row(d_ref, j)) for j in (0, 1, 2, 13, 14, 15)}
    all_rows = (15, 14, 13, 0, 1, 2)

    def partial_lap(ref, pack, j, inward):
        f = load_row(ref, j)
        halo, dry = unpack(pack, j), unpack(packs[3], j)
        yield
        right, left = east(f, halo, lane), west(f, halo, lane)
        dry = wet_of(dry)
        wet_r, wet_l = east(wet[j], dry, lane), west(wet[j], dry, lane)
        yield
        return wet[j] * (
            wet_r * (right - f)
            + wet_l * (left - f)
            + wet[inward] * (load_row(ref, inward) - f)
        )

    def corner_tile(j):
        depth = depth_row(d_ref, j)[:8]
        far = roll(depth, W // 2)
        parts = []
        for at, (pack, top) in enumerate(
            ((packs[2], 0), (packs[4], 0), (packs[2], 8), (packs[4], 8), (packs[3], 0))
        ):
            home = -(WIN * j + 3)
            part = pack[top : top + 8]
            parts += [(at, roll(part, home + at)), (W - 1 - at, roll(part, home - at))]
        yield
        corner = jnp.where(sub8 < 4, depth, far)
        for at, part in parts:
            corner = jnp.where(lane8 == at, part, corner)
        return corner

    sides = ((J - 1, J - 2), (0, 1))
    flows = ((u_ref, packs[2]), (v_ref, packs[4]))
    seam_walks = zonal.seam_walks()
    done = in_step(
        seam_walks
        + [zonal.row((t_ref, s_ref), j) for j in all_rows]
        + [partial_lap(*flow, *rows) for rows in sides for flow in flows]
        + [corner_tile(rows[0]) for rows in sides]
    )[len(seam_walks) :]
    halves = []
    for side, (edge, _) in enumerate(sides):
        planes = done[3 * side : 3 * side + 3]
        for j, (t, s) in zip(all_rows[3 * side : 3 * side + 3], planes):
            swept_ref[j if j < 3 else j - 10] = t
            swept_ref[6 + (j if j < 3 else j - 10)] = s
        half = [p[0] for p in planes] + [p[1] for p in planes]
        for n, (ref, _) in enumerate(flows):
            half += [load_row(ref, edge), done[6 + 2 * side + n]]
        halves.append((half, done[10 + side]))
    lat = lax.axis_index("lat")
    even = (lat & 1) == 0
    (north, north_c), (south, south_c) = halves
    for n, (a, b) in enumerate(zip(north, south)):
        e_ref[2 * n : 2 * n + 2] = jnp.where(even, a, b).reshape(2, 8, W)
        o_ref[2 * n : 2 * n + 2] = jnp.where(even, b, a).reshape(2, 8, W)
    e_ref[SEND_ROWS - 1] = jnp.where(even, north_c, south_c)
    o_ref[SEND_ROWS - 1] = jnp.where(even, south_c, north_c)

    @pl.when(lat == lax.axis_size("lat") - 1)
    def _():
        for n in range(SEND_ROWS):
            x = jnp.take_along_axis(o_ref[n], W - 1 - lane8, axis=1)
            if 12 <= n < 20:
                x = -x
            elif n == 20:
                x = jnp.where((lane8 < 4) | (lane8 > W - 5), -x, x)
            o_ref[n] = x

    late = (lat == lax.axis_size("lat") - 1) & seam_first()

    @pl.when(late)
    def _():
        a_ref[...] = o_ref[...]
        f_ref[...] = e_ref[...]

    @pl.when(jnp.logical_not(late))
    def _():
        a_ref[...] = e_ref[...]
        f_ref[...] = o_ref[...]


def low_longitude():
    return lax.axis_index("lon") < lax.axis_size("lon") // 2


def seam_first():
    return jnp.logical_not(low_longitude()) & (lax.axis_index("lon") < lax.axis_size("lon") - 1)


def merid_cell(step, fall_before, j):
    rise, fall = rise_fall(step[j - 1], step[j], step[j + 1])
    down, up = limited(fall_before, rise)
    return down, up, fall


def merid_flux(c, wet_pair, q, q_next, cell, cell_next):
    forward = c > 0.0
    rest = 1.0 - jnp.abs(c)
    square = rest * rest
    near = jnp.where(forward, cell[0], cell_next[1])
    far = jnp.where(forward, cell[1], cell_next[0])
    return c * wet_pair * (
        jnp.where(forward, q, q_next) + (c * rest * near + jnp.where(forward, square, -square) * far)
    )


AUX_TRACER, AUX_FLOW = 12, 10


def inner_kernel(
    t_ref,
    s_ref,
    u_ref,
    v_ref,
    d_ref,
    visc_hbm,
    own_ref,
    ev_ref,
    od_ref,
    swept_ref,
    t_out,
    s_out,
    u_out,
    v_out,
    aux_ref,
    visc_ref,
    sem,
    mask_ref,
    lap_ref,
):
    copy = pltpu.make_async_copy(visc_hbm, visc_ref, sem)
    copy.start()
    lane = lanes()
    packs = seams(own_ref, ev_ref, od_ref)
    zonal = Zonal(packs, u_ref, d_ref)
    rows = [{}, {}]
    for j in (0, 1, 2, 13, 14, 15):
        for n in range(2):
            rows[n][j] = swept_ref[6 * n + (j if j < 3 else j - 10)]
    in_step(zonal.seam_walks())
    for at in range(3, 13, 10):
        group = range(at, min(at + 10, 13))
        for j, (t, s) in zip(group, in_step([zonal.row((t_ref, s_ref), j) for j in group])):
            rows[0][j], rows[1][j] = t, s
    wet = [wet_of(depth_row(d_ref, j)) for j in range(J)]
    for n, out in enumerate((t_out, s_out)):
        q = rows[n]
        for at, j in enumerate((0, 1, 2, 3, 4, 11, 12, 13, 14, 15)):
            aux_ref[AUX_TRACER * n + at] = q[j]
        step = [q[j + 1] - q[j] for j in range(J - 1)]
        cell = merid_cell(step, rise_fall(step[0], step[1], step[2])[1], 2)
        before = None
        for j in range(2, 13):
            after = merid_cell(step, cell[2], j + 1)
            flux = merid_flux(load_row(v_ref, j), wet[j] * wet[j + 1], q[j], q[j + 1], cell, after)
            if j == 2:
                aux_ref[AUX_TRACER * n + 10] = flux
            else:
                store_row(out, j, q[j] - (flux - before))
            if j == 12:
                aux_ref[AUX_TRACER * n + 11] = flux
            cell, before = after, flux
    wet_w, wet_e = wet_of(packs[3][1]), wet_of(packs[3][2])
    low = low_half(lane)
    halo_wet = {}

    def mask_row(j):
        halo = unpack(packs[3][0], j)
        yield
        halo = wet_of(halo)
        if j in (0, J - 1):
            halo_wet[j] = halo
        right, left = east(wet[j], halo, lane), west(wet[j], halo, lane)
        yield
        mask_ref[j] = wet[j] * right
        mask_ref[J + j] = wet[j] * left
        if j < J - 1:
            mask_ref[2 * J + j] = wet[j] * wet[j + 1]

    def lap_row(n, packed, load, j, first, last):
        here = load(n, j)
        halo = unpack(packed, j)
        yield
        right, left = east(here, halo, lane), west(here, halo, lane)
        yield
        total = mask_ref[j] * (right - here) - mask_ref[J + j] * (here - left)
        if j > first:
            total = total - mask_ref[2 * J + j - 1] * (here - load(n, j - 1))
        if j < last:
            total = total + mask_ref[2 * J + j] * (load(n, j + 1) - here)
        return total

    def walk(makers):
        for at in range(0, len(makers), 16):
            in_step([m() for m in makers[at : at + 16]])

    walk([functools.partial(mask_row, j) for j in range(J)])
    flows = ((u_ref, packs[2], u_out), (v_ref, packs[4], v_out))

    def inner(n, j):
        lap_ref[J * n + j] = yield from lap_row(n, flows[n][1][0], lambda n, j: load_row(flows[n][0], j), j, 0, J - 1)

    walk([functools.partial(inner, n, j) for j in range(J) for n in range(2)])
    halo_laps = [
        jnp.where(low, seam_lap(pack[1], wet_w), seam_lap(pack[2], wet_e)) for _, pack, _ in flows
    ]
    copy.wait()
    visc = viscosity(visc_ref)

    def outer(n, j):
        total = yield from lap_row(n, halo_laps[n], lambda n, j: lap_ref[J * n + j], j, 1, J - 2)
        base = 2 * AUX_TRACER + AUX_FLOW * n
        if j == 1:
            aux_ref[base + 2] = total
        elif j == J - 2:
            aux_ref[base + 5] = total
        else:
            store_row(flows[n][2], j, load_row(flows[n][0], j) - visc * total)

    walk([functools.partial(outer, n, j) for j in range(1, J - 1) for n in range(2)])
    for n, (_, pack, _) in enumerate(flows):
        base = 2 * AUX_TRACER + AUX_FLOW * n
        aux_ref[base + 0] = lap_ref[J * n]
        aux_ref[base + 1] = lap_ref[J * n + 1]
        aux_ref[base + 3] = lap_ref[J * n + J - 1]
        aux_ref[base + 4] = lap_ref[J * n + J - 2]
        aux_ref[base + 6] = unpack(halo_laps[n], 0)
        aux_ref[base + 7] = unpack(halo_laps[n], J - 1)
        aux_ref[base + 8] = unpack(pack[0], 0)
        aux_ref[base + 9] = unpack(pack[0], J - 1)
    aux_ref[2 * AUX_TRACER + 2 * AUX_FLOW] = halo_wet[0]
    aux_ref[2 * AUX_TRACER + 2 * AUX_FLOW + 1] = halo_wet[J - 1]
    aux_ref[2 * AUX_TRACER + 2 * AUX_FLOW + 2] = visc


def viscosity(visc_ref):
    level = lax.broadcasted_iota(jnp.int32, (K, W), 0)
    visc = jnp.zeros((K, W), F32)
    for k in range(K):
        visc = jnp.where(level == k, visc_ref[k], visc)
    return visc


def finish_side(side, got_ref, u_ref, v_ref, d_ref, aux_ref, outs, finals, sems):
    lane = lanes()
    t_out, s_out, u_out, v_out = outs
    half = pl.ds(8 * (1 - side), 8)
    copies = [
        pltpu.make_async_copy(
            src.reshape(K, J, W).at[:, half], dst.reshape(K, J, W).at[:, half], sems.at[4 * side + n]
        )
        for n, (src, dst) in enumerate(zip(outs, finals))
    ]
    halo_at = 2 * AUX_TRACER + 2 * AUX_FLOW
    visc = aux_ref[halo_at + 2]

    def recv(n):
        return got_ref[2 * n : 2 * n + 2].reshape(K, W)

    faces = (13, 14, 15) if side == 0 else (-1, 0, 1)
    edge, inward, beyond = (15, 14, 16) if side == 0 else (0, 1, -1)
    wet = {j: wet_of(depth_row(d_ref, j)) for j in ((13, 14, 15) if side == 0 else (0, 1, 2))}
    tile = got_ref[SEND_ROWS - 1]
    lane8 = lane[:8]
    inside = (lane8 > 4) & (lane8 < W - 5)
    row = jnp.where(inside[:1], tile[:1], roll(tile, W // 2)[4:5])
    wet[beyond] = wet_of(jnp.broadcast_to(row, (K, W)))
    part = [tile] + [
        jnp.where(lane8 < W // 2, roll(tile, -m), roll(tile, m)) for m in range(1, 5)
    ]
    corner_flow = [jnp.concatenate([part[n], part[n + 2]], axis=0) for n in range(2)]
    corner_wet = wet_of(jnp.concatenate([part[4], part[4]], axis=0))
    courant = {j: recv(8) if j < 0 else load_row(v_ref, j) for j in faces}
    for n, out in enumerate((t_out, s_out)):
        aux = AUX_TRACER * n
        if side == 0:
            q = {11 + m: aux_ref[aux + 5 + m] for m in range(5)}
            q.update({16 + m: recv(3 * n + m) for m in range(3)})
            before = aux_ref[aux + 11]
        else:
            q = {j: aux_ref[aux + j] for j in range(5)}
            q.update({-1 - m: recv(3 * n + m) for m in range(3)})
            before = None
        step = {j: q[j + 1] - q[j] for j in q if j + 1 in q}
        first = faces[0]
        fall = rise_fall(step[first - 2], step[first - 1], step[first])[1]
        cell = merid_cell(step, fall, first)
        for j in faces:
            after = merid_cell(step, cell[2], j + 1)
            flux = merid_flux(courant[j], wet[j] * wet[j + 1], q[j], q[j + 1], cell, after)
            if before is not None:
                store_row(out, j, q[j] - (flux - before))
            cell, before = after, flux
        if side == 1:
            store_row(out, 2, q[2] - (aux_ref[aux + 10] - before))
        copies[n].start()
    halo_wet = aux_ref[halo_at + 1 - side]
    masks = zonal_masks(wet[edge], halo_wet, lane)
    across = wet[edge] * wet[beyond]
    for n, (ref, out) in enumerate(((u_ref, u_out), (v_ref, v_out))):
        base = 2 * AUX_TRACER + AUX_FLOW * n
        at = (3, 4, 5, 7, 9) if side == 0 else (0, 1, 2, 6, 8)
        lap_edge, lap_in, partial, halo_lap, halo_f = (aux_ref[base + a] for a in at)
        f, f_in = load_row(ref, edge), load_row(ref, inward)
        f_out, lap_out = recv(6 + 2 * n), recv(7 + 2 * n)
        step = across * (f_out - f)
        lap_edge = lap_edge + step
        lap_out = lap_out - step
        halo_lap = halo_lap + halo_wet * corner_wet * (corner_flow[n] - halo_f)
        inner_step = wet[edge] * wet[inward] * (lap_in - lap_edge)
        total = (
            zonal_lap(lap_edge, halo_lap, masks, lane)
            + inner_step
            + across * (lap_out - lap_edge)
        )
        store_row(out, edge, f - visc * total)
        store_row(out, inward, f_in - visc * (partial - inner_step))
        copies[2 + n].start()
    return copies


def at_once(copies):
    for copy in copies:
        copy.wait()


def first_kernel(u_ref, v_ref, d_ref, aux_ref, even_ref, o_ref, *refs):
    fixed = (u_ref, v_ref, d_ref, aux_ref, refs[-5:-1], refs[-9:-5], refs[-1])
    lat = lax.axis_index("lat")
    top = lax.axis_size("lat") - 1
    even = (lat & 1) == 0
    late = (lat == top - 1) & seam_first()

    @pl.when(even & jnp.logical_not(late))
    def _():
        at_once(finish_side(0, even_ref, *fixed) + finish_side(1, o_ref, *fixed))

    @pl.when(late)
    def _():
        at_once(finish_side(1, o_ref, *fixed))


def last_kernel(u_ref, v_ref, d_ref, aux_ref, odd_ref, f_ref, even_ref, o_ref, *refs):
    fixed = (u_ref, v_ref, d_ref, aux_ref, refs[-5:-1], refs[-9:-5], refs[-1])
    lat = lax.axis_index("lat")
    top = lax.axis_size("lat") - 1
    low = low_longitude()
    high = jnp.logical_not(low)

    @pl.when(lat == 1)
    def _():
        at_once(finish_side(0, o_ref, *fixed) + finish_side(1, even_ref, *fixed))

    @pl.when(((lat & 1) == 1) & (lat != 1) & (lat != top))
    def _():
        at_once(finish_side(0, o_ref, *fixed) + finish_side(1, odd_ref, *fixed))

    first = lax.axis_index("lon") == 0

    @pl.when((lat == top) & low & jnp.logical_not(first))
    def _():
        at_once(finish_side(1, odd_ref, *fixed) + finish_side(0, even_ref, *fixed))

    @pl.when((lat == top) & first)
    def _():
        at_once(finish_side(1, odd_ref, *fixed) + finish_side(0, o_ref, *fixed))

    @pl.when((lat == top) & high)
    def _():
        at_once(finish_side(1, odd_ref, *fixed) + finish_side(0, f_ref, *fixed))

    @pl.when((lat == top - 1) & seam_first())
    def _():
        at_once(finish_side(0, f_ref, *fixed))


VMEM = pl.BlockSpec(memory_space=pltpu.VMEM)
HBM = pl.BlockSpec(memory_space=pltpu.HBM)
FLAT = (K * J, W)
AUX = 2 * AUX_TRACER + 2 * AUX_FLOW + 3


def call(kernel, in_specs, out_specs, out_shapes, flops, args, scratch=(), aliases=()):
    return pl.pallas_call(
        kernel,
        out_shape=[jax.ShapeDtypeStruct(s, F32) for s in out_shapes],
        in_specs=in_specs,
        out_specs=out_specs,
        scratch_shapes=list(scratch),
        input_output_aliases=dict(aliases),
        cost_estimate=pl.CostEstimate(flops=flops, bytes_accessed=1 << 20, transcendentals=0),
        compiler_params=pltpu.CompilerParams(vmem_limit_bytes=32 << 20),
    )(*args)


def body(t, s, u, v, ind, lay, visc):
    t, s, u, v = (x.reshape(FLAT) for x in (t, s, u, v))
    n_lon, n_lat = lax.axis_size("lon"), lax.axis_size("lat")
    t, s, u, v, depth, own, ev, od = call(
        pack_kernel,
        [HBM] * 6,
        [VMEM] * 8,
        [FLAT] * 4 + [(J, W), (K, 5 * W), (K, 3 * W), (K, 3 * W)],
        1 << 20,
        [pltpu.with_memory_space_constraint(x, pltpu.HBM) for x in (t, s, u, v, ind, lay)],
        [pltpu.VMEM((J, W), jnp.int32)] * 2 + [pltpu.SemaphoreType.DMA((6,))],
    )
    od = lax.ppermute(od, "lon", [(i, (((i + 1) ^ 1) - 1) % n_lon) for i in range(n_lon)])
    ev = lax.all_gather(
        ev, "lon", axis_index_groups=[[i, i + 1] for i in range(0, n_lon, 2)], tiled=True
    )
    swept, edge_e, edge_o, edge_a, edge_f = call(
        edge_kernel,
        [VMEM] * 8,
        [VMEM] * 5,
        [(12, K, W)] + [(SEND_ROWS, 8, W)] * 4,
        1 << 20,
        (t, s, u, v, depth, own, ev, od),
    )
    to_even, to_odd, pairs_o, last = [], [], [], []
    top = n_lat - 1
    for p in range(n_lon):
        low = p < n_lon // 2
        ahead = not low and p < n_lon - 1
        for l in range(n_lat):
            pair = (p * n_lat + l, p * n_lat + (l ^ 1))
            if l & 1:
                (last if ahead and l == top else to_even).append(pair)
            else:
                (to_odd if l else to_even).append(pair)
            if 0 < l < top:
                pairs_o.append((p * n_lat + l, p * n_lat + ((l + 1) ^ 1) - 1))
        across = (p * n_lat + top, (n_lon - 1 - p) * n_lat + top)
        (last if low else to_even if ahead else pairs_o).append(across)
    got_even = lax.ppermute(edge_a, ("lon", "lat"), to_even)
    got_o = lax.ppermute(edge_o, ("lon", "lat"), pairs_o)
    got_odd = lax.ppermute(edge_e, ("lon", "lat"), to_odd)
    got_f = lax.ppermute(edge_f, ("lon", "lat"), last)
    *parts, aux = call(
        inner_kernel,
        [VMEM] * 5 + [HBM] + [VMEM] * 4,
        [VMEM] * 5,
        [FLAT] * 4 + [(AUX, K, W)],
        1 << 24,
        (t, s, u, v, depth, pltpu.with_memory_space_constraint(visc, pltpu.HBM), own, ev, od, swept),
        [
            pltpu.SMEM((K,), F32),
            pltpu.SemaphoreType.DMA,
            pltpu.VMEM((3 * J, K, W), F32),
            pltpu.VMEM((2 * J, K, W), F32),
        ],
    )
    flow = (u, v, depth, aux)
    outs = call(
        first_kernel,
        [VMEM] * 10,
        [HBM] * 4 + [VMEM] * 4,
        [FLAT] * 8,
        1 << 21,
        (*flow, got_even, got_o, *parts),
        [pltpu.SemaphoreType.DMA((8,))],
        {6 + n: 4 + n for n in range(4)},
    )
    outs = call(
        last_kernel,
        [VMEM] * 8 + [HBM] * 4 + [VMEM] * 4,
        [HBM] * 4 + [VMEM] * 4,
        [FLAT] * 8,
        1 << 21,
        (*flow, got_odd, got_f, got_even, got_o, *outs),
        [pltpu.SemaphoreType.DMA((8,))],
        {8 + n: n for n in range(8)},
    )
    return tuple(x.reshape(K, J, W) for x in outs[:4])


def solution(mesh):
    field, flat = P(None, "lat", "lon"), P("lat", "lon")
    return jax.shard_map(
        body,
        mesh=mesh,
        in_specs=(field, field, field, field, flat, flat, P()),
        out_specs=(field,) * 4,
        check_vma=False,
    )
```

```python
import functools

import jax
import jax.numpy as jnp
from jax import lax
from jax.experimental import pallas as pl
from jax.experimental.pallas import tpu as pltpu
from jax.sharding import PartitionSpec as P

K, J, W = 16, 16, 128
WIN = 6
PHASE = (0, 3, 0, 3, 0)
SEND_ROWS = 21
F32 = jnp.float32


def lanes():
    return lax.broadcasted_iota(jnp.int32, (K, W), 1)


def levels():
    return lax.broadcasted_iota(jnp.int32, (K, W), 0).astype(F32)


def low_half(lane):
    return lane - WIN * ((lane * 43) >> 8) < WIN // 2


def roll(x, shift):
    shift %= W
    return x if shift == 0 else pltpu.roll(x, shift, 1)


def load_row(ref, j):
    return ref[pl.ds(j, K, stride=J), :]


def store_row(ref, j, value):
    ref[pl.ds(j, K, stride=J), :] = value


def depth_row(depth_ref, j):
    return jnp.broadcast_to(depth_ref[pl.ds(j, 1), :], (K, W))


def wet_of(depth):
    return jnp.where(levels() < depth, 1.0, 0.0).astype(F32)


def unpack(packed, j):
    return roll(packed, -(WIN * j + 3))


def east(x, halo, lane):
    return roll(jnp.where(lane < 1, halo, x), -1)


def west(x, halo, lane):
    return roll(jnp.where(lane == W - 1, halo, x), 1)


def minmod(a, b):
    return jnp.maximum(jnp.minimum(a, jnp.maximum(b, 0.0)), jnp.minimum(b, 0.0))


def rise_fall(before, here, after):
    rise = minmod(0.5 * here + (1.0 / 12.0) * (before - after), here)
    return rise, here - rise


def limited(fall, rise):
    return minmod(fall, rise + rise), minmod(rise, fall + fall)


def weights(c):
    size = jnp.abs(c)
    rest = 1.0 - size
    return size * rest, rest * rest


def pack_columns(rows, phase):
    lane = lanes()
    packed = jnp.zeros((K, W), F32)
    moved = [roll(row, WIN * j + phase + 3) for j, row in enumerate(rows)]
    for j, row in enumerate(moved):
        first = WIN * j + phase
        packed = jnp.where((lane >= first) & (lane < first + WIN), row, packed)
    return packed


def pack_kernel(*refs):
    sources, (t_ref, s_ref, u_ref, v_ref, d_ref, own_ref, ev_ref, od_ref) = refs[:6], refs[6:14]
    ind_ref, lay_ref, sems = refs[14:]
    copies = [
        pltpu.make_async_copy(src, dst, sems.at[n])
        for n, (src, dst) in enumerate(zip(sources, (t_ref, s_ref, u_ref, v_ref, ind_ref, lay_ref)))
    ]
    for n in (4, 5, 0, 1, 2, 3):
        copies[n].start()
    copies[4].wait()
    copies[5].wait()
    d_ref[...] = (ind_ref[...] * lay_ref[...]).astype(F32)
    d = pack_columns([depth_row(d_ref, j) for j in range(J)], 3)
    fields = []
    for n, ref in enumerate((t_ref, s_ref, u_ref, v_ref)):
        copies[n].wait()
        fields.append(pack_columns([load_row(ref, j) for j in range(J)], 3 if n == 1 else 0))
    fields.insert(3, d)
    for n, x in enumerate(fields):
        own_ref[:, n * W : (n + 1) * W] = x
    t, s, u, d, v = fields
    low = low_half(lanes())
    even = (lax.axis_index("lon") & 1) == 0
    for n, (a, b) in enumerate(((t, s), (u, d), (v, v))):
        to_east = jnp.where(low, a, b)
        to_west = jnp.where(low, b, a)
        at = slice(n * W, (n + 1) * W)
        ev_ref[:, at] = jnp.where(even, to_east, to_west)
        od_ref[:, at] = jnp.where(even, to_west, to_east)


def arrived(ev_ref, od_ref, n):
    even = (lax.axis_index("lon") & 1) == 0
    mate = pl.multiple_of(jnp.where(even, K, 0), K)
    at = slice((n // 2) * W, (n // 2 + 1) * W)
    ev = ev_ref[pl.ds(mate, K), at]
    od = od_ref[:, at]
    return jnp.where(even, od, ev), jnp.where(even, ev, od)


def seams(own_ref, ev_ref, od_ref):
    low = low_half(lanes())
    out = []
    for n in range(5):
        from_west, from_east = arrived(ev_ref, od_ref, n)
        own = own_ref[:, n * W : (n + 1) * W]
        if PHASE[n]:
            from_west, from_east, own = (roll(x, -3) for x in (from_west, from_east, own))
        out.append(
            (
                jnp.where(low, from_west, from_east),
                jnp.where(low, from_west, own),
                jnp.where(low, own, from_east),
            )
        )
    return out


def in_step(walks):
    out = [None] * len(walks)
    live = list(range(len(walks)))
    while live:
        for n in tuple(live):
            try:
                next(walks[n])
            except StopIteration as end:
                out[n] = end.value
                live.remove(n)
    return out


class Zonal:
    def __init__(self, packs, u_ref, d_ref):
        self.packs, self.u_ref, self.d_ref = packs, u_ref, d_ref
        self.flux = {}
        self.fall = {}

    def seam_walks(self):
        return [self.seam(n, side) for n in range(2) for side in (1, 2)]

    def seam(self, n, side):
        q, c, wet = self.packs[n][side], self.packs[2][side], wet_of(self.packs[3][side])
        q_next, c_west, wet_next = roll(q, -1), roll(c, 1), roll(wet, -1)
        yield
        step = q_next - q
        before, after = roll(step, 1), roll(step, -1)
        yield
        rise, fall = rise_fall(before, step, after)
        fall_before = roll(fall, 1)
        yield
        down, up = limited(fall_before, rise)
        near, far = weights(c_west)
        from_right = roll(q - (near * up + far * down), -1)
        yield
        near, far = weights(c)
        self.flux[n, side] = c * wet * wet_next * jnp.where(
            c > 0.0, q + (near * down + far * up), from_right
        )
        self.fall[n, side] = fall_before

    def fixes(self, n):
        lane = lanes()
        third = lane - WIN * ((lane * 43) >> 8) == 2
        return jnp.where(third, self.flux[n, 2], self.fall[n, 1]), self.flux[n, 1]

    def row(self, refs, j):
        lane = lanes()
        last = lane == W - 1
        u = load_row(self.u_ref, j)
        wet = wet_of(depth_row(self.d_ref, j))
        halo_wet = unpack(self.packs[3][0], j)
        halo_u = unpack(self.packs[2][0], j)
        halos = [unpack(self.packs[n][0], j) for n in range(2)]
        q = [load_row(ref, j) for ref in refs]
        yield
        halo_wet = wet_of(halo_wet)
        right = [east(q[n], halos[n], lane) for n in range(2)]
        left = [west(q[n], halos[n], lane) for n in range(2)]
        beyond = [roll(jnp.where(lane < 2, halos[n], q[n]), -2) for n in range(2)]
        u_west = west(u, halo_u, lane)
        wet_east = east(wet, halo_wet, lane)
        yield
        edges = [rise_fall(q[n] - left[n], right[n] - q[n], beyond[n] - right[n]) for n in range(2)]
        falls = [roll(edges[n][1], 1) for n in range(2)]
        yield
        near, far = weights(u)
        near_w, far_w = weights(u_west)
        face = u * wet * wet_east
        while (1, 2) not in self.flux:
            yield
        fixes = [[unpack(x, j) for x in self.fixes(n)] for n in range(2)]
        yield
        forward = u > 0.0
        cells = [
            limited(jnp.where(lane == 0, fixes[n][0], falls[n]), edges[n][0]) for n in range(2)
        ]
        from_right = [roll(q[n] - (near_w * cells[n][1] + far_w * cells[n][0]), -1) for n in range(2)]
        yield
        flux = [
            face * jnp.where(forward, q[n] + (near * cells[n][0] + far * cells[n][1]), from_right[n])
            for n in range(2)
        ]
        before = [roll(jnp.where(last, fixes[n][1], flux[n]), 1) for n in range(2)]
        yield
        return [q[n] - (jnp.where(last, fixes[n][0], flux[n]) - before[n]) for n in range(2)]


def zonal_masks(wet, halo_wet, lane):
    return wet * east(wet, halo_wet, lane), wet * west(wet, halo_wet, lane)


def zonal_lap(f, halo, masks, lane):
    return masks[0] * (east(f, halo, lane) - f) - masks[1] * (f - west(f, halo, lane))


def seam_lap(f, wet):
    total = None
    for shift in (1, -1, WIN, -WIN):
        term = wet * roll(wet, shift) * (roll(f, shift) - f)
        total = term if total is None else total + term
    return total


def edge_kernel(
    t_ref, s_ref, u_ref, v_ref, d_ref, own_ref, ev_ref, od_ref, swept_ref, e_ref, o_ref, a_ref, f_ref
):
    lane = lanes()
    lane8, sub8 = lane[:8], lax.broadcasted_iota(jnp.int32, (8, W), 0)
    packs = seams(own_ref, ev_ref, od_ref)
    zonal = Zonal(packs, u_ref, d_ref)
    packs = [p[0] for p in packs]
    wet = {j: wet_of(depth_row(d_ref, j)) for j in (0, 1, 2, 13, 14, 15)}
    all_rows = (15, 14, 13, 0, 1, 2)

    def partial_lap(ref, pack, j, inward):
        f = load_row(ref, j)
        halo, dry = unpack(pack, j), unpack(packs[3], j)
        yield
        right, left = east(f, halo, lane), west(f, halo, lane)
        dry = wet_of(dry)
        wet_r, wet_l = east(wet[j], dry, lane), west(wet[j], dry, lane)
        yield
        return wet[j] * (
            wet_r * (right - f)
            + wet_l * (left - f)
            + wet[inward] * (load_row(ref, inward) - f)
        )

    def corner_tile(j):
        depth = depth_row(d_ref, j)[:8]
        far = roll(depth, W // 2)
        parts = []
        for at, (pack, top) in enumerate(
            ((packs[2], 0), (packs[4], 0), (packs[2], 8), (packs[4], 8), (packs[3], 0))
        ):
            home = -(WIN * j + 3)
            part = pack[top : top + 8]
            parts += [(at, roll(part, home + at)), (W - 1 - at, roll(part, home - at))]
        yield
        corner = jnp.where(sub8 < 4, depth, far)
        for at, part in parts:
            corner = jnp.where(lane8 == at, part, corner)
        return corner

    sides = ((J - 1, J - 2), (0, 1))
    flows = ((u_ref, packs[2]), (v_ref, packs[4]))
    seam_walks = zonal.seam_walks()
    done = in_step(
        seam_walks
        + [zonal.row((t_ref, s_ref), j) for j in all_rows]
        + [partial_lap(*flow, *rows) for rows in sides for flow in flows]
        + [corner_tile(rows[0]) for rows in sides]
    )[len(seam_walks) :]
    halves = []
    for side, (edge, _) in enumerate(sides):
        planes = done[3 * side : 3 * side + 3]
        for j, (t, s) in zip(all_rows[3 * side : 3 * side + 3], planes):
            swept_ref[j if j < 3 else j - 10] = t
            swept_ref[6 + (j if j < 3 else j - 10)] = s
        half = [p[0] for p in planes] + [p[1] for p in planes]
        for n, (ref, _) in enumerate(flows):
            half += [load_row(ref, edge), done[6 + 2 * side + n]]
        halves.append((half, done[10 + side]))
    lat = lax.axis_index("lat")
    even = (lat & 1) == 0
    (north, north_c), (south, south_c) = halves
    for n, (a, b) in enumerate(zip(north, south)):
        e_ref[2 * n : 2 * n + 2] = jnp.where(even, a, b).reshape(2, 8, W)
        o_ref[2 * n : 2 * n + 2] = jnp.where(even, b, a).reshape(2, 8, W)
    e_ref[SEND_ROWS - 1] = jnp.where(even, north_c, south_c)
    o_ref[SEND_ROWS - 1] = jnp.where(even, south_c, north_c)

    @pl.when(lat == lax.axis_size("lat") - 1)
    def _():
        for n in range(SEND_ROWS):
            x = jnp.take_along_axis(o_ref[n], W - 1 - lane8, axis=1)
            if 12 <= n < 20:
                x = -x
            elif n == 20:
                x = jnp.where((lane8 < 4) | (lane8 > W - 5), -x, x)
            o_ref[n] = x

    late = (lat == lax.axis_size("lat") - 1) & seam_first()

    @pl.when(late)
    def _():
        a_ref[...] = o_ref[...]
        f_ref[...] = e_ref[...]

    @pl.when(jnp.logical_not(late))
    def _():
        a_ref[...] = e_ref[...]
        f_ref[...] = o_ref[...]


def low_longitude():
    return lax.axis_index("lon") < lax.axis_size("lon") // 2


def seam_first():
    return jnp.logical_not(low_longitude()) & (lax.axis_index("lon") < lax.axis_size("lon") - 1)


def merid_cell(step, fall_before, j):
    rise, fall = rise_fall(step[j - 1], step[j], step[j + 1])
    down, up = limited(fall_before, rise)
    return down, up, fall


def merid_flux(c, wet_pair, q, q_next, cell, cell_next):
    forward = c > 0.0
    rest = 1.0 - jnp.abs(c)
    square = rest * rest
    near = jnp.where(forward, cell[0], cell_next[1])
    far = jnp.where(forward, cell[1], cell_next[0])
    return c * wet_pair * (
        jnp.where(forward, q, q_next) + (c * rest * near + jnp.where(forward, square, -square) * far)
    )


AUX_TRACER, AUX_FLOW = 12, 10


def inner_kernel(
    t_ref,
    s_ref,
    u_ref,
    v_ref,
    d_ref,
    visc_hbm,
    own_ref,
    ev_ref,
    od_ref,
    swept_ref,
    t_out,
    s_out,
    u_out,
    v_out,
    aux_ref,
    visc_ref,
    sem,
    mask_ref,
    lap_ref,
):
    copy = pltpu.make_async_copy(visc_hbm, visc_ref, sem)
    copy.start()
    lane = lanes()
    packs = seams(own_ref, ev_ref, od_ref)
    zonal = Zonal(packs, u_ref, d_ref)
    rows = [{}, {}]
    for j in (0, 1, 2, 13, 14, 15):
        for n in range(2):
            rows[n][j] = swept_ref[6 * n + (j if j < 3 else j - 10)]
    in_step(zonal.seam_walks())
    for at in range(3, 13, 10):
        group = range(at, min(at + 10, 13))
        for j, (t, s) in zip(group, in_step([zonal.row((t_ref, s_ref), j) for j in group])):
            rows[0][j], rows[1][j] = t, s
    wet = [wet_of(depth_row(d_ref, j)) for j in range(J)]

    def meridional(n, out):
        q = rows[n]
        for at, j in enumerate((0, 1, 2, 3, 4, 11, 12, 13, 14, 15)):
            aux_ref[AUX_TRACER * n + at] = q[j]
        step = [q[j + 1] - q[j] for j in range(J - 1)]
        cell = merid_cell(step, rise_fall(step[0], step[1], step[2])[1], 2)
        before = None
        for j in range(2, 13):
            after = merid_cell(step, cell[2], j + 1)
            yield
            flux = merid_flux(load_row(v_ref, j), wet[j] * wet[j + 1], q[j], q[j + 1], cell, after)
            if j == 2:
                aux_ref[AUX_TRACER * n + 10] = flux
            else:
                store_row(out, j, q[j] - (flux - before))
            if j == 12:
                aux_ref[AUX_TRACER * n + 11] = flux
            cell, before = after, flux

    merids = [meridional(0, t_out), meridional(1, s_out)]
    wet_w, wet_e = wet_of(packs[3][1]), wet_of(packs[3][2])
    low = low_half(lane)
    halo_wet = {}

    def mask_row(j):
        halo = unpack(packs[3][0], j)
        yield
        halo = wet_of(halo)
        if j in (0, J - 1):
            halo_wet[j] = halo
        right, left = east(wet[j], halo, lane), west(wet[j], halo, lane)
        yield
        mask_ref[j] = wet[j] * right
        mask_ref[J + j] = wet[j] * left
        if j < J - 1:
            mask_ref[2 * J + j] = wet[j] * wet[j + 1]

    def lap_row(n, packed, load, j, first, last):
        here = load(n, j)
        halo = unpack(packed, j)
        yield
        right, left = east(here, halo, lane), west(here, halo, lane)
        yield
        total = mask_ref[j] * (right - here) - mask_ref[J + j] * (here - left)
        if j > first:
            total = total - mask_ref[2 * J + j - 1] * (here - load(n, j - 1))
        if j < last:
            total = total + mask_ref[2 * J + j] * (load(n, j + 1) - here)
        return total

    def walk(makers):
        for at in range(0, len(makers), 16):
            in_step([m() for m in makers[at : at + 16]])

    walk([functools.partial(mask_row, j) for j in range(J)])
    flows = ((u_ref, packs[2], u_out), (v_ref, packs[4], v_out))

    def inner(n, j):
        lap_ref[J * n + j] = yield from lap_row(n, flows[n][1][0], lambda n, j: load_row(flows[n][0], j), j, 0, J - 1)

    in_step(merids + [inner(n, j) for j in range(J) for n in range(2)])
    halo_laps = [
        jnp.where(low, seam_lap(pack[1], wet_w), seam_lap(pack[2], wet_e)) for _, pack, _ in flows
    ]
    copy.wait()
    visc = viscosity(visc_ref)

    def outer(n, j):
        total = yield from lap_row(n, halo_laps[n], lambda n, j: lap_ref[J * n + j], j, 1, J - 2)
        base = 2 * AUX_TRACER + AUX_FLOW * n
        if j == 1:
            aux_ref[base + 2] = total
        elif j == J - 2:
            aux_ref[base + 5] = total
        else:
            store_row(flows[n][2], j, load_row(flows[n][0], j) - visc * total)

    walk([functools.partial(outer, n, j) for j in range(1, J - 1) for n in range(2)])
    for n, (_, pack, _) in enumerate(flows):
        base = 2 * AUX_TRACER + AUX_FLOW * n
        aux_ref[base + 0] = lap_ref[J * n]
        aux_ref[base + 1] = lap_ref[J * n + 1]
        aux_ref[base + 3] = lap_ref[J * n + J - 1]
        aux_ref[base + 4] = lap_ref[J * n + J - 2]
        aux_ref[base + 6] = unpack(halo_laps[n], 0)
        aux_ref[base + 7] = unpack(halo_laps[n], J - 1)
        aux_ref[base + 8] = unpack(pack[0], 0)
        aux_ref[base + 9] = unpack(pack[0], J - 1)
    aux_ref[2 * AUX_TRACER + 2 * AUX_FLOW] = halo_wet[0]
    aux_ref[2 * AUX_TRACER + 2 * AUX_FLOW + 1] = halo_wet[J - 1]
    aux_ref[2 * AUX_TRACER + 2 * AUX_FLOW + 2] = visc


def viscosity(visc_ref):
    level = lax.broadcasted_iota(jnp.int32, (K, W), 0)
    visc = jnp.zeros((K, W), F32)
    for k in range(K):
        visc = jnp.where(level == k, visc_ref[k], visc)
    return visc


def finish_side(side, got_ref, u_ref, v_ref, d_ref, aux_ref, outs, finals, sems):
    lane = lanes()
    t_out, s_out, u_out, v_out = outs
    half = pl.ds(8 * (1 - side), 8)
    copies = [
        pltpu.make_async_copy(
            src.reshape(K, J, W).at[:, half], dst.reshape(K, J, W).at[:, half], sems.at[4 * side + n]
        )
        for n, (src, dst) in enumerate(zip(outs, finals))
    ]
    halo_at = 2 * AUX_TRACER + 2 * AUX_FLOW
    visc = aux_ref[halo_at + 2]

    def recv(n):
        return got_ref[2 * n : 2 * n + 2].reshape(K, W)

    faces = (13, 14, 15) if side == 0 else (-1, 0, 1)
    edge, inward, beyond = (15, 14, 16) if side == 0 else (0, 1, -1)
    wet = {j: wet_of(depth_row(d_ref, j)) for j in ((13, 14, 15) if side == 0 else (0, 1, 2))}
    tile = got_ref[SEND_ROWS - 1]
    lane8 = lane[:8]
    inside = (lane8 > 4) & (lane8 < W - 5)
    row = jnp.where(inside[:1], tile[:1], roll(tile, W // 2)[4:5])
    wet[beyond] = wet_of(jnp.broadcast_to(row, (K, W)))
    part = [tile] + [
        jnp.where(lane8 < W // 2, roll(tile, -m), roll(tile, m)) for m in range(1, 5)
    ]
    corner_flow = [jnp.concatenate([part[n], part[n + 2]], axis=0) for n in range(2)]
    corner_wet = wet_of(jnp.concatenate([part[4], part[4]], axis=0))
    courant = {j: recv(8) if j < 0 else load_row(v_ref, j) for j in faces}
    for n, out in enumerate((t_out, s_out)):
        aux = AUX_TRACER * n
        if side == 0:
            q = {11 + m: aux_ref[aux + 5 + m] for m in range(5)}
            q.update({16 + m: recv(3 * n + m) for m in range(3)})
            before = aux_ref[aux + 11]
        else:
            q = {j: aux_ref[aux + j] for j in range(5)}
            q.update({-1 - m: recv(3 * n + m) for m in range(3)})
            before = None
        step = {j: q[j + 1] - q[j] for j in q if j + 1 in q}
        first = faces[0]
        fall = rise_fall(step[first - 2], step[first - 1], step[first])[1]
        cell = merid_cell(step, fall, first)
        for j in faces:
            after = merid_cell(step, cell[2], j + 1)
            flux = merid_flux(courant[j], wet[j] * wet[j + 1], q[j], q[j + 1], cell, after)
            if before is not None:
                store_row(out, j, q[j] - (flux - before))
            cell, before = after, flux
        if side == 1:
            store_row(out, 2, q[2] - (aux_ref[aux + 10] - before))
        copies[n].start()
    halo_wet = aux_ref[halo_at + 1 - side]
    masks = zonal_masks(wet[edge], halo_wet, lane)
    across = wet[edge] * wet[beyond]
    for n, (ref, out) in enumerate(((u_ref, u_out), (v_ref, v_out))):
        base = 2 * AUX_TRACER + AUX_FLOW * n
        at = (3, 4, 5, 7, 9) if side == 0 else (0, 1, 2, 6, 8)
        lap_edge, lap_in, partial, halo_lap, halo_f = (aux_ref[base + a] for a in at)
        f, f_in = load_row(ref, edge), load_row(ref, inward)
        f_out, lap_out = recv(6 + 2 * n), recv(7 + 2 * n)
        step = across * (f_out - f)
        lap_edge = lap_edge + step
        lap_out = lap_out - step
        halo_lap = halo_lap + halo_wet * corner_wet * (corner_flow[n] - halo_f)
        inner_step = wet[edge] * wet[inward] * (lap_in - lap_edge)
        total = (
            zonal_lap(lap_edge, halo_lap, masks, lane)
            + inner_step
            + across * (lap_out - lap_edge)
        )
        store_row(out, edge, f - visc * total)
        store_row(out, inward, f_in - visc * (partial - inner_step))
        copies[2 + n].start()
    return copies


def at_once(copies):
    for copy in copies:
        copy.wait()


def first_kernel(u_ref, v_ref, d_ref, aux_ref, even_ref, o_ref, *refs):
    fixed = (u_ref, v_ref, d_ref, aux_ref, refs[-5:-1], refs[-9:-5], refs[-1])
    lat = lax.axis_index("lat")
    top = lax.axis_size("lat") - 1
    even = (lat & 1) == 0
    late = (lat == top - 1) & seam_first()

    @pl.when(even & jnp.logical_not(late))
    def _():
        at_once(finish_side(0, even_ref, *fixed) + finish_side(1, o_ref, *fixed))

    @pl.when(late)
    def _():
        at_once(finish_side(1, o_ref, *fixed))


def last_kernel(u_ref, v_ref, d_ref, aux_ref, odd_ref, f_ref, even_ref, o_ref, *refs):
    fixed = (u_ref, v_ref, d_ref, aux_ref, refs[-5:-1], refs[-9:-5], refs[-1])
    lat = lax.axis_index("lat")
    top = lax.axis_size("lat") - 1
    low = low_longitude()
    high = jnp.logical_not(low)

    @pl.when(lat == 1)
    def _():
        at_once(finish_side(0, o_ref, *fixed) + finish_side(1, even_ref, *fixed))

    @pl.when(((lat & 1) == 1) & (lat != 1) & (lat != top))
    def _():
        at_once(finish_side(0, o_ref, *fixed) + finish_side(1, odd_ref, *fixed))

    first = lax.axis_index("lon") == 0

    @pl.when((lat == top) & low & jnp.logical_not(first))
    def _():
        at_once(finish_side(1, odd_ref, *fixed) + finish_side(0, even_ref, *fixed))

    @pl.when((lat == top) & first)
    def _():
        at_once(finish_side(1, odd_ref, *fixed) + finish_side(0, o_ref, *fixed))

    @pl.when((lat == top) & high)
    def _():
        at_once(finish_side(1, odd_ref, *fixed) + finish_side(0, f_ref, *fixed))

    @pl.when((lat == top - 1) & seam_first())
    def _():
        at_once(finish_side(0, f_ref, *fixed))


VMEM = pl.BlockSpec(memory_space=pltpu.VMEM)
HBM = pl.BlockSpec(memory_space=pltpu.HBM)
FLAT = (K * J, W)
AUX = 2 * AUX_TRACER + 2 * AUX_FLOW + 3


def call(kernel, in_specs, out_specs, out_shapes, flops, args, scratch=(), aliases=()):
    return pl.pallas_call(
        kernel,
        out_shape=[jax.ShapeDtypeStruct(s, F32) for s in out_shapes],
        in_specs=in_specs,
        out_specs=out_specs,
        scratch_shapes=list(scratch),
        input_output_aliases=dict(aliases),
        cost_estimate=pl.CostEstimate(flops=flops, bytes_accessed=1 << 20, transcendentals=0),
        compiler_params=pltpu.CompilerParams(vmem_limit_bytes=32 << 20),
    )(*args)


def body(t, s, u, v, ind, lay, visc):
    t, s, u, v = (x.reshape(FLAT) for x in (t, s, u, v))
    n_lon, n_lat = lax.axis_size("lon"), lax.axis_size("lat")
    t, s, u, v, depth, own, ev, od = call(
        pack_kernel,
        [HBM] * 6,
        [VMEM] * 8,
        [FLAT] * 4 + [(J, W), (K, 5 * W), (K, 3 * W), (K, 3 * W)],
        1 << 20,
        [pltpu.with_memory_space_constraint(x, pltpu.HBM) for x in (t, s, u, v, ind, lay)],
        [pltpu.VMEM((J, W), jnp.int32)] * 2 + [pltpu.SemaphoreType.DMA((6,))],
    )
    od = lax.ppermute(od, "lon", [(i, (((i + 1) ^ 1) - 1) % n_lon) for i in range(n_lon)])
    ev = lax.all_gather(
        ev, "lon", axis_index_groups=[[i, i + 1] for i in range(0, n_lon, 2)], tiled=True
    )
    swept, edge_e, edge_o, edge_a, edge_f = call(
        edge_kernel,
        [VMEM] * 8,
        [VMEM] * 5,
        [(12, K, W)] + [(SEND_ROWS, 8, W)] * 4,
        1 << 20,
        (t, s, u, v, depth, own, ev, od),
    )
    to_even, to_odd, pairs_o, last = [], [], [], []
    top = n_lat - 1
    for p in range(n_lon):
        low = p < n_lon // 2
        ahead = not low and p < n_lon - 1
        for l in range(n_lat):
            pair = (p * n_lat + l, p * n_lat + (l ^ 1))
            if l & 1:
                (last if ahead and l == top else to_even).append(pair)
            else:
                (to_odd if l else to_even).append(pair)
            if 0 < l < top:
                pairs_o.append((p * n_lat + l, p * n_lat + ((l + 1) ^ 1) - 1))
        across = (p * n_lat + top, (n_lon - 1 - p) * n_lat + top)
        (last if low else to_even if ahead else pairs_o).append(across)
    got_even = lax.ppermute(edge_a, ("lon", "lat"), to_even)
    got_o = lax.ppermute(edge_o, ("lon", "lat"), pairs_o)
    got_odd = lax.ppermute(edge_e, ("lon", "lat"), to_odd)
    got_f = lax.ppermute(edge_f, ("lon", "lat"), last)
    *parts, aux = call(
        inner_kernel,
        [VMEM] * 5 + [HBM] + [VMEM] * 4,
        [VMEM] * 5,
        [FLAT] * 4 + [(AUX, K, W)],
        1 << 24,
        (t, s, u, v, depth, pltpu.with_memory_space_constraint(visc, pltpu.HBM), own, ev, od, swept),
        [
            pltpu.SMEM((K,), F32),
            pltpu.SemaphoreType.DMA,
            pltpu.VMEM((3 * J, K, W), F32),
            pltpu.VMEM((2 * J, K, W), F32),
        ],
    )
    flow = (u, v, depth, aux)
    outs = call(
        first_kernel,
        [VMEM] * 10,
        [HBM] * 4 + [VMEM] * 4,
        [FLAT] * 8,
        1 << 21,
        (*flow, got_even, got_o, *parts),
        [pltpu.SemaphoreType.DMA((8,))],
        {6 + n: 4 + n for n in range(4)},
    )
    outs = call(
        last_kernel,
        [VMEM] * 8 + [HBM] * 4 + [VMEM] * 4,
        [HBM] * 4 + [VMEM] * 4,
        [FLAT] * 8,
        1 << 21,
        (*flow, got_odd, got_f, got_even, got_o, *outs),
        [pltpu.SemaphoreType.DMA((8,))],
        {8 + n: n for n in range(8)},
    )
    return tuple(x.reshape(K, J, W) for x in outs[:4])


def solution(mesh):
    field, flat = P(None, "lat", "lon"), P("lat", "lon")
    return jax.shard_map(
        body,
        mesh=mesh,
        in_specs=(field, field, field, field, flat, flat, P()),
        out_specs=(field,) * 4,
        check_vma=False,
    )
```

```python
import functools

import jax
import jax.numpy as jnp
from jax import lax
from jax.experimental import pallas as pl
from jax.experimental.pallas import tpu as pltpu
from jax.sharding import PartitionSpec as P

K, J, W = 16, 16, 128
WIN = 6
PHASE = (0, 3, 0, 3, 0)
SEND_ROWS = 21
F32 = jnp.float32


def lanes():
    return lax.broadcasted_iota(jnp.int32, (K, W), 1)


def levels():
    return lax.broadcasted_iota(jnp.int32, (K, W), 0).astype(F32)


def low_half(lane):
    return lane - WIN * ((lane * 43) >> 8) < WIN // 2


def roll(x, shift):
    shift %= W
    return x if shift == 0 else pltpu.roll(x, shift, 1)


def load_row(ref, j):
    return ref[pl.ds(j, K, stride=J), :]


def store_row(ref, j, value):
    ref[pl.ds(j, K, stride=J), :] = value


def depth_row(depth_ref, j):
    return jnp.broadcast_to(depth_ref[pl.ds(j, 1), :], (K, W))


def wet_of(depth):
    return jnp.where(levels() < depth, 1.0, 0.0).astype(F32)


def unpack(packed, j):
    return roll(packed, -(WIN * j + 3))


def east(x, halo, lane):
    return roll(jnp.where(lane < 1, halo, x), -1)


def west(x, halo, lane):
    return roll(jnp.where(lane == W - 1, halo, x), 1)


def minmod(a, b):
    return jnp.maximum(jnp.minimum(a, jnp.maximum(b, 0.0)), jnp.minimum(b, 0.0))


def rise_fall(before, here, after):
    rise = minmod(0.5 * here + (1.0 / 12.0) * (before - after), here)
    return rise, here - rise


def limited(fall, rise):
    return minmod(fall, rise + rise), minmod(rise, fall + fall)


def weights(c):
    size = jnp.abs(c)
    rest = 1.0 - size
    return size * rest, rest * rest


def pack_columns(rows, phase):
    lane = lanes()
    packed = jnp.zeros((K, W), F32)
    moved = [roll(row, WIN * j + phase + 3) for j, row in enumerate(rows)]
    for j, row in enumerate(moved):
        first = WIN * j + phase
        packed = jnp.where((lane >= first) & (lane < first + WIN), row, packed)
    return packed


def pack_kernel(*refs):
    sources, (t_ref, s_ref, u_ref, v_ref, d_ref, own_ref, ev_ref, od_ref) = refs[:6], refs[6:14]
    ind_ref, lay_ref, sems = refs[14:]
    copies = [
        pltpu.make_async_copy(src, dst, sems.at[n])
        for n, (src, dst) in enumerate(zip(sources, (t_ref, s_ref, u_ref, v_ref, ind_ref, lay_ref)))
    ]
    for n in (4, 5, 0, 1, 2, 3):
        copies[n].start()
    copies[4].wait()
    copies[5].wait()
    d_ref[...] = (ind_ref[...] * lay_ref[...]).astype(F32)
    d = pack_columns([depth_row(d_ref, j) for j in range(J)], 3)
    fields = []
    for n, ref in enumerate((t_ref, s_ref, u_ref, v_ref)):
        copies[n].wait()
        fields.append(pack_columns([load_row(ref, j) for j in range(J)], 3 if n == 1 else 0))
    fields.insert(3, d)
    for n, x in enumerate(fields):
        own_ref[:, n * W : (n + 1) * W] = x
    t, s, u, d, v = fields
    low = low_half(lanes())
    even = (lax.axis_index("lon") & 1) == 0
    for n, (a, b) in enumerate(((t, s), (u, d), (v, v))):
        to_east = jnp.where(low, a, b)
        to_west = jnp.where(low, b, a)
        at = slice(n * W, (n + 1) * W)
        ev_ref[:, at] = jnp.where(even, to_east, to_west)
        od_ref[:, at] = jnp.where(even, to_west, to_east)


def arrived(ev_ref, od_ref, n):
    even = (lax.axis_index("lon") & 1) == 0
    mate = pl.multiple_of(jnp.where(even, K, 0), K)
    at = slice((n // 2) * W, (n // 2 + 1) * W)
    ev = ev_ref[pl.ds(mate, K), at]
    od = od_ref[:, at]
    return jnp.where(even, od, ev), jnp.where(even, ev, od)


def seams(own_ref, ev_ref, od_ref):
    low = low_half(lanes())
    out = []
    for n in range(5):
        from_west, from_east = arrived(ev_ref, od_ref, n)
        own = own_ref[:, n * W : (n + 1) * W]
        if PHASE[n]:
            from_west, from_east, own = (roll(x, -3) for x in (from_west, from_east, own))
        out.append(
            (
                jnp.where(low, from_west, from_east),
                jnp.where(low, from_west, own),
                jnp.where(low, own, from_east),
            )
        )
    return out


def in_step(walks):
    out = [None] * len(walks)
    live = list(range(len(walks)))
    while live:
        for n in tuple(live):
            try:
                next(walks[n])
            except StopIteration as end:
                out[n] = end.value
                live.remove(n)
    return out


class Zonal:
    def __init__(self, packs, u_ref, d_ref):
        self.packs, self.u_ref, self.d_ref = packs, u_ref, d_ref
        self.flux = {}
        self.fall = {}

    def seam_walks(self):
        return [self.seam(n, side) for n in range(2) for side in (1, 2)]

    def seam(self, n, side):
        q, c, wet = self.packs[n][side], self.packs[2][side], wet_of(self.packs[3][side])
        q_next, c_west, wet_next = roll(q, -1), roll(c, 1), roll(wet, -1)
        yield
        step = q_next - q
        before, after = roll(step, 1), roll(step, -1)
        yield
        rise, fall = rise_fall(before, step, after)
        fall_before = roll(fall, 1)
        yield
        down, up = limited(fall_before, rise)
        near, far = weights(c_west)
        from_right = roll(q - (near * up + far * down), -1)
        yield
        near, far = weights(c)
        self.flux[n, side] = c * wet * wet_next * jnp.where(
            c > 0.0, q + (near * down + far * up), from_right
        )
        self.fall[n, side] = fall_before

    def fixes(self, n):
        lane = lanes()
        third = lane - WIN * ((lane * 43) >> 8) == 2
        return jnp.where(third, self.flux[n, 2], self.fall[n, 1]), self.flux[n, 1]

    def row(self, refs, j):
        lane = lanes()
        last = lane == W - 1
        u = load_row(self.u_ref, j)
        wet = wet_of(depth_row(self.d_ref, j))
        halo_wet = unpack(self.packs[3][0], j)
        halo_u = unpack(self.packs[2][0], j)
        halos = [unpack(self.packs[n][0], j) for n in range(2)]
        q = [load_row(ref, j) for ref in refs]
        yield
        halo_wet = wet_of(halo_wet)
        right = [east(q[n], halos[n], lane) for n in range(2)]
        left = [west(q[n], halos[n], lane) for n in range(2)]
        beyond = [roll(jnp.where(lane < 2, halos[n], q[n]), -2) for n in range(2)]
        u_west = west(u, halo_u, lane)
        wet_east = east(wet, halo_wet, lane)
        yield
        edges = [rise_fall(q[n] - left[n], right[n] - q[n], beyond[n] - right[n]) for n in range(2)]
        falls = [roll(edges[n][1], 1) for n in range(2)]
        yield
        near, far = weights(u)
        near_w, far_w = weights(u_west)
        face = u * wet * wet_east
        while (1, 2) not in self.flux:
            yield
        fixes = [[unpack(x, j) for x in self.fixes(n)] for n in range(2)]
        yield
        forward = u > 0.0
        cells = [
            limited(jnp.where(lane == 0, fixes[n][0], falls[n]), edges[n][0]) for n in range(2)
        ]
        from_right = [roll(q[n] - (near_w * cells[n][1] + far_w * cells[n][0]), -1) for n in range(2)]
        yield
        flux = [
            face * jnp.where(forward, q[n] + (near * cells[n][0] + far * cells[n][1]), from_right[n])
            for n in range(2)
        ]
        before = [roll(jnp.where(last, fixes[n][1], flux[n]), 1) for n in range(2)]
        yield
        return [q[n] - (jnp.where(last, fixes[n][0], flux[n]) - before[n]) for n in range(2)]


def zonal_masks(wet, halo_wet, lane):
    return wet * east(wet, halo_wet, lane), wet * west(wet, halo_wet, lane)


def zonal_lap(f, halo, masks, lane):
    return masks[0] * (east(f, halo, lane) - f) - masks[1] * (f - west(f, halo, lane))


def seam_lap(f, wet):
    total = None
    for shift in (1, -1, WIN, -WIN):
        term = wet * roll(wet, shift) * (roll(f, shift) - f)
        total = term if total is None else total + term
    return total


def edge_kernel(
    t_ref, s_ref, u_ref, v_ref, d_ref, own_ref, ev_ref, od_ref, swept_ref, e_ref, o_ref, a_ref, f_ref
):
    lane = lanes()
    lane8, sub8 = lane[:8], lax.broadcasted_iota(jnp.int32, (8, W), 0)
    packs = seams(own_ref, ev_ref, od_ref)
    zonal = Zonal(packs, u_ref, d_ref)
    packs = [p[0] for p in packs]
    wet = {j: wet_of(depth_row(d_ref, j)) for j in (0, 1, 2, 13, 14, 15)}
    all_rows = (15, 14, 13, 0, 1, 2)

    def partial_lap(ref, pack, j, inward):
        f = load_row(ref, j)
        halo, dry = unpack(pack, j), unpack(packs[3], j)
        yield
        right, left = east(f, halo, lane), west(f, halo, lane)
        dry = wet_of(dry)
        wet_r, wet_l = east(wet[j], dry, lane), west(wet[j], dry, lane)
        yield
        return wet[j] * (
            wet_r * (right - f)
            + wet_l * (left - f)
            + wet[inward] * (load_row(ref, inward) - f)
        )

    def corner_tile(j):
        depth = depth_row(d_ref, j)[:8]
        far = roll(depth, W // 2)
        parts = []
        for at, (pack, top) in enumerate(
            ((packs[2], 0), (packs[4], 0), (packs[2], 8), (packs[4], 8), (packs[3], 0))
        ):
            home = -(WIN * j + 3)
            part = pack[top : top + 8]
            parts += [(at, roll(part, home + at)), (W - 1 - at, roll(part, home - at))]
        yield
        corner = jnp.where(sub8 < 4, depth, far)
        for at, part in parts:
            corner = jnp.where(lane8 == at, part, corner)
        return corner

    sides = ((J - 1, J - 2), (0, 1))
    flows = ((u_ref, packs[2]), (v_ref, packs[4]))
    seam_walks = zonal.seam_walks()
    done = in_step(
        seam_walks
        + [zonal.row((t_ref, s_ref), j) for j in all_rows]
        + [partial_lap(*flow, *rows) for rows in sides for flow in flows]
        + [corner_tile(rows[0]) for rows in sides]
    )[len(seam_walks) :]
    halves = []
    for side, (edge, _) in enumerate(sides):
        planes = done[3 * side : 3 * side + 3]
        for j, (t, s) in zip(all_rows[3 * side : 3 * side + 3], planes):
            swept_ref[j if j < 3 else j - 10] = t
            swept_ref[6 + (j if j < 3 else j - 10)] = s
        half = [p[0] for p in planes] + [p[1] for p in planes]
        for n, (ref, _) in enumerate(flows):
            half += [load_row(ref, edge), done[6 + 2 * side + n]]
        halves.append((half, done[10 + side]))
    lat = lax.axis_index("lat")
    even = (lat & 1) == 0
    (north, north_c), (south, south_c) = halves
    for n, (a, b) in enumerate(zip(north, south)):
        e_ref[2 * n : 2 * n + 2] = jnp.where(even, a, b).reshape(2, 8, W)
        o_ref[2 * n : 2 * n + 2] = jnp.where(even, b, a).reshape(2, 8, W)
    e_ref[SEND_ROWS - 1] = jnp.where(even, north_c, south_c)
    o_ref[SEND_ROWS - 1] = jnp.where(even, south_c, north_c)

    @pl.when(lat == lax.axis_size("lat") - 1)
    def _():
        for n in range(SEND_ROWS):
            x = jnp.take_along_axis(o_ref[n], W - 1 - lane8, axis=1)
            if 12 <= n < 20:
                x = -x
            elif n == 20:
                x = jnp.where((lane8 < 4) | (lane8 > W - 5), -x, x)
            o_ref[n] = x

    late = (lat == lax.axis_size("lat") - 1) & seam_first()

    @pl.when(late)
    def _():
        a_ref[...] = o_ref[...]
        f_ref[...] = e_ref[...]

    @pl.when(jnp.logical_not(late))
    def _():
        a_ref[...] = e_ref[...]

    @pl.when((lat == lax.axis_size("lat") - 1) & jnp.logical_not(late))
    def _():
        f_ref[...] = o_ref[...]


def low_longitude():
    return lax.axis_index("lon") < lax.axis_size("lon") // 2


def seam_first():
    return jnp.logical_not(low_longitude()) & (lax.axis_index("lon") < lax.axis_size("lon") - 1)


def merid_cell(step, fall_before, j):
    rise, fall = rise_fall(step[j - 1], step[j], step[j + 1])
    down, up = limited(fall_before, rise)
    return down, up, fall


def merid_flux(c, wet_pair, q, q_next, cell, cell_next):
    forward = c > 0.0
    rest = 1.0 - jnp.abs(c)
    square = rest * rest
    near = jnp.where(forward, cell[0], cell_next[1])
    far = jnp.where(forward, cell[1], cell_next[0])
    return c * wet_pair * (
        jnp.where(forward, q, q_next) + (c * rest * near + jnp.where(forward, square, -square) * far)
    )


AUX_TRACER, AUX_FLOW = 12, 10


def inner_kernel(
    t_ref,
    s_ref,
    u_ref,
    v_ref,
    d_ref,
    visc_hbm,
    own_ref,
    ev_ref,
    od_ref,
    swept_ref,
    t_out,
    s_out,
    u_out,
    v_out,
    aux_ref,
    visc_ref,
    sem,
    mask_ref,
    lap_ref,
):
    copy = pltpu.make_async_copy(visc_hbm, visc_ref, sem)
    copy.start()
    lane = lanes()
    packs = seams(own_ref, ev_ref, od_ref)
    zonal = Zonal(packs, u_ref, d_ref)
    rows = [{}, {}]
    for j in (0, 1, 2, 13, 14, 15):
        for n in range(2):
            rows[n][j] = swept_ref[6 * n + (j if j < 3 else j - 10)]
    in_step(zonal.seam_walks())
    for at in range(3, 13, 10):
        group = range(at, min(at + 10, 13))
        for j, (t, s) in zip(group, in_step([zonal.row((t_ref, s_ref), j) for j in group])):
            rows[0][j], rows[1][j] = t, s
    wet = [wet_of(depth_row(d_ref, j)) for j in range(J)]

    def meridional(n, out):
        q = rows[n]
        for at, j in enumerate((0, 1, 2, 3, 4, 11, 12, 13, 14, 15)):
            aux_ref[AUX_TRACER * n + at] = q[j]
        step = [q[j + 1] - q[j] for j in range(J - 1)]
        cell = merid_cell(step, rise_fall(step[0], step[1], step[2])[1], 2)
        before = None
        for j in range(2, 13):
            after = merid_cell(step, cell[2], j + 1)
            yield
            flux = merid_flux(load_row(v_ref, j), wet[j] * wet[j + 1], q[j], q[j + 1], cell, after)
            if j == 2:
                aux_ref[AUX_TRACER * n + 10] = flux
            else:
                store_row(out, j, q[j] - (flux - before))
            if j == 12:
                aux_ref[AUX_TRACER * n + 11] = flux
            cell, before = after, flux

    merids = [meridional(0, t_out), meridional(1, s_out)]
    wet_w, wet_e = wet_of(packs[3][1]), wet_of(packs[3][2])
    low = low_half(lane)
    halo_wet = {}

    def mask_row(j):
        halo = unpack(packs[3][0], j)
        yield
        halo = wet_of(halo)
        if j in (0, J - 1):
            halo_wet[j] = halo
        right, left = east(wet[j], halo, lane), west(wet[j], halo, lane)
        yield
        mask_ref[j] = wet[j] * right
        mask_ref[J + j] = wet[j] * left
        if j < J - 1:
            mask_ref[2 * J + j] = wet[j] * wet[j + 1]

    def lap_row(n, packed, load, j, first, last):
        here = load(n, j)
        halo = unpack(packed, j)
        yield
        right, left = east(here, halo, lane), west(here, halo, lane)
        yield
        total = mask_ref[j] * (right - here) - mask_ref[J + j] * (here - left)
        if j > first:
            total = total - mask_ref[2 * J + j - 1] * (here - load(n, j - 1))
        if j < last:
            total = total + mask_ref[2 * J + j] * (load(n, j + 1) - here)
        return total

    def walk(makers):
        for at in range(0, len(makers), 16):
            in_step([m() for m in makers[at : at + 16]])

    walk([functools.partial(mask_row, j) for j in range(J)])
    flows = ((u_ref, packs[2], u_out), (v_ref, packs[4], v_out))

    def inner(n, j):
        lap_ref[J * n + j] = yield from lap_row(n, flows[n][1][0], lambda n, j: load_row(flows[n][0], j), j, 0, J - 1)

    in_step(merids + [inner(n, j) for j in range(J) for n in range(2)])
    halo_laps = [
        jnp.where(low, seam_lap(pack[1], wet_w), seam_lap(pack[2], wet_e)) for _, pack, _ in flows
    ]
    copy.wait()
    visc = viscosity(visc_ref)

    def outer(n, j):
        total = yield from lap_row(n, halo_laps[n], lambda n, j: lap_ref[J * n + j], j, 1, J - 2)
        base = 2 * AUX_TRACER + AUX_FLOW * n
        if j == 1:
            aux_ref[base + 2] = total
        elif j == J - 2:
            aux_ref[base + 5] = total
        else:
            store_row(flows[n][2], j, load_row(flows[n][0], j) - visc * total)

    walk([functools.partial(outer, n, j) for j in range(1, J - 1) for n in range(2)])
    for n, (_, pack, _) in enumerate(flows):
        base = 2 * AUX_TRACER + AUX_FLOW * n
        aux_ref[base + 0] = lap_ref[J * n]
        aux_ref[base + 1] = lap_ref[J * n + 1]
        aux_ref[base + 3] = lap_ref[J * n + J - 1]
        aux_ref[base + 4] = lap_ref[J * n + J - 2]
        aux_ref[base + 6] = unpack(halo_laps[n], 0)
        aux_ref[base + 7] = unpack(halo_laps[n], J - 1)
        aux_ref[base + 8] = unpack(pack[0], 0)
        aux_ref[base + 9] = unpack(pack[0], J - 1)
    aux_ref[2 * AUX_TRACER + 2 * AUX_FLOW] = halo_wet[0]
    aux_ref[2 * AUX_TRACER + 2 * AUX_FLOW + 1] = halo_wet[J - 1]
    aux_ref[2 * AUX_TRACER + 2 * AUX_FLOW + 2] = visc


def viscosity(visc_ref):
    level = lax.broadcasted_iota(jnp.int32, (K, W), 0)
    visc = jnp.zeros((K, W), F32)
    for k in range(K):
        visc = jnp.where(level == k, visc_ref[k], visc)
    return visc


def finish_side(side, got_ref, u_ref, v_ref, d_ref, aux_ref, outs, finals, sems):
    lane = lanes()
    t_out, s_out, u_out, v_out = outs
    half = pl.ds(8 * (1 - side), 8)
    copies = [
        pltpu.make_async_copy(
            src.reshape(K, J, W).at[:, half], dst.reshape(K, J, W).at[:, half], sems.at[4 * side + n]
        )
        for n, (src, dst) in enumerate(zip(outs, finals))
    ]
    halo_at = 2 * AUX_TRACER + 2 * AUX_FLOW
    visc = aux_ref[halo_at + 2]

    def recv(n):
        return got_ref[2 * n : 2 * n + 2].reshape(K, W)

    faces = (13, 14, 15) if side == 0 else (-1, 0, 1)
    edge, inward, beyond = (15, 14, 16) if side == 0 else (0, 1, -1)
    wet = {j: wet_of(depth_row(d_ref, j)) for j in ((13, 14, 15) if side == 0 else (0, 1, 2))}
    tile = got_ref[SEND_ROWS - 1]
    lane8 = lane[:8]
    inside = (lane8 > 4) & (lane8 < W - 5)
    row = jnp.where(inside[:1], tile[:1], roll(tile, W // 2)[4:5])
    wet[beyond] = wet_of(jnp.broadcast_to(row, (K, W)))
    part = [tile] + [
        jnp.where(lane8 < W // 2, roll(tile, -m), roll(tile, m)) for m in range(1, 5)
    ]
    corner_flow = [jnp.concatenate([part[n], part[n + 2]], axis=0) for n in range(2)]
    corner_wet = wet_of(jnp.concatenate([part[4], part[4]], axis=0))
    courant = {j: recv(8) if j < 0 else load_row(v_ref, j) for j in faces}
    for n, out in enumerate((t_out, s_out)):
        aux = AUX_TRACER * n
        if side == 0:
            q = {11 + m: aux_ref[aux + 5 + m] for m in range(5)}
            q.update({16 + m: recv(3 * n + m) for m in range(3)})
            before = aux_ref[aux + 11]
        else:
            q = {j: aux_ref[aux + j] for j in range(5)}
            q.update({-1 - m: recv(3 * n + m) for m in range(3)})
            before = None
        step = {j: q[j + 1] - q[j] for j in q if j + 1 in q}
        first = faces[0]
        fall = rise_fall(step[first - 2], step[first - 1], step[first])[1]
        cell = merid_cell(step, fall, first)
        for j in faces:
            after = merid_cell(step, cell[2], j + 1)
            flux = merid_flux(courant[j], wet[j] * wet[j + 1], q[j], q[j + 1], cell, after)
            if before is not None:
                store_row(out, j, q[j] - (flux - before))
            cell, before = after, flux
        if side == 1:
            store_row(out, 2, q[2] - (aux_ref[aux + 10] - before))
        copies[n].start()
    halo_wet = aux_ref[halo_at + 1 - side]
    masks = zonal_masks(wet[edge], halo_wet, lane)
    across = wet[edge] * wet[beyond]
    for n, (ref, out) in enumerate(((u_ref, u_out), (v_ref, v_out))):
        base = 2 * AUX_TRACER + AUX_FLOW * n
        at = (3, 4, 5, 7, 9) if side == 0 else (0, 1, 2, 6, 8)
        lap_edge, lap_in, partial, halo_lap, halo_f = (aux_ref[base + a] for a in at)
        f, f_in = load_row(ref, edge), load_row(ref, inward)
        f_out, lap_out = recv(6 + 2 * n), recv(7 + 2 * n)
        step = across * (f_out - f)
        lap_edge = lap_edge + step
        lap_out = lap_out - step
        halo_lap = halo_lap + halo_wet * corner_wet * (corner_flow[n] - halo_f)
        inner_step = wet[edge] * wet[inward] * (lap_in - lap_edge)
        total = (
            zonal_lap(lap_edge, halo_lap, masks, lane)
            + inner_step
            + across * (lap_out - lap_edge)
        )
        store_row(out, edge, f - visc * total)
        store_row(out, inward, f_in - visc * (partial - inner_step))
        copies[2 + n].start()
    return copies


def at_once(copies):
    for copy in copies:
        copy.wait()


def first_kernel(u_ref, v_ref, d_ref, aux_ref, even_ref, o_ref, *refs):
    fixed = (u_ref, v_ref, d_ref, aux_ref, refs[-5:-1], refs[-9:-5], refs[-1])
    lat = lax.axis_index("lat")
    top = lax.axis_size("lat") - 1
    even = (lat & 1) == 0
    late = (lat == top - 1) & seam_first()

    @pl.when(even & jnp.logical_not(late))
    def _():
        at_once(finish_side(0, even_ref, *fixed) + finish_side(1, o_ref, *fixed))

    @pl.when(late)
    def _():
        at_once(finish_side(1, o_ref, *fixed))


def last_kernel(u_ref, v_ref, d_ref, aux_ref, odd_ref, f_ref, even_ref, o_ref, *refs):
    fixed = (u_ref, v_ref, d_ref, aux_ref, refs[-5:-1], refs[-9:-5], refs[-1])
    lat = lax.axis_index("lat")
    top = lax.axis_size("lat") - 1
    low = low_longitude()
    high = jnp.logical_not(low)

    @pl.when(lat == 1)
    def _():
        at_once(finish_side(0, o_ref, *fixed) + finish_side(1, even_ref, *fixed))

    @pl.when(((lat & 1) == 1) & (lat != 1) & (lat != top))
    def _():
        at_once(finish_side(0, o_ref, *fixed) + finish_side(1, odd_ref, *fixed))

    first = lax.axis_index("lon") == 0

    @pl.when((lat == top) & low & jnp.logical_not(first))
    def _():
        at_once(finish_side(1, odd_ref, *fixed) + finish_side(0, even_ref, *fixed))

    @pl.when((lat == top) & first)
    def _():
        at_once(finish_side(1, odd_ref, *fixed) + finish_side(0, o_ref, *fixed))

    @pl.when((lat == top) & high)
    def _():
        at_once(finish_side(1, odd_ref, *fixed) + finish_side(0, f_ref, *fixed))

    @pl.when((lat == top - 1) & seam_first())
    def _():
        at_once(finish_side(0, f_ref, *fixed))


VMEM = pl.BlockSpec(memory_space=pltpu.VMEM)
HBM = pl.BlockSpec(memory_space=pltpu.HBM)
FLAT = (K * J, W)
AUX = 2 * AUX_TRACER + 2 * AUX_FLOW + 3


def call(kernel, in_specs, out_specs, out_shapes, flops, args, scratch=(), aliases=()):
    return pl.pallas_call(
        kernel,
        out_shape=[jax.ShapeDtypeStruct(s, F32) for s in out_shapes],
        in_specs=in_specs,
        out_specs=out_specs,
        scratch_shapes=list(scratch),
        input_output_aliases=dict(aliases),
        cost_estimate=pl.CostEstimate(flops=flops, bytes_accessed=1 << 20, transcendentals=0),
        compiler_params=pltpu.CompilerParams(vmem_limit_bytes=32 << 20),
    )(*args)


def body(t, s, u, v, ind, lay, visc):
    t, s, u, v = (x.reshape(FLAT) for x in (t, s, u, v))
    n_lon, n_lat = lax.axis_size("lon"), lax.axis_size("lat")
    t, s, u, v, depth, own, ev, od = call(
        pack_kernel,
        [HBM] * 6,
        [VMEM] * 8,
        [FLAT] * 4 + [(J, W), (K, 5 * W), (K, 3 * W), (K, 3 * W)],
        1 << 20,
        [pltpu.with_memory_space_constraint(x, pltpu.HBM) for x in (t, s, u, v, ind, lay)],
        [pltpu.VMEM((J, W), jnp.int32)] * 2 + [pltpu.SemaphoreType.DMA((6,))],
    )
    od = lax.ppermute(od, "lon", [(i, (((i + 1) ^ 1) - 1) % n_lon) for i in range(n_lon)])
    ev = lax.all_gather(
        ev, "lon", axis_index_groups=[[i, i + 1] for i in range(0, n_lon, 2)], tiled=True
    )
    swept, edge_e, edge_o, edge_a, edge_f = call(
        edge_kernel,
        [VMEM] * 8,
        [VMEM] * 5,
        [(12, K, W)] + [(SEND_ROWS, 8, W)] * 4,
        1 << 20,
        (t, s, u, v, depth, own, ev, od),
    )
    to_even, to_odd, pairs_o, last = [], [], [], []
    top = n_lat - 1
    for p in range(n_lon):
        low = p < n_lon // 2
        ahead = not low and p < n_lon - 1
        for l in range(n_lat):
            pair = (p * n_lat + l, p * n_lat + (l ^ 1))
            if l & 1:
                (last if ahead and l == top else to_even).append(pair)
            else:
                (to_odd if l else to_even).append(pair)
            if 0 < l < top:
                pairs_o.append((p * n_lat + l, p * n_lat + ((l + 1) ^ 1) - 1))
        across = (p * n_lat + top, (n_lon - 1 - p) * n_lat + top)
        (last if low else to_even if ahead else pairs_o).append(across)
    got_even = lax.ppermute(edge_a, ("lon", "lat"), to_even)
    got_o = lax.ppermute(edge_o, ("lon", "lat"), pairs_o)
    got_odd = lax.ppermute(edge_e, ("lon", "lat"), to_odd)
    got_f = lax.ppermute(edge_f, ("lon", "lat"), last)
    *parts, aux = call(
        inner_kernel,
        [VMEM] * 5 + [HBM] + [VMEM] * 4,
        [VMEM] * 5,
        [FLAT] * 4 + [(AUX, K, W)],
        1 << 24,
        (t, s, u, v, depth, pltpu.with_memory_space_constraint(visc, pltpu.HBM), own, ev, od, swept),
        [
            pltpu.SMEM((K,), F32),
            pltpu.SemaphoreType.DMA,
            pltpu.VMEM((3 * J, K, W), F32),
            pltpu.VMEM((2 * J, K, W), F32),
        ],
    )
    flow = (u, v, depth, aux)
    outs = call(
        first_kernel,
        [VMEM] * 10,
        [HBM] * 4 + [VMEM] * 4,
        [FLAT] * 8,
        1 << 21,
        (*flow, got_even, got_o, *parts),
        [pltpu.SemaphoreType.DMA((8,))],
        {6 + n: 4 + n for n in range(4)},
    )
    outs = call(
        last_kernel,
        [VMEM] * 8 + [HBM] * 4 + [VMEM] * 4,
        [HBM] * 4 + [VMEM] * 4,
        [FLAT] * 8,
        1 << 21,
        (*flow, got_odd, got_f, got_even, got_o, *outs),
        [pltpu.SemaphoreType.DMA((8,))],
        {8 + n: n for n in range(8)},
    )
    return tuple(x.reshape(K, J, W) for x in outs[:4])


def solution(mesh):
    field, flat = P(None, "lat", "lon"), P("lat", "lon")
    return jax.shard_map(
        body,
        mesh=mesh,
        in_specs=(field, field, field, field, flat, flat, P()),
        out_specs=(field,) * 4,
        check_vma=False,
    )
```
